32 devices in a mesh: slab: 8 (over z, x), case: 4 (over y, core).
Axes of the slice: x: 2, y: 2, z: 4, core: 2. Of those that a mesh axis runs over, the one named last changes fastest.
Arguments:
- tokens: bfloat16 [4, 16, 8, 8, 512], P('case', 'slab'), may hold values from -6 to 6
- cotangent: bfloat16 [4, 16, 8, 8, 512], P('case', 'slab'), may hold values from -6 to 6
- w_qkv: bfloat16 [512, 1536], replicated, may hold values from -4 to 4
- w_out: bfloat16 [512, 512], replicated, may hold values from -0.25 to 0.25
- w_up: bfloat16 [512, 2048], replicated, may hold values from -0.25 to 0.25
- w_down: bfloat16 [2048, 512], replicated, may hold values from -0.125 to 0.125
- gain_attn: float32 [512], replicated, may hold values from 0.1 to 1.9
- gain_mlp: float32 [512], replicated, may hold values from 0.1 to 1.9
Outputs:
- grad_tokens: bfloat16 [4, 16, 8, 8, 512], P('case', 'slab')
- grad_qkv: float32 [512, 1536], P('slab')
- grad_out: float32 [512, 512], P('slab')
- grad_up: float32 [512, 2048], P('slab')
- grad_down: float32 [2048, 512], P('slab')
- grad_gain_attn: float32 [512], P('slab')
- grad_gain_mlp: float32 [512], P('slab')
The draws below stay inside these ranges and needn't reach their ends.
All inputs are finite; a program needn't handle non-finite values.
Results may differ from the reference program's by a relative error of at most 0.022.
Values may be sent and summed in bfloat16 or wider, within the bound.
No kernel may reach another device: no remote copies, remote signals or barrier semaphores. Data moves between devices by JAX's collectives and lax.ppermute only.
A program may use at most 128 MiB of HBM per device.

```python
import math
import jax
import jax.numpy as jnp
from jax import lax

D = 512
HEADS = 8
FF = 2048
GX = 8
GY = 8
Z = 16
CASES = 4
TOKENS_ALL = 4096


def draw_w_qkv(key, part):
    key = jax.random.fold_in(key, 11)
    base = jnp.clip(jax.random.normal(key, (D, 3 * D), jnp.float32), -4.5, 4.5) / math.sqrt(D)
    return base.astype(jnp.bfloat16)


def steps_of(rng, dims, pieces, least, top_value):
    def one(axis_at, parts):
        heights = jax.random.uniform(jax.random.fold_in(jax.random.fold_in(rng, 6), axis_at), (parts,), jnp.float32, least / len(pieces), top_value / len(pieces))
        return jnp.repeat(jnp.exp(heights), dims[axis_at] // parts).reshape((-1,) + (1,) * (len(dims) - axis_at - 1))

    level = one(*pieces[0])
    for cut in pieces[1:]:
        level = level * one(*cut)
    return level


def bell_draw(rng, shape, spread, limit, pieces=(), dtype=jnp.bfloat16):
    array = jax.random.normal(rng, shape, jnp.float32) * spread
    if len(pieces) > 0:
        array = steps_of(rng, shape, pieces, -0.22, 0.18) * array
    return jnp.clip(array, min=-limit, max=limit).astype(dtype)


def setup_inputs(seed: int = 0) -> dict:
    key_list = jax.random.split(jax.random.key(seed), 9)
    tokens = bell_draw(key_list[0], (CASES, Z, GY, GX, D), 1.0, 6.0, ((0, 4), (1, 8)))
    cotangent = bell_draw(key_list[1], (CASES, Z, GY, GX, D), 1.0, 6.0, ((0, 4), (1, 8)))
    w_qkv = draw_w_qkv(jax.random.fold_in(key_list[8], 71), 0)
    w_out = bell_draw(key_list[3], (D, D), D ** -0.5, 0.25)
    w_up = bell_draw(key_list[4], (D, FF), D ** -0.5, 0.25)
    w_down = bell_draw(key_list[5], (FF, D), FF ** -0.5, 0.125)
    gain_attn = jnp.clip(1.0 + 0.18 * jax.random.normal(key_list[6], (D,), jnp.float32), 0.1, 1.9)
    gain_mlp = jnp.clip(1.0 + 0.18 * jax.random.normal(key_list[7], (D,), jnp.float32), 0.1, 1.9)
    return dict(tokens=tokens, cotangent=cotangent, w_qkv=w_qkv, w_out=w_out, w_up=w_up, w_down=w_down, gain_attn=gain_attn, gain_mlp=gain_mlp)


epsilon = 1e-06
root_two_pi = math.sqrt(2.0 / math.pi)

def normalize(values, gain):
    inverse = lax.rsqrt(lax.optimization_barrier(jnp.mean(values * values, axis=-1, keepdims=True)) + epsilon)
    normed = values * inverse
    return (normed, inverse, (normed * gain).astype(jnp.bfloat16))

def norm_back(grad_normed, normed, inverse, gain):
    scaled = grad_normed * gain
    return inverse * (scaled - normed * lax.optimization_barrier(jnp.mean(scaled * normed, axis=-1, keepdims=True)))

def gelu_value(inputs):
    inner = root_two_pi * (inputs + 0.044715 * inputs * inputs * inputs)
    return 0.5 * inputs * (1.0 + jnp.tanh(inner))

def gelu_slope(inputs):
    tangent = jnp.tanh(root_two_pi * (inputs + 0.044715 * inputs * inputs * inputs))
    return 0.5 * (1.0 + tangent) + 0.5 * inputs * (1.0 - tangent * tangent) * root_two_pi * (1.0 + 3.0 * 0.044715 * inputs * inputs)

def line_probs(queries, key_rows):
    scale = queries.shape[-1] ** (-0.5)
    scores = jnp.einsum('blhe,bmhe->bhlm', queries.astype(jnp.float32), key_rows.astype(jnp.float32)) * scale
    top = lax.optimization_barrier(jnp.max(scores, axis=-1, keepdims=True))
    weights = jnp.exp(scores - top)
    return weights / lax.optimization_barrier(jnp.sum(weights, axis=-1, keepdims=True))

def attend_lines(queries, key_rows, value_rows):
    probs = line_probs(queries, key_rows)
    rounded = lax.optimization_barrier(probs.astype(jnp.bfloat16)).astype(jnp.float32)
    return jnp.einsum('bhlm,bmhe->blhe', rounded, value_rows.astype(jnp.float32))

def attend_back(queries, key_rows, value_rows, grad_lines):
    scale = queries.shape[-1] ** (-0.5)
    probs = line_probs(queries, key_rows)
    rounded = lax.optimization_barrier(probs.astype(jnp.bfloat16)).astype(jnp.float32)
    grad_float = grad_lines.astype(jnp.float32)
    grad_values = jnp.einsum('bhlm,blhe->bmhe', rounded, grad_float)
    grad_probs = jnp.einsum('blhe,bmhe->bhlm', grad_float, value_rows.astype(jnp.float32))
    grad_scores = probs * (grad_probs - lax.optimization_barrier(jnp.sum(probs * grad_probs, axis=-1, keepdims=True)))
    score_b = lax.optimization_barrier(grad_scores.astype(jnp.bfloat16)).astype(jnp.float32)
    grad_queries = jnp.einsum('bhlm,bmhe->blhe', score_b, key_rows.astype(jnp.float32)) * scale
    grad_keys = jnp.einsum('bhlm,blhe->bmhe', score_b, queries.astype(jnp.float32)) * scale
    return (grad_queries, grad_keys, grad_values)

def lines_x(grid):
    return grid.reshape(grid.shape[0] * grid.shape[1], grid.shape[2], grid.shape[3], grid.shape[4])

def lines_y(grid):
    return jnp.swapaxes(grid, 1, 2).reshape(grid.shape[0] * grid.shape[2], grid.shape[1], grid.shape[3], grid.shape[4])

def unlines_y(lines, shape):
    return jnp.swapaxes(lines.reshape(shape[0], shape[2], shape[1], shape[3], shape[4]), 1, 2)

def lines_z(grid):
    return jnp.transpose(grid, (1, 2, 0, 3, 4)).reshape(grid.shape[1] * grid.shape[2], grid.shape[0], grid.shape[3], grid.shape[4])

def unlines_z(lines, shape):
    return jnp.transpose(lines.reshape(shape[1], shape[2], shape[0], shape[3], shape[4]), (2, 0, 1, 3, 4))

def case_step(totals, inputs):
    tokens_case, cotangent_case, w_qkv, w_out, w_up, w_down, gain_attn, gain_mlp = inputs
    depth, height, across, width = tokens_case.shape
    count = depth * height * across
    head_size = width // HEADS
    shape = (depth, height, across, HEADS, head_size)
    flat = tokens_case.reshape(count, width).astype(jnp.float32)
    normed_one, inverse_one, hidden_one = normalize(flat, gain_attn)
    projected = jnp.dot(hidden_one, w_qkv, preferred_element_type=jnp.float32).astype(jnp.bfloat16)
    queries = projected[:, :width].reshape(shape)
    key_rows = projected[:, width:2 * width].reshape(shape)
    value_rows = projected[:, 2 * width:].reshape(shape)
    out_x = attend_lines(lines_x(queries), lines_x(key_rows), lines_x(value_rows)).reshape(shape)
    out_y = unlines_y(attend_lines(lines_y(queries), lines_y(key_rows), lines_y(value_rows)), shape)
    out_z = unlines_z(attend_lines(lines_z(queries), lines_z(key_rows), lines_z(value_rows)), shape).astype(jnp.bfloat16)
    mixed = (out_x + out_y + out_z.astype(jnp.float32)).reshape(count, width).astype(jnp.bfloat16)
    residual = (flat + jnp.dot(mixed, w_out, preferred_element_type=jnp.float32)).astype(jnp.bfloat16)
    normed_two, inverse_two, hidden_two = normalize(residual.astype(jnp.float32), gain_mlp)
    upper = jnp.dot(hidden_two, w_up, preferred_element_type=jnp.float32)
    active = gelu_value(upper).astype(jnp.bfloat16)
    grad_rows = cotangent_case.reshape(count, width)
    grad_active = jnp.dot(grad_rows, w_down.T, preferred_element_type=jnp.float32)
    total_down = jnp.dot(active.T, grad_rows, preferred_element_type=jnp.float32)
    grad_upper = (grad_active * gelu_slope(upper)).astype(jnp.bfloat16)
    total_up = jnp.dot(hidden_two.T, grad_upper, preferred_element_type=jnp.float32)
    grad_hidden_two = jnp.dot(grad_upper, w_up.T, preferred_element_type=jnp.float32)
    total_gain_two = lax.optimization_barrier(jnp.sum(grad_hidden_two * normed_two, axis=0))
    grad_residual = grad_rows.astype(jnp.float32) + norm_back(grad_hidden_two, normed_two, inverse_two, gain_mlp)
    grad_res_b = grad_residual.astype(jnp.bfloat16)
    total_out = jnp.dot(mixed.T, grad_res_b, preferred_element_type=jnp.float32)
    grad_mixed = jnp.dot(grad_res_b, w_out.T, preferred_element_type=jnp.float32).astype(jnp.bfloat16).reshape(shape)
    back_x = attend_back(lines_x(queries), lines_x(key_rows), lines_x(value_rows), lines_x(grad_mixed))
    back_y = attend_back(lines_y(queries), lines_y(key_rows), lines_y(value_rows), lines_y(grad_mixed))
    back_z = attend_back(lines_z(queries), lines_z(key_rows), lines_z(value_rows), lines_z(grad_mixed))
    columns = []
    columns_z = []
    for which in range(3):
        part_x = back_x[which].reshape(shape)
        part_y = unlines_y(back_y[which], shape)
        columns.append((part_x + part_y).reshape(count, width))
        columns_z.append(unlines_z(back_z[which], shape).astype(jnp.bfloat16).reshape(count, width))
    grad_proj = jnp.concatenate(columns, axis=1).astype(jnp.bfloat16)
    grad_proj_z = jnp.concatenate(columns_z, axis=1)
    total_qkv = jnp.dot(hidden_one.T, grad_proj, preferred_element_type=jnp.float32) + jnp.dot(hidden_one.T, grad_proj_z, preferred_element_type=jnp.float32)
    grad_hidden_one = jnp.dot(grad_proj, w_qkv.T, preferred_element_type=jnp.float32) + jnp.dot(grad_proj_z, w_qkv.T, preferred_element_type=jnp.float32)
    total_gain_one = lax.optimization_barrier(jnp.sum(grad_hidden_one * normed_one, axis=0))
    grad_tokens = (grad_residual + norm_back(grad_hidden_one, normed_one, inverse_one, gain_attn)).astype(jnp.bfloat16)
    updated = (totals[0] + total_qkv, totals[1] + total_out, totals[2] + total_up, totals[3] + total_down, totals[4] + total_gain_one, totals[5] + total_gain_two)
    return (updated, grad_tokens.reshape(depth, height, across, width))

def reference(tokens, cotangent, w_qkv, w_out, w_up, w_down, gain_attn, gain_mlp):
    width = tokens.shape[-1]
    hidden_units = w_up.shape[1]
    start = (jnp.zeros((width, 3 * width), jnp.float32), jnp.zeros((width, width), jnp.float32), jnp.zeros((width, hidden_units), jnp.float32), jnp.zeros((hidden_units, width), jnp.float32), jnp.zeros((width,), jnp.float32), jnp.zeros((width,), jnp.float32))

    def step(totals, pair):
        return case_step(totals, (pair[0], pair[1], w_qkv, w_out, w_up, w_down, gain_attn, gain_mlp))
    totals, grad_tokens = lax.scan(step, start, (tokens, cotangent))
    factor = 1.0 / math.sqrt(TOKENS_ALL)
    return (grad_tokens, totals[0] * factor, totals[1] * factor, totals[2] * factor, totals[3] * factor, totals[4] * factor, totals[5] * factor)
```

```python
import functools
import math

import jax
import jax.numpy as jnp
from jax import lax
from jax.experimental import pallas as pl
from jax.experimental.pallas import tpu as pltpu
from jax.sharding import PartitionSpec as P

HEADS = 8
LANES = 128
EPSILON = 1e-06
ROOT_TWO_PI = math.sqrt(2.0 / math.pi)
F32 = jnp.float32
BF16 = jnp.bfloat16
BOTH = ("slab", "case")
VMEM_BYTES = 24 * 1024 * 1024


def dot(a, b):
    return lax.dot_general(a, b, (((1,), (0,)), ((), ())), preferred_element_type=F32)


def dot_nt(a, b):
    return lax.dot_general(a, b, (((1,), (1,)), ((), ())), preferred_element_type=F32)


def dot_tn(a, b):
    return lax.dot_general(a, b, (((0,), (0,)), ((), ())), preferred_element_type=F32)


def norm_stats(values):
    inverse = lax.rsqrt(jnp.mean(values * values, axis=-1, keepdims=True) + EPSILON)
    return values * inverse, inverse


def norm_back(scaled, normed, inverse):
    return inverse * (scaled - normed * jnp.mean(scaled * normed, axis=-1, keepdims=True))


def call(kernel, outs, *args, after=(), scratch=(), near=None, flops=10**7):
    count = len(args)
    near = [True] * count if near is None else near

    def run(*refs):
        kernel(*refs[:count], *refs[count + len(after) :])

    vmem, far = pl.BlockSpec(memory_space=pltpu.VMEM), pl.BlockSpec(memory_space=pltpu.HBM)
    return pl.pallas_call(
        run,
        out_shape=outs,
        in_specs=[vmem if one else far for one in near] + [pl.BlockSpec(memory_space=pl.ANY)] * len(after),
        out_specs=[vmem] * len(outs),
        scratch_shapes=list(scratch),
        cost_estimate=pl.CostEstimate(flops=flops, transcendentals=0, bytes_accessed=10**4),
        compiler_params=pltpu.CompilerParams(vmem_limit_bytes=VMEM_BYTES),
    )(
        *[
            arg if one else pltpu.with_memory_space_constraint(arg, pltpu.HBM)
            for arg, one in zip(args, near)
        ],
        *after,
    )


def shape_of(shape, dtype):
    return jax.ShapeDtypeStruct(shape, dtype)


def line_masks(sizes, kind):
    depth, per, across, count = sizes
    rows = lax.broadcasted_iota(jnp.int32, (2 * count, count), 0) & (count - 1)
    cols = lax.broadcasted_iota(jnp.int32, (2 * count, count), 1)

    def parts(t):
        chunk = t // (depth * per)
        plane = (t // per) & (depth - 1)
        spot = chunk * per + (t & (per - 1))
        return plane, spot // across, spot & (across - 1), t & (per - 1)

    a, b = parts(rows), parts(cols)
    if kind == "z":
        return [a[3] == b[3]]
    same = a[0] == b[0]
    return [same & (a[1] == b[1]), same & (a[2] == b[2])]


def softmax_in(scores, mask):
    held = jnp.where(mask, scores, -1e30)
    weights = jnp.exp(held - jnp.max(held, axis=-1, keepdims=True))
    return weights / jnp.sum(weights, axis=-1, keepdims=True)


def pair_parts(proj, pair, width):
    at = pair * LANES
    return [proj[:, which * width + at : which * width + at + LANES] for which in range(3)]


def halves():
    lane = lax.broadcasted_iota(jnp.int32, (1, LANES), 1)
    low = (lane < LANES // 2).astype(F32)
    return low.astype(BF16), (1.0 - low).astype(BF16)


def stack(block, low, high):
    return jnp.concatenate([block * low, block * high], axis=0)


def side(block):
    count = block.shape[0] // 2
    return jnp.concatenate([block[:count], block[count:]], axis=1)


def attend(proj, masks, width):
    low, high = halves()
    scale = (width // HEADS) ** (-0.5)
    outs = []
    for pair in range(HEADS // 2):
        q2, k2, v2 = pair_parts(proj, pair, width)
        scores = dot_nt(stack(q2, low, high), k2) * scale
        probs = sum(softmax_in(scores, mask).astype(BF16).astype(F32) for mask in masks)
        outs.append(dot(side(probs.astype(BF16)), stack(v2, low, high)))
    return jnp.concatenate(outs, axis=1)


def attend_back(proj, grad, masks, width, out_ref, at):
    low, high = halves()
    scale = (width // HEADS) ** (-0.5)
    for pair in range(HEADS // 2):
        q2, k2, v2 = pair_parts(proj, pair, width)
        g2 = grad[:, pair * LANES : (pair + 1) * LANES]
        qs, gs = stack(q2, low, high), stack(g2, low, high)
        scores = dot_nt(qs, k2) * scale
        grad_probs = dot_nt(gs, v2)
        probs = jnp.zeros_like(scores)
        grad_scores = jnp.zeros_like(scores)
        for mask in masks:
            one = softmax_in(scores, mask)
            probs += one.astype(BF16).astype(F32)
            grad_scores += one * (grad_probs - jnp.sum(one * grad_probs, axis=-1, keepdims=True))
        probs, grad_scores = probs.astype(BF16), grad_scores.astype(BF16)
        found = (
            dot(side(grad_scores), stack(k2, low, high)) * scale,
            dot_tn(grad_scores, qs) * scale,
            dot_tn(probs, gs),
        )
        for which in range(3):
            start = at + which * width + pair * LANES
            out_ref[0 : q2.shape[0], start : start + LANES] = found[which].astype(BF16)


def chunk_order(sizes, parts):
    depth, per, _, count = sizes
    rows = lax.broadcasted_iota(jnp.int32, (count, count), 0)
    cols = lax.broadcasted_iota(jnp.int32, (count, count), 1)
    chunk = rows // (depth * per)
    if parts > 1:
        chunk = chunk ^ lax.axis_index("slab")
    plane = (rows // per) & (depth - 1)
    return plane * (count // depth) + chunk * per + (rows & (per - 1)) == cols


def put_parts(refs, at, value):
    rows = refs[0].shape[0]
    for j, ref in enumerate(refs):
        ref[:, at : at + value.shape[1]] = value[j * rows : (j + 1) * rows]


def joined(refs, start, stop):
    return jnp.concatenate([ref[:, start:stop] for ref in refs], axis=0)


def plane_kernel(sizes, x_ref, cot_ref, gain_ref, w_ref, *refs):
    parts, hold_x = refs[:-7], refs[-7]
    x_in, cot_in, gain_in, w_in, proj, sems = refs[-6:]
    copies = [
        pltpu.make_async_copy(src, dst, sems.at[i])
        for i, (src, dst) in enumerate(
            ((x_ref, x_in), (gain_ref, gain_in), (w_ref, w_in), (cot_ref, cot_in))
        )
    ]
    for copy in copies:
        copy.start()
    width = w_in.shape[0]
    order = chunk_order(sizes, len(parts)).astype(F32).astype(BF16)
    masks = line_masks(sizes, "xy")
    copies[0].wait()
    x = dot(order, x_in[...])
    hold_x[...] = x.astype(BF16)
    put_parts(parts, 0, hold_x[...])
    copies[1].wait()
    normed, _ = norm_stats(x)
    hidden = (normed * gain_in[...]).astype(BF16)
    copies[2].wait()
    proj[...] = dot(hidden, w_in[...]).astype(BF16)
    put_parts(parts, 2 * width, attend(proj[...], masks, width).astype(BF16))
    copies[3].wait()
    put_parts(parts, width, dot(order, cot_in[...]).astype(BF16))


def prepare_kernel(slabs, w_up_ref, w_down_ref, up_ref, down_ref):
    x = lax.axis_index("slab") & 1
    quarter = lax.axis_index("case")
    units = w_up_ref.shape[1]
    fine = units // slabs // 4
    rows = lax.broadcasted_iota(jnp.int32, (8 * LANES, LANES), 0)
    cols = lax.broadcasted_iota(jnp.int32, (8 * LANES, LANES), 1)
    wanted = ((cols // fine * 2 + x) * 4 + quarter) * fine + (cols & (fine - 1))
    pick = (rows == wanted).astype(F32).astype(BF16)
    for group in range(up_ref.shape[1] // LANES):
        up_ref[:, group * LANES : (group + 1) * LANES] = dot(
            w_up_ref[:, group * 8 * LANES : (group + 1) * 8 * LANES], pick
        ).astype(BF16)
    for z in range(slabs // 2):
        start = pl.multiple_of(((z * 2 + x) * 4 + quarter) * fine, 8)
        down_ref[z * fine : (z + 1) * fine, :] = w_down_ref[pl.ds(start, fine), :]


def lines_kernel(sizes, parts, *refs):
    got = refs[:parts]
    gain_one_ref, gain_two_ref, w_ref, w_out_ref = refs[parts : parts + 4]
    shared_ref, proj_ref, mixed_ref, residual_ref, hold_x = refs[parts + 4 :]
    width = w_ref.shape[0]
    hold_x[...] = joined(got, 0, width)
    x = hold_x[...].astype(F32)
    normed, _ = norm_stats(x)
    proj_ref[...] = dot((normed * gain_one_ref[...]).astype(BF16), w_ref[...]).astype(BF16)
    out_z = attend(proj_ref[...], line_masks(sizes, "z"), width).astype(BF16)
    mixed = (joined(got, 2 * width, 3 * width).astype(F32) + out_z.astype(F32)).astype(BF16)
    residual = (x + dot(mixed, w_out_ref[...])).astype(BF16)
    normed_two, _ = norm_stats(residual.astype(F32))
    shared_ref[:, :width] = (normed_two * gain_two_ref[...]).astype(BF16)
    shared_ref[:, width:] = joined(got, width, 2 * width)
    mixed_ref[...] = mixed
    residual_ref[...] = residual


def gelu_parts(upper):
    square = upper * upper
    tangent = jnp.tanh(ROOT_TWO_PI * (upper + 0.044715 * upper * square))
    half = 0.5 * (1.0 + tangent)
    slope = half + 0.5 * upper * (1.0 - tangent * tangent) * ROOT_TWO_PI * (
        1.0 + 3.0 * 0.044715 * square
    )
    return (upper * half).astype(BF16), slope


def mlp_kernel(
    shared_ref, residual_ref, gain_ref, w_out_ref, w_up_ref, w_down_ref, grad_ref, gres_ref
):
    width, units = w_up_ref.shape
    hidden, cot = shared_ref[:, :width], shared_ref[:, width:]
    normed, inverse = norm_stats(residual_ref[...].astype(F32))
    step = min(512, units)
    grad_hidden = jnp.zeros(normed.shape, F32)
    for at in range(0, units, step):
        _, slope = gelu_parts(dot(hidden, w_up_ref[:, at : at + step]))
        grad_upper = (dot_nt(cot, w_down_ref[at : at + step, :]) * slope).astype(BF16)
        grad_hidden += dot_nt(grad_upper, w_up_ref[:, at : at + step])
    grad_residual = cot.astype(F32) + norm_back(grad_hidden * gain_ref[...], normed, inverse)
    gres_ref[...] = grad_residual
    grad_ref[...] = dot_nt(grad_residual.astype(BF16), w_out_ref[...]).astype(BF16)


def lines_back_kernel(sizes, proj_ref, grad_ref, gres_ref, mixed_ref, x_ref, gain_ref, w_ref, *refs):
    backs, pack_ref = refs[:-1], refs[-1]
    width = w_ref.shape[0]
    put_parts(backs, 0, grad_ref[...])
    pack_ref[:, 4 * width : 5 * width] = mixed_ref[...]
    pack_ref[:, 5 * width :] = gres_ref[...].astype(BF16)
    attend_back(proj_ref[...], grad_ref[...], line_masks(sizes, "z"), width, pack_ref, width)
    normed, inverse = norm_stats(x_ref[...].astype(F32))
    pack_ref[:, :width] = (normed * gain_ref[...]).astype(BF16)
    grad_hidden = dot_nt(pack_ref[:, width : 4 * width], w_ref[...])
    back = norm_back(grad_hidden * gain_ref[...], normed, inverse)
    put_parts(backs, width, (gres_ref[...] + back).astype(BF16))


def join_kernel(*refs):
    put = refs[-1]
    rows = refs[0].shape[0]
    for j, ref in enumerate(refs[:-1]):
        put[j * rows : (j + 1) * rows, :] = ref[...]


def plane_grads_kernel(sizes, parts, *refs):
    backs = refs[:parts]
    x_ref, gain_ref, w_ref, pack_ref, proj = refs[parts:]
    width = w_ref.shape[0]
    normed, _ = norm_stats(x_ref[...].astype(F32))
    pack_ref[:, :width] = (normed * gain_ref[...]).astype(BF16)
    proj[...] = dot(pack_ref[:, :width], w_ref[...]).astype(BF16)
    grad = joined(backs, 0, width)
    attend_back(proj[...], grad, line_masks(sizes, "xy"), width, pack_ref, width)


def plane_tokens_kernel(sizes, parts, *refs):
    backs = refs[:parts]
    pack_ref, x_ref, gain_ref, w_ref, grad_ref = refs[parts:]
    width = w_ref.shape[0]
    normed, inverse = norm_stats(x_ref[...].astype(F32))
    grad_hidden = dot_nt(pack_ref[:, width:], w_ref[...])
    back = norm_back(grad_hidden * gain_ref[...], normed, inverse)
    part = joined(backs, width, 2 * width).astype(F32)
    order = chunk_order(sizes, parts).astype(F32).astype(BF16)
    grad_ref[...] = dot_tn(order, (back + part).astype(BF16)).astype(BF16)


def place():
    slab, case = lax.axis_index("slab"), lax.axis_index("case")
    return slab & 1, case >> 1, case & 1, slab >> 1


def store_units(scratch, rows, units, x, flip, outs, at):
    blocks = outs[0].shape[0]
    for z in range(blocks):
        start = pl.multiple_of((z * 2 + (x ^ flip)) * rows, 8)
        block = scratch[pl.ds(start, rows), 0 : units * LANES].astype(BF16)
        for unit in range(units):
            outs[flip][z, at + unit * rows : at + (unit + 1) * rows, :] = block[
                :, unit * LANES : (unit + 1) * LANES
            ]


def grads_mlp_kernel(factor, shift, here_ref, there_ref, w_up_ref, w_down_ref, *refs):
    outs, down, up = refs[:-2], refs[-2], refs[-1]
    width, units = w_up_ref.shape
    slab = lax.axis_index("slab")
    digit = (slab >> shift) & (len(outs) - 1)
    hidden = jnp.concatenate([ref[:, :width] for ref in (here_ref, there_ref)], axis=0)
    cot = jnp.concatenate([ref[:, width:] for ref in (here_ref, there_ref)], axis=0)
    active, slope = gelu_parts(dot(hidden, w_up_ref[...]))
    grad_upper = (dot_nt(cot, w_down_ref[...]) * slope).astype(BF16)
    down[...] = dot_tn(active, cot) * factor
    up[...] = dot_tn(hidden, grad_upper) * factor
    rest, rows = outs[0].shape[:2]
    for j, out in enumerate(outs):
        for k in range(rest):
            z = (digit ^ j) * rest + k
            at = pl.ds(pl.multiple_of(z * rows, 8), rows)
            out[k, :, :width] = down[at, :].astype(BF16)
            for flip in range(2):
                at = pl.ds(pl.multiple_of((z * 2 + ((slab & 1) ^ flip)) * rows, 8), rows)
                out[k, :, width + flip * units : width + (flip + 1) * units] = up[at, :].astype(BF16)


def total_kernel(keep, *refs):
    ins, (mine_ref, other_ref) = refs[:-2], refs[-2:]
    total = sum(ref[0].astype(F32) for ref in ins).astype(BF16)
    mine_ref[...] = total[:, :keep]
    other_ref[...] = total[:, keep:]


def beside_kernel(a_ref, b_ref, out_ref):
    out_ref[...] = jnp.concatenate([a_ref[...], b_ref[...]], axis=1)


def grads_qkv_kernel(factor, width, slabs, za_ref, zb_ref, pa_ref, pb_ref, *refs):
    outs, scratch = refs[:4], refs[4]
    x, y, core, _ = place()
    size, narrow = 3 * width // 4, width // 4
    rows = width // slabs
    hidden = jnp.concatenate([r[:, :width] for r in (za_ref, zb_ref, pa_ref, pb_ref)], axis=0)
    mixed = jnp.concatenate([r[:, 4 * width : 5 * width] for r in (za_ref, zb_ref)], axis=0)
    for flip_y in range(2):
        quarter = (y ^ flip_y) * 2 + core
        at = pl.multiple_of(width + quarter * size, LANES)
        cols = jnp.concatenate(
            [r[:, pl.ds(at, size)] for r in (za_ref, zb_ref, pa_ref, pb_ref)], axis=0
        )
        scratch[:, :size] = dot_tn(hidden, cols) * factor
        at = pl.multiple_of(5 * width + quarter * narrow, LANES)
        cols = jnp.concatenate([r[:, pl.ds(at, narrow)] for r in (za_ref, zb_ref)], axis=0)
        scratch[:, size:] = dot_tn(mixed, cols) * factor
        for flip in range(2):
            store_units(scratch, rows, width // LANES, x, flip, outs[2 * flip_y : 2 * flip_y + 2], 0)


def fold_kernel(shift, radix, count, *refs):
    ins, outs = refs[:count], refs[count:]
    digit = (lax.axis_index("slab") >> shift) & (radix - 1)
    rest = ins[0].shape[0] // radix
    for j in range(radix):
        for k in range(rest):
            at = (digit ^ j) * rest + k
            total = ins[0][at].astype(F32)
            for ref in ins[1:]:
                total += ref[at].astype(F32)
            outs[j][k] = total.astype(BF16)


def fold(shift, radix, pieces, after=()):
    first = pieces[0].shape
    outs = [shape_of((first[0] // radix,) + first[1:], BF16)] * radix
    kernel = functools.partial(fold_kernel, shift, radix, len(pieces))
    return call(kernel, outs, *pieces, after=after)


def swap_pairs(slabs, cases, flip_slab, flip_case):
    return [
        (s * cases + c, (s ^ flip_slab) * cases + (c ^ flip_case))
        for s in range(slabs)
        for c in range(cases)
    ]


def gain_sums(grad, w_rows, gain_ref):
    rows, width = grad.shape[0], gain_ref.shape[1]
    spot = lax.axis_index("slab") * rows + lax.broadcasted_iota(jnp.int32, (rows, width), 0)
    lanes = lax.broadcasted_iota(jnp.int32, (rows, width), 1)
    gain = jnp.sum(jnp.where(lanes == spot, gain_ref[...], 0.0), axis=1, keepdims=True)
    total = jnp.sum(grad * w_rows.astype(F32), axis=1, keepdims=True) / gain
    return jnp.transpose(jnp.broadcast_to(total, (rows, LANES)))[0:1, :]


def place_mlp_kernel(slabs, width, units, *refs):
    pieces, (gain_ref, w_up_ref, w_ref) = refs[:4], refs[4:7]
    up, down, two, w_rows, held, up_rows, sems = refs[7:]
    rows = width // slabs
    here = pl.ds(pl.multiple_of(lax.axis_index("slab") * rows, 8), rows)
    copies = [
        pltpu.make_async_copy(w_up_ref.at[here], up_rows, sems.at[0]),
        pltpu.make_async_copy(w_ref.at[here], w_rows, sems.at[1]),
    ]
    for copy in copies:
        copy.start()
    case, x = lax.axis_index("case"), lax.axis_index("slab") & 1
    eighth, fine = units // 8, units // 4 // slabs
    for j in range(4):
        piece = pieces[j][...].astype(F32)
        held[case ^ j, :, :width] = piece[:, :width]
        for flip in range(2):
            at = pl.multiple_of(width + (x ^ flip) * eighth, LANES)
            held[case ^ j, :, pl.ds(at, eighth)] = piece[
                :, width + flip * eighth : width + (flip + 1) * eighth
            ]
    for quarter in range(4):
        down[quarter * rows : (quarter + 1) * rows, :] = held[quarter, :, :width]
    for block in range(slabs):
        up[:, block * 4 * fine : (block + 1) * 4 * fine] = jnp.concatenate(
            [
                held[quarter, :, pl.ds(width + block % 2 * eighth + block // 2 * fine, fine)]
                for quarter in range(4)
            ],
            axis=1,
        )
    for copy in copies:
        copy.wait()
    two[...] = gain_sums(up[...], up_rows[...], gain_ref)


def place_qkv_kernel(slabs, width, *refs):
    pieces, (gain_ref, w_rows), (qkv, out, one) = refs[:4], refs[4:6], refs[6:]
    case = lax.axis_index("case")
    rows = width // slabs
    size = 3 * width // 4
    for j in range(4):
        quarter = case ^ j
        for unit in range(width // LANES):
            piece = pieces[j][0, unit * rows : (unit + 1) * rows, :].astype(F32)
            if unit < size // LANES:
                start = pl.multiple_of(quarter * size + unit * LANES, LANES)
                qkv[:, pl.ds(start, LANES)] = piece
            else:
                start = pl.multiple_of(quarter * (width // 4) + unit * LANES - size, LANES)
                out[:, pl.ds(start, LANES)] = piece
    one[...] = gain_sums(qkv[...], w_rows[...], gain_ref)


def body(tokens, cotangent, w_qkv, w_out, w_up, w_down, gain_attn, gain_mlp):
    slabs, cases = lax.axis_size("slab"), lax.axis_size("case")
    depth, height, across, width = tokens.shape[1:]
    units = w_up.shape[1]
    lines = height * across
    per = lines // slabs
    count = depth * lines
    sizes = (depth, per, across, count)
    factor = 1.0 / math.sqrt(count * slabs * cases)
    gain_one, gain_two = gain_attn.reshape(1, width), gain_mlp.reshape(1, width)
    spans = slabs // 2
    rows = width // slabs
    parts = slabs if depth * per % 16 == 0 else 1

    def permute(array, flip_slab, flip_case):
        return lax.ppermute(array, BOTH, swap_pairs(slabs, cases, flip_slab, flip_case))

    def exchange(blocks):
        if parts == 1:
            return [lax.all_to_all(blocks[0], "slab", split_axis=0, concat_axis=0, tiled=True)]
        got = {j: permute(blocks[j], j, 0) for j in range(parts - 1, 0, -1)}
        return [blocks[0]] + [got[j] for j in range(1, parts)]

    proj_bf = shape_of((count, 3 * width), BF16)
    rows_bf = shape_of((count, width), BF16)
    *mine, hold_x = call(
        functools.partial(plane_kernel, sizes),
        [shape_of((count // parts, 3 * width), BF16)] * parts + [rows_bf],
        tokens.reshape(count, width),
        cotangent.reshape(count, width),
        gain_one,
        w_qkv,
        near=[False] * 4,
        scratch=[
            pltpu.VMEM((count, width), BF16),
            pltpu.VMEM((count, width), BF16),
            pltpu.VMEM((1, width), F32),
            pltpu.VMEM((width, 3 * width), BF16),
            pltpu.VMEM((count, 3 * width), BF16),
            pltpu.SemaphoreType.DMA((4,)),
        ],
    )
    w_up_mine, w_down_mine = call(
        functools.partial(prepare_kernel, slabs),
        [shape_of((width, units // 8), BF16), shape_of((units // 8, width), BF16)],
        w_up,
        w_down,
    )
    got = exchange(mine)
    shared, proj_z, mixed, residual, hold_z = call(
        functools.partial(lines_kernel, sizes, parts),
        [shape_of((count, 2 * width), BF16), proj_bf, rows_bf, rows_bf, rows_bf],
        *got,
        gain_one,
        gain_two,
        w_qkv,
        w_out,
        after=[w_up_mine],
    )
    around = [shared, permute(shared, 0, 2), permute(shared, 1, 0), permute(shared, 1, 2)]
    grad_mixed, grad_residual = call(
        mlp_kernel,
        [rows_bf, shape_of((count, width), F32)],
        shared,
        residual,
        gain_two,
        w_out,
        w_up,
        w_down,
    )
    *backs, pack_z = call(
        functools.partial(lines_back_kernel, sizes),
        [shape_of((count // parts, 2 * width), BF16)] * parts + [shape_of((count, 6 * width), BF16)],
        proj_z,
        grad_mixed,
        grad_residual,
        mixed,
        hold_z,
        gain_one,
        w_qkv,
    )
    backs = exchange(backs)
    (around,) = call(
        join_kernel, [shape_of((4 * count, 2 * width), BF16)], *around, after=backs[1:]
    )
    around_core = permute(around, 0, 1)
    radix = min(4, spans)
    shift = (slabs // radix).bit_length() - 1
    big = call(
        functools.partial(grads_mlp_kernel, factor, shift),
        [shape_of((spans // radix, rows, 2 * width), BF16)] * radix,
        around,
        around_core,
        w_up_mine,
        w_down_mine,
        scratch=[pltpu.VMEM((units // 8, width), F32), pltpu.VMEM((width, units // 8), F32)],
    )
    pack_z_core = permute(pack_z, 0, 1)
    def reduce_z(split):
        left = spans
        while True:
            radix = len(split)
            left //= radix
            shift = (left * 2).bit_length() - 1
            pieces = [split[0]] + [permute(split[j], j << shift, 0) for j in range(1, radix)]
            if left == 1:
                return pieces
            radix = min(4, left)
            split = fold((left // radix * 2).bit_length() - 1, radix, pieces)

    def gather(last):
        return [last] + [permute(last, 0, j) for j in range(1, 4)]

    early = big[0]
    big = reduce_z(big)
    (pack_p,) = call(
        functools.partial(plane_grads_kernel, sizes, parts),
        [shape_of((count, 4 * width), BF16)],
        *backs,
        hold_x,
        gain_one,
        w_qkv,
        scratch=[pltpu.VMEM((count, 3 * width), BF16)],
    )
    small = call(
        functools.partial(grads_qkv_kernel, factor, width, slabs),
        [shape_of((spans, rows * (width // LANES), LANES), BF16)] * 4,
        pack_z,
        pack_z_core,
        pack_p,
        permute(pack_p, 0, 1),
        after=[early],
        scratch=[pltpu.VMEM((width, width), F32)],
    )
    ready = small[0]
    small = [small[0], permute(small[1], 1, 0), permute(small[2], 0, 2), permute(small[3], 1, 2)]
    (grad_tokens,) = call(
        functools.partial(plane_tokens_kernel, sizes, parts),
        [rows_bf],
        *backs,
        pack_p,
        hold_x,
        gain_one,
        w_qkv,
        after=[ready],
    )

    small = reduce_z(fold(shift, radix, small))
    keep = width + units // 8
    mine_big, other_big = call(
        functools.partial(total_kernel, keep),
        [shape_of((rows, keep), BF16), shape_of((rows, units // 8), BF16)],
        *big,
        after=[small[0]],
    )
    (last,) = call(
        beside_kernel, [shape_of((rows, 2 * width), BF16)], mine_big, permute(other_big, 1, 0)
    )
    big = gather(last)
    full_up, full_down, full_two, w_rows = call(
        functools.partial(place_mlp_kernel, slabs, width, units),
        [
            shape_of((rows, units), F32),
            shape_of((units // slabs, width), F32),
            shape_of((1, rows), F32),
            shape_of((rows, 3 * width), BF16),
        ],
        *big,
        gain_two,
        w_up,
        w_qkv,
        near=[True] * 5 + [False] * 2,
        scratch=[
            pltpu.VMEM((4, rows, 2 * width), F32),
            pltpu.VMEM((rows, units), BF16),
            pltpu.SemaphoreType.DMA((2,)),
        ],
    )
    small = gather(fold(0, 1, small)[0])
    full_qkv, full_out, full_one = call(
        functools.partial(place_qkv_kernel, slabs, width),
        [shape_of((rows, 3 * width), F32), shape_of((rows, width), F32), shape_of((1, rows), F32)],
        *small,
        gain_one,
        w_rows,
    )
    return (
        grad_tokens.reshape(tokens.shape),
        full_qkv,
        full_out,
        full_up,
        full_down,
        full_one.reshape(rows),
        full_two.reshape(rows),
    )


def solution(mesh):
    grid = P("case", "slab", None, None, None)
    return jax.shard_map(
        body,
        mesh=mesh,
        in_specs=(grid, grid, P(), P(), P(), P(), P(), P()),
        out_specs=(
            grid,
            P("slab", None),
            P("slab", None),
            P("slab", None),
            P("slab", None),
            P("slab"),
            P("slab"),
        ),
        check_vma=False,
    )
```

```python
import functools
import math

import jax
import jax.numpy as jnp
from jax import lax
from jax.experimental import pallas as pl
from jax.experimental.pallas import tpu as pltpu
from jax.sharding import PartitionSpec as P

HEADS = 8
LANES = 128
EPSILON = 1e-06
ROOT_TWO_PI = math.sqrt(2.0 / math.pi)
F32 = jnp.float32
BF16 = jnp.bfloat16
BOTH = ("slab", "case")
VMEM_BYTES = 16 * 1024 * 1024


def dot(a, b):
    return lax.dot_general(a, b, (((1,), (0,)), ((), ())), preferred_element_type=F32)


def dot_nt(a, b):
    return lax.dot_general(a, b, (((1,), (1,)), ((), ())), preferred_element_type=F32)


def dot_tn(a, b):
    return lax.dot_general(a, b, (((0,), (0,)), ((), ())), preferred_element_type=F32)


def norm_stats(values):
    inverse = lax.rsqrt(jnp.mean(values * values, axis=-1, keepdims=True) + EPSILON)
    return values * inverse, inverse


def norm_back(scaled, normed, inverse):
    return inverse * (scaled - normed * jnp.mean(scaled * normed, axis=-1, keepdims=True))


def call(kernel, outs, *args, after=(), scratch=(), near=None, flops=10**7):
    count = len(args)
    near = [True] * count if near is None else near

    def run(*refs):
        kernel(*refs[:count], *refs[count + len(after) :])

    vmem, far = pl.BlockSpec(memory_space=pltpu.VMEM), pl.BlockSpec(memory_space=pltpu.HBM)
    return pl.pallas_call(
        run,
        out_shape=outs,
        in_specs=[vmem if one else far for one in near] + [pl.BlockSpec(memory_space=pl.ANY)] * len(after),
        out_specs=[vmem] * len(outs),
        scratch_shapes=list(scratch),
        cost_estimate=pl.CostEstimate(flops=flops, transcendentals=0, bytes_accessed=10**4),
        compiler_params=pltpu.CompilerParams(vmem_limit_bytes=VMEM_BYTES),
    )(
        *[
            arg if one else pltpu.with_memory_space_constraint(arg, pltpu.HBM)
            for arg, one in zip(args, near)
        ],
        *after,
    )


def shape_of(shape, dtype):
    return jax.ShapeDtypeStruct(shape, dtype)


def line_masks(sizes, kind):
    depth, per, across, count = sizes
    rows = lax.broadcasted_iota(jnp.int32, (2 * count, count), 0) & (count - 1)
    cols = lax.broadcasted_iota(jnp.int32, (2 * count, count), 1)

    def parts(t):
        chunk = t // (depth * per)
        plane = (t // per) & (depth - 1)
        spot = chunk * per + (t & (per - 1))
        return plane, spot // across, spot & (across - 1), t & (per - 1)

    a, b = parts(rows), parts(cols)
    if kind == "z":
        return [a[3] == b[3]]
    same = a[0] == b[0]
    return [same & (a[1] == b[1]), same & (a[2] == b[2])]


def softmax_in(scores, mask):
    held = jnp.where(mask, scores, -1e30)
    weights = jnp.exp(held - jnp.max(held, axis=-1, keepdims=True))
    return weights / jnp.sum(weights, axis=-1, keepdims=True)


def pair_parts(proj, pair, width):
    at = pair * LANES
    return [proj[:, which * width + at : which * width + at + LANES] for which in range(3)]


def halves():
    lane = lax.broadcasted_iota(jnp.int32, (1, LANES), 1)
    low = (lane < LANES // 2).astype(F32)
    return low.astype(BF16), (1.0 - low).astype(BF16)


def stack(block, low, high):
    return jnp.concatenate([block * low, block * high], axis=0)


def side(block):
    count = block.shape[0] // 2
    return jnp.concatenate([block[:count], block[count:]], axis=1)


def attend(proj, masks, width):
    low, high = halves()
    scale = (width // HEADS) ** (-0.5)
    outs = []
    for pair in range(HEADS // 2):
        q2, k2, v2 = pair_parts(proj, pair, width)
        scores = dot_nt(stack(q2, low, high), k2) * scale
        probs = sum(softmax_in(scores, mask).astype(BF16).astype(F32) for mask in masks)
        outs.append(dot(side(probs.astype(BF16)), stack(v2, low, high)))
    return jnp.concatenate(outs, axis=1)


def attend_back(proj, grad, masks, width, out_ref, at):
    low, high = halves()
    scale = (width // HEADS) ** (-0.5)
    for pair in range(HEADS // 2):
        q2, k2, v2 = pair_parts(proj, pair, width)
        g2 = grad[:, pair * LANES : (pair + 1) * LANES]
        qs, gs = stack(q2, low, high), stack(g2, low, high)
        scores = dot_nt(qs, k2) * scale
        grad_probs = dot_nt(gs, v2)
        probs = jnp.zeros_like(scores)
        grad_scores = jnp.zeros_like(scores)
        for mask in masks:
            one = softmax_in(scores, mask)
            probs += one.astype(BF16).astype(F32)
            grad_scores += one * (grad_probs - jnp.sum(one * grad_probs, axis=-1, keepdims=True))
        probs, grad_scores = probs.astype(BF16), grad_scores.astype(BF16)
        found = (
            dot(side(grad_scores), stack(k2, low, high)) * scale,
            dot_tn(grad_scores, qs) * scale,
            dot_tn(probs, gs),
        )
        for which in range(3):
            start = at + which * width + pair * LANES
            out_ref[0 : q2.shape[0], start : start + LANES] = found[which].astype(BF16)


def chunk_order(sizes, parts):
    depth, per, _, count = sizes
    rows = lax.broadcasted_iota(jnp.int32, (count, count), 0)
    cols = lax.broadcasted_iota(jnp.int32, (count, count), 1)
    chunk = rows // (depth * per)
    if parts > 1:
        chunk = chunk ^ lax.axis_index("slab")
    plane = (rows // per) & (depth - 1)
    return plane * (count // depth) + chunk * per + (rows & (per - 1)) == cols


def put_parts(refs, at, value):
    rows = refs[0].shape[0]
    for j, ref in enumerate(refs):
        ref[:, at : at + value.shape[1]] = value[j * rows : (j + 1) * rows]


def joined(refs, start, stop):
    return jnp.concatenate([ref[:, start:stop] for ref in refs], axis=0)


def plane_kernel(sizes, x_ref, cot_ref, gain_ref, w_ref, *refs):
    parts, hold_x = refs[:-7], refs[-7]
    x_in, cot_in, gain_in, w_in, proj, sems = refs[-6:]
    copies = [
        pltpu.make_async_copy(src, dst, sems.at[i])
        for i, (src, dst) in enumerate(
            ((x_ref, x_in), (gain_ref, gain_in), (w_ref, w_in), (cot_ref, cot_in))
        )
    ]
    for copy in copies:
        copy.start()
    width = w_in.shape[0]
    order = chunk_order(sizes, len(parts)).astype(F32).astype(BF16)
    masks = line_masks(sizes, "xy")
    copies[0].wait()
    x = dot(order, x_in[...])
    hold_x[...] = x.astype(BF16)
    put_parts(parts, 0, hold_x[...])
    copies[1].wait()
    normed, _ = norm_stats(x)
    hidden = (normed * gain_in[...]).astype(BF16)
    copies[2].wait()
    proj[...] = dot(hidden, w_in[...]).astype(BF16)
    put_parts(parts, 2 * width, attend(proj[...], masks, width).astype(BF16))
    copies[3].wait()
    put_parts(parts, width, dot(order, cot_in[...]).astype(BF16))


def prepare_kernel(slabs, w_up_ref, w_down_ref, up_ref, down_ref):
    quarter = lax.axis_index("case")
    units = w_up_ref.shape[1]
    fine = units // slabs // 4
    pack = LANES // fine
    rows = lax.broadcasted_iota(jnp.int32, (4 * LANES, LANES), 0)
    cols = lax.broadcasted_iota(jnp.int32, (4 * LANES, LANES), 1)
    wanted = (cols // fine) * (4 * fine) + quarter * fine + (cols & (fine - 1))
    pick = (rows == wanted).astype(F32).astype(BF16)
    for group in range(slabs // pack):
        up_ref[:, group * LANES : (group + 1) * LANES] = dot(
            w_up_ref[:, group * 4 * LANES : (group + 1) * 4 * LANES], pick
        ).astype(BF16)
    for block in range(slabs):
        start = pl.multiple_of((block * 4 + quarter) * fine, 8)
        down_ref[block * fine : (block + 1) * fine, :] = w_down_ref[pl.ds(start, fine), :]


def lines_kernel(sizes, parts, *refs):
    got = refs[:parts]
    gain_one_ref, gain_two_ref, w_ref, w_out_ref = refs[parts : parts + 4]
    shared_ref, proj_ref, mixed_ref, residual_ref, hold_x = refs[parts + 4 :]
    width = w_ref.shape[0]
    hold_x[...] = joined(got, 0, width)
    x = hold_x[...].astype(F32)
    normed, _ = norm_stats(x)
    proj_ref[...] = dot((normed * gain_one_ref[...]).astype(BF16), w_ref[...]).astype(BF16)
    out_z = attend(proj_ref[...], line_masks(sizes, "z"), width).astype(BF16)
    mixed = (joined(got, 2 * width, 3 * width).astype(F32) + out_z.astype(F32)).astype(BF16)
    residual = (x + dot(mixed, w_out_ref[...])).astype(BF16)
    normed_two, _ = norm_stats(residual.astype(F32))
    shared_ref[:, :width] = (normed_two * gain_two_ref[...]).astype(BF16)
    shared_ref[:, width:] = joined(got, width, 2 * width)
    mixed_ref[...] = mixed
    residual_ref[...] = residual


def gelu_parts(upper):
    square = upper * upper
    tangent = jnp.tanh(ROOT_TWO_PI * (upper + 0.044715 * upper * square))
    half = 0.5 * (1.0 + tangent)
    slope = half + 0.5 * upper * (1.0 - tangent * tangent) * ROOT_TWO_PI * (
        1.0 + 3.0 * 0.044715 * square
    )
    return (upper * half).astype(BF16), slope


def mlp_kernel(
    shared_ref, residual_ref, gain_ref, w_out_ref, w_up_ref, w_down_ref, grad_ref, gres_ref
):
    width, units = w_up_ref.shape
    hidden, cot = shared_ref[:, :width], shared_ref[:, width:]
    normed, inverse = norm_stats(residual_ref[...].astype(F32))
    step = min(512, units)
    grad_hidden = jnp.zeros(normed.shape, F32)
    for at in range(0, units, step):
        _, slope = gelu_parts(dot(hidden, w_up_ref[:, at : at + step]))
        grad_upper = (dot_nt(cot, w_down_ref[at : at + step, :]) * slope).astype(BF16)
        grad_hidden += dot_nt(grad_upper, w_up_ref[:, at : at + step])
    grad_residual = cot.astype(F32) + norm_back(grad_hidden * gain_ref[...], normed, inverse)
    gres_ref[...] = grad_residual
    grad_ref[...] = dot_nt(grad_residual.astype(BF16), w_out_ref[...]).astype(BF16)


def lines_back_kernel(
    sizes, parts, proj_ref, grad_ref, gres_ref, mixed_ref, x_ref, gain_ref, w_ref, back_ref, pack_ref
):
    width = w_ref.shape[0]
    pack_ref[:, 4 * width : 5 * width] = mixed_ref[...]
    pack_ref[:, 5 * width :] = gres_ref[...].astype(BF16)
    attend_back(proj_ref[...], grad_ref[...], line_masks(sizes, "z"), width, pack_ref, width)
    normed, inverse = norm_stats(x_ref[...].astype(F32))
    pack_ref[:, :width] = (normed * gain_ref[...]).astype(BF16)
    grad_hidden = dot_nt(pack_ref[:, width : 4 * width], w_ref[...])
    back = norm_back(grad_hidden * gain_ref[...], normed, inverse)
    part = (gres_ref[...] + back).astype(BF16)
    for j, (spot, size) in enumerate(blocks_of(part.shape[0], parts)):
        back_ref[pl.ds(spot, size), :width] = grad_ref[j * size : (j + 1) * size, :]
        back_ref[pl.ds(spot, size), width:] = part[j * size : (j + 1) * size]


def blocks_of(count, parts):
    size = count // parts
    if parts == 1:
        return [(0, size)]
    me = lax.axis_index("slab")
    return [(pl.multiple_of((me ^ j) * size, 16), size) for j in range(parts)]


def partner_order(ref, parts, start, stop):
    return jnp.concatenate(
        [ref[pl.ds(spot, size), start:stop] for spot, size in blocks_of(ref.shape[0], parts)], axis=0
    )


def join_kernel(a_ref, b_ref, back_ref, out_ref, passed_ref):
    rows = a_ref.shape[0]
    out_ref[:rows, :] = a_ref[...]
    out_ref[rows:, :] = b_ref[...]
    passed_ref[...] = back_ref[...]


def plane_grads_kernel(sizes, parts, *refs):
    back_ref, x_ref, gain_ref, w_ref, pack_ref, proj = refs
    width = w_ref.shape[0]
    normed, _ = norm_stats(x_ref[...].astype(F32))
    pack_ref[:, :width] = (normed * gain_ref[...]).astype(BF16)
    proj[...] = dot(pack_ref[:, :width], w_ref[...]).astype(BF16)
    grad = partner_order(back_ref, parts, 0, width)
    attend_back(proj[...], grad, line_masks(sizes, "xy"), width, pack_ref, width)


def plane_tokens_kernel(sizes, parts, *refs):
    back_ref, pack_ref, x_ref, gain_ref, w_ref, grad_ref = refs
    width = w_ref.shape[0]
    normed, inverse = norm_stats(x_ref[...].astype(F32))
    grad_hidden = dot_nt(pack_ref[:, width:], w_ref[...])
    back = norm_back(grad_hidden * gain_ref[...], normed, inverse)
    part = partner_order(back_ref, parts, width, 2 * width).astype(F32)
    order = chunk_order(sizes, parts).astype(F32).astype(BF16)
    grad_ref[...] = dot_tn(order, (back + part).astype(BF16)).astype(BF16)


def place():
    slab, case = lax.axis_index("slab"), lax.axis_index("case")
    return slab & 1, case >> 1, case & 1, slab >> 1


def store_units(scratch, rows, units, x, flip, outs, at):
    blocks = outs[0].shape[0]
    for z in range(blocks):
        start = pl.multiple_of((z * 2 + (x ^ flip)) * rows, 8)
        block = scratch[pl.ds(start, rows), 0 : units * LANES].astype(BF16)
        for unit in range(units):
            outs[flip][z, at + unit * rows : at + (unit + 1) * rows, :] = block[
                :, unit * LANES : (unit + 1) * LANES
            ]


def grads_mlp_kernel(factor, here_ref, there_ref, w_up_ref, w_down_ref, keep_ref, send_ref, down, up):
    width, units = w_up_ref.shape
    x, _, _, _ = place()
    hidden = jnp.concatenate([ref[:, :width] for ref in (here_ref, there_ref)], axis=0)
    cot = jnp.concatenate([ref[:, width:] for ref in (here_ref, there_ref)], axis=0)
    active, slope = gelu_parts(dot(hidden, w_up_ref[...]))
    grad_upper = (dot_nt(cot, w_down_ref[...]) * slope).astype(BF16)
    down[...] = dot_tn(active, cot) * factor
    up[...] = dot_tn(hidden, grad_upper) * factor
    spans, rows = keep_ref.shape[:2]
    for flip, out in ((0, keep_ref), (1, send_ref)):
        for z in range(spans):
            at = pl.ds(pl.multiple_of((z * 2 + (x ^ flip)) * rows, 8), rows)
            out[z, :, :width] = down[at, :].astype(BF16)
            out[z, :, width:] = up[at, :].astype(BF16)


def grads_qkv_kernel(factor, width, slabs, za_ref, zb_ref, pa_ref, pb_ref, *refs):
    outs, scratch = refs[:4], refs[4]
    x, y, core, _ = place()
    size, narrow = 3 * width // 4, width // 4
    rows = width // slabs
    hidden = jnp.concatenate([r[:, :width] for r in (za_ref, zb_ref, pa_ref, pb_ref)], axis=0)
    mixed = jnp.concatenate([r[:, 4 * width : 5 * width] for r in (za_ref, zb_ref)], axis=0)
    for flip_y in range(2):
        quarter = (y ^ flip_y) * 2 + core
        at = pl.multiple_of(width + quarter * size, LANES)
        cols = jnp.concatenate(
            [r[:, pl.ds(at, size)] for r in (za_ref, zb_ref, pa_ref, pb_ref)], axis=0
        )
        scratch[:, :size] = dot_tn(hidden, cols) * factor
        at = pl.multiple_of(5 * width + quarter * narrow, LANES)
        cols = jnp.concatenate([r[:, pl.ds(at, narrow)] for r in (za_ref, zb_ref)], axis=0)
        scratch[:, size:] = dot_tn(mixed, cols) * factor
        for flip in range(2):
            store_units(scratch, rows, width // LANES, x, flip, outs[2 * flip_y : 2 * flip_y + 2], 0)


def fold_kernel(shift, radix, count, *refs):
    ins, outs = refs[:count], refs[count:]
    digit = (lax.axis_index("slab") >> shift) & (radix - 1)
    rest = ins[0].shape[0] // radix
    for j in range(radix):
        for k in range(rest):
            at = (digit ^ j) * rest + k
            total = ins[0][at].astype(F32)
            for ref in ins[1:]:
                total += ref[at].astype(F32)
            outs[j][k] = total.astype(BF16)


def fold(shift, radix, pieces, after=()):
    first = pieces[0].shape
    outs = [shape_of((first[0] // radix,) + first[1:], BF16)] * radix
    kernel = functools.partial(fold_kernel, shift, radix, len(pieces))
    return call(kernel, outs, *pieces, after=after)


def swap_pairs(slabs, cases, flip_slab, flip_case):
    return [
        (s * cases + c, (s ^ flip_slab) * cases + (c ^ flip_case))
        for s in range(slabs)
        for c in range(cases)
    ]


def gain_sums(grad, w_rows, gain_ref):
    rows, width = grad.shape[0], gain_ref.shape[1]
    spot = lax.axis_index("slab") * rows + lax.broadcasted_iota(jnp.int32, (rows, width), 0)
    lanes = lax.broadcasted_iota(jnp.int32, (rows, width), 1)
    gain = jnp.sum(jnp.where(lanes == spot, gain_ref[...], 0.0), axis=1, keepdims=True)
    total = jnp.sum(grad * w_rows.astype(F32), axis=1, keepdims=True) / gain
    return jnp.transpose(jnp.broadcast_to(total, (rows, LANES)))[0:1, :]


def place_mlp_kernel(slabs, width, units, *refs):
    pieces, (gain_ref, w_up_ref, w_ref) = refs[:4], refs[4:7]
    up, down, two, w_rows, held, up_rows, sems = refs[7:]
    rows = width // slabs
    here = pl.ds(pl.multiple_of(lax.axis_index("slab") * rows, 8), rows)
    copies = [
        pltpu.make_async_copy(w_up_ref.at[here], up_rows, sems.at[0]),
        pltpu.make_async_copy(w_ref.at[here], w_rows, sems.at[1]),
    ]
    for copy in copies:
        copy.start()
    case = lax.axis_index("case")
    for j in range(4):
        held[case ^ j] = pieces[j][0].astype(F32)
    fine = units // 4 // slabs
    for quarter in range(4):
        down[quarter * rows : (quarter + 1) * rows, :] = held[quarter, :, :width]
    for block in range(slabs):
        up[:, block * 4 * fine : (block + 1) * 4 * fine] = jnp.concatenate(
            [held[quarter, :, width + block * fine : width + (block + 1) * fine] for quarter in range(4)],
            axis=1,
        )
    for copy in copies:
        copy.wait()
    two[...] = gain_sums(up[...], up_rows[...], gain_ref)


def place_qkv_kernel(slabs, width, *refs):
    pieces, (gain_ref, w_rows), (qkv, out, one) = refs[:4], refs[4:6], refs[6:]
    case = lax.axis_index("case")
    rows = width // slabs
    size = 3 * width // 4
    for j in range(4):
        quarter = case ^ j
        for unit in range(width // LANES):
            piece = pieces[j][0, unit * rows : (unit + 1) * rows, :].astype(F32)
            if unit < size // LANES:
                start = pl.multiple_of(quarter * size + unit * LANES, LANES)
                qkv[:, pl.ds(start, LANES)] = piece
            else:
                start = pl.multiple_of(quarter * (width // 4) + unit * LANES - size, LANES)
                out[:, pl.ds(start, LANES)] = piece
    one[...] = gain_sums(qkv[...], w_rows[...], gain_ref)


def body(tokens, cotangent, w_qkv, w_out, w_up, w_down, gain_attn, gain_mlp):
    slabs, cases = lax.axis_size("slab"), lax.axis_size("case")
    depth, height, across, width = tokens.shape[1:]
    units = w_up.shape[1]
    lines = height * across
    per = lines // slabs
    count = depth * lines
    sizes = (depth, per, across, count)
    factor = 1.0 / math.sqrt(count * slabs * cases)
    gain_one, gain_two = gain_attn.reshape(1, width), gain_mlp.reshape(1, width)
    spans = slabs // 2
    rows = width // slabs
    parts = slabs if depth * per % 16 == 0 else 1

    def permute(array, flip_slab, flip_case):
        return lax.ppermute(array, BOTH, swap_pairs(slabs, cases, flip_slab, flip_case))

    def exchange(blocks):
        if parts == 1:
            return [lax.all_to_all(blocks[0], "slab", split_axis=0, concat_axis=0, tiled=True)]
        got = {j: permute(blocks[j], j, 0) for j in range(parts - 1, 0, -1)}
        return [blocks[0]] + [got[j] for j in range(1, parts)]

    proj_bf = shape_of((count, 3 * width), BF16)
    rows_bf = shape_of((count, width), BF16)
    *mine, hold_x = call(
        functools.partial(plane_kernel, sizes),
        [shape_of((count // parts, 3 * width), BF16)] * parts + [rows_bf],
        tokens.reshape(count, width),
        cotangent.reshape(count, width),
        gain_one,
        w_qkv,
        near=[False] * 4,
        scratch=[
            pltpu.VMEM((count, width), BF16),
            pltpu.VMEM((count, width), BF16),
            pltpu.VMEM((1, width), F32),
            pltpu.VMEM((width, 3 * width), BF16),
            pltpu.VMEM((count, 3 * width), BF16),
            pltpu.SemaphoreType.DMA((4,)),
        ],
    )
    w_up_mine, w_down_mine = call(
        functools.partial(prepare_kernel, slabs),
        [shape_of((width, units // 4), BF16), shape_of((units // 4, width), BF16)],
        w_up,
        w_down,
    )
    got = exchange(mine)
    shared, proj_z, mixed, residual, hold_z = call(
        functools.partial(lines_kernel, sizes, parts),
        [shape_of((count, 2 * width), BF16), proj_bf, rows_bf, rows_bf, rows_bf],
        *got,
        gain_one,
        gain_two,
        w_qkv,
        w_out,
        after=[w_up_mine],
    )
    shared_y = permute(shared, 0, 2)
    grad_mixed, grad_residual = call(
        mlp_kernel,
        [rows_bf, shape_of((count, width), F32)],
        shared,
        residual,
        gain_two,
        w_out,
        w_up,
        w_down,
    )
    back, pack_z = call(
        functools.partial(lines_back_kernel, sizes, parts),
        [shape_of((count, 2 * width), BF16), shape_of((count, 6 * width), BF16)],
        proj_z,
        grad_mixed,
        grad_residual,
        mixed,
        hold_z,
        gain_one,
        w_qkv,
    )
    around, back = call(
        join_kernel,
        [shape_of((2 * count, 2 * width), BF16), shape_of((count, 2 * width), BF16)],
        shared,
        shared_y,
        back,
    )
    back = lax.all_to_all(back, "slab", split_axis=0, concat_axis=0, tiled=True)
    pack_z_core = permute(pack_z, 0, 1)
    big_keep, big_send = call(
        functools.partial(grads_mlp_kernel, factor),
        [shape_of((spans, rows, 2 * width), BF16)] * 2,
        around,
        permute(around, 0, 1),
        w_up_mine,
        w_down_mine,
        scratch=[pltpu.VMEM((units // 4, width), F32), pltpu.VMEM((width, units // 4), F32)],
    )
    (pack_p,) = call(
        functools.partial(plane_grads_kernel, sizes, parts),
        [shape_of((count, 4 * width), BF16)],
        back,
        hold_x,
        gain_one,
        w_qkv,
        scratch=[pltpu.VMEM((count, 3 * width), BF16)],
    )
    small = call(
        functools.partial(grads_qkv_kernel, factor, width, slabs),
        [shape_of((spans, rows * (width // LANES), LANES), BF16)] * 4,
        pack_z,
        pack_z_core,
        pack_p,
        permute(pack_p, 0, 1),
        after=[big_keep],
        scratch=[pltpu.VMEM((width, width), F32)],
    )
    ready = small[0]
    small = [small[0], permute(small[1], 1, 0), permute(small[2], 0, 2), permute(small[3], 1, 2)]
    (grad_tokens,) = call(
        functools.partial(plane_tokens_kernel, sizes, parts),
        [rows_bf],
        back,
        pack_p,
        hold_x,
        gain_one,
        w_qkv,
        after=[ready],
    )

    def reduce_z(pieces, after=()):
        left = spans
        while left > 1:
            radix = min(4, left)
            left //= radix
            shift = (left * 2).bit_length() - 1
            split = fold(shift, radix, pieces, after)
            pieces = [split[0]] + [permute(split[j], j << shift, 0) for j in range(1, radix)]
        return pieces

    def gather(pieces, after=()):
        (last,) = fold(0, 1, pieces, after)
        return [last] + [permute(last, 0, j) for j in range(1, 4)]

    big = reduce_z([big_keep, permute(big_send, 1, 0)], [ready])
    small = reduce_z(small)
    big = gather(big, [small[0]])
    full_up, full_down, full_two, w_rows = call(
        functools.partial(place_mlp_kernel, slabs, width, units),
        [
            shape_of((rows, units), F32),
            shape_of((units // slabs, width), F32),
            shape_of((1, rows), F32),
            shape_of((rows, 3 * width), BF16),
        ],
        *big,
        gain_two,
        w_up,
        w_qkv,
        near=[True] * 5 + [False] * 2,
        scratch=[
            pltpu.VMEM((4, rows, 2 * width), F32),
            pltpu.VMEM((rows, units), BF16),
            pltpu.SemaphoreType.DMA((2,)),
        ],
    )
    small = gather(small)
    full_qkv, full_out, full_one = call(
        functools.partial(place_qkv_kernel, slabs, width),
        [shape_of((rows, 3 * width), F32), shape_of((rows, width), F32), shape_of((1, rows), F32)],
        *small,
        gain_one,
        w_rows,
    )
    return (
        grad_tokens.reshape(tokens.shape),
        full_qkv,
        full_out,
        full_up,
        full_down,
        full_one.reshape(rows),
        full_two.reshape(rows),
    )


def solution(mesh):
    grid = P("case", "slab", None, None, None)
    return jax.shard_map(
        body,
        mesh=mesh,
        in_specs=(grid, grid, P(), P(), P(), P(), P(), P()),
        out_specs=(
            grid,
            P("slab", None),
            P("slab", None),
            P("slab", None),
            P("slab", None),
            P("slab"),
            P("slab"),
        ),
        check_vma=False,
    )
```

```python
import functools
import math

import jax
import jax.numpy as jnp
from jax import lax
from jax.experimental import pallas as pl
from jax.experimental.pallas import tpu as pltpu
from jax.sharding import PartitionSpec as P

HEADS = 8
LANES = 128
EPSILON = 1e-06
ROOT_TWO_PI = math.sqrt(2.0 / math.pi)
F32 = jnp.float32
BF16 = jnp.bfloat16
BOTH = ("slab", "case")
VMEM_BYTES = 16 * 1024 * 1024


def dot(a, b):
    return lax.dot_general(a, b, (((1,), (0,)), ((), ())), preferred_element_type=F32)


def dot_nt(a, b):
    return lax.dot_general(a, b, (((1,), (1,)), ((), ())), preferred_element_type=F32)


def dot_tn(a, b):
    return lax.dot_general(a, b, (((0,), (0,)), ((), ())), preferred_element_type=F32)


def norm_stats(values):
    inverse = lax.rsqrt(jnp.mean(values * values, axis=-1, keepdims=True) + EPSILON)
    return values * inverse, inverse


def norm_back(scaled, normed, inverse):
    return inverse * (scaled - normed * jnp.mean(scaled * normed, axis=-1, keepdims=True))


def call(kernel, outs, *args, after=(), scratch=(), near=None, flops=10**7):
    count = len(args)
    near = [True] * count if near is None else near

    def run(*refs):
        kernel(*refs[:count], *refs[count + len(after) :])

    vmem, far = pl.BlockSpec(memory_space=pltpu.VMEM), pl.BlockSpec(memory_space=pltpu.HBM)
    return pl.pallas_call(
        run,
        out_shape=outs,
        in_specs=[vmem if one else far for one in near] + [pl.BlockSpec(memory_space=pl.ANY)] * len(after),
        out_specs=[vmem] * len(outs),
        scratch_shapes=list(scratch),
        cost_estimate=pl.CostEstimate(flops=flops, transcendentals=0, bytes_accessed=10**4),
        compiler_params=pltpu.CompilerParams(vmem_limit_bytes=VMEM_BYTES),
    )(
        *[
            arg if one else pltpu.with_memory_space_constraint(arg, pltpu.HBM)
            for arg, one in zip(args, near)
        ],
        *after,
    )


def shape_of(shape, dtype):
    return jax.ShapeDtypeStruct(shape, dtype)


def line_masks(sizes, kind):
    depth, per, across, count = sizes
    rows = lax.broadcasted_iota(jnp.int32, (2 * count, count), 0) & (count - 1)
    cols = lax.broadcasted_iota(jnp.int32, (2 * count, count), 1)

    def parts(t):
        chunk = t // (depth * per)
        plane = (t // per) & (depth - 1)
        spot = chunk * per + (t & (per - 1))
        return plane, spot // across, spot & (across - 1), t & (per - 1)

    a, b = parts(rows), parts(cols)
    if kind == "z":
        return [a[3] == b[3]]
    same = a[0] == b[0]
    return [same & (a[1] == b[1]), same & (a[2] == b[2])]


def softmax_in(scores, mask):
    held = jnp.where(mask, scores, -1e30)
    weights = jnp.exp(held - jnp.max(held, axis=-1, keepdims=True))
    return weights / jnp.sum(weights, axis=-1, keepdims=True)


def pair_parts(proj, pair, width):
    at = pair * LANES
    return [proj[:, which * width + at : which * width + at + LANES] for which in range(3)]


def halves():
    lane = lax.broadcasted_iota(jnp.int32, (1, LANES), 1)
    low = (lane < LANES // 2).astype(F32)
    return low.astype(BF16), (1.0 - low).astype(BF16)


def stack(block, low, high):
    return jnp.concatenate([block * low, block * high], axis=0)


def side(block):
    count = block.shape[0] // 2
    return jnp.concatenate([block[:count], block[count:]], axis=1)


def attend(proj, masks, width):
    low, high = halves()
    scale = (width // HEADS) ** (-0.5)
    outs = []
    for pair in range(HEADS // 2):
        q2, k2, v2 = pair_parts(proj, pair, width)
        scores = dot_nt(stack(q2, low, high), k2) * scale
        probs = sum(softmax_in(scores, mask).astype(BF16).astype(F32) for mask in masks)
        outs.append(dot(side(probs.astype(BF16)), stack(v2, low, high)))
    return jnp.concatenate(outs, axis=1)


def attend_back(proj, grad, masks, width, out_ref, at):
    low, high = halves()
    scale = (width // HEADS) ** (-0.5)
    for pair in range(HEADS // 2):
        q2, k2, v2 = pair_parts(proj, pair, width)
        g2 = grad[:, pair * LANES : (pair + 1) * LANES]
        qs, gs = stack(q2, low, high), stack(g2, low, high)
        scores = dot_nt(qs, k2) * scale
        grad_probs = dot_nt(gs, v2)
        probs = jnp.zeros_like(scores)
        grad_scores = jnp.zeros_like(scores)
        for mask in masks:
            one = softmax_in(scores, mask)
            probs += one.astype(BF16).astype(F32)
            grad_scores += one * (grad_probs - jnp.sum(one * grad_probs, axis=-1, keepdims=True))
        probs, grad_scores = probs.astype(BF16), grad_scores.astype(BF16)
        found = (
            dot(side(grad_scores), stack(k2, low, high)) * scale,
            dot_tn(grad_scores, qs) * scale,
            dot_tn(probs, gs),
        )
        for which in range(3):
            start = at + which * width + pair * LANES
            out_ref[0 : q2.shape[0], start : start + LANES] = found[which].astype(BF16)


def chunk_order(sizes, parts):
    depth, per, _, count = sizes
    rows = lax.broadcasted_iota(jnp.int32, (count, count), 0)
    cols = lax.broadcasted_iota(jnp.int32, (count, count), 1)
    chunk = rows // (depth * per)
    if parts > 1:
        chunk = chunk ^ lax.axis_index("slab")
    plane = (rows // per) & (depth - 1)
    return plane * (count // depth) + chunk * per + (rows & (per - 1)) == cols


def put_parts(refs, at, value):
    rows = refs[0].shape[0]
    for j, ref in enumerate(refs):
        ref[:, at : at + value.shape[1]] = value[j * rows : (j + 1) * rows]


def joined(refs, start, stop):
    return jnp.concatenate([ref[:, start:stop] for ref in refs], axis=0)


def plane_kernel(sizes, x_ref, cot_ref, gain_ref, w_ref, *refs):
    parts, hold_x = refs[:-7], refs[-7]
    x_in, cot_in, gain_in, w_in, proj, sems = refs[-6:]
    copies = [
        pltpu.make_async_copy(src, dst, sems.at[i])
        for i, (src, dst) in enumerate(
            ((x_ref, x_in), (gain_ref, gain_in), (w_ref, w_in), (cot_ref, cot_in))
        )
    ]
    for copy in copies:
        copy.start()
    width = w_in.shape[0]
    order = chunk_order(sizes, len(parts)).astype(F32).astype(BF16)
    masks = line_masks(sizes, "xy")
    copies[0].wait()
    x = dot(order, x_in[...])
    hold_x[...] = x.astype(BF16)
    put_parts(parts, 0, hold_x[...])
    copies[1].wait()
    normed, _ = norm_stats(x)
    hidden = (normed * gain_in[...]).astype(BF16)
    copies[2].wait()
    proj[...] = dot(hidden, w_in[...]).astype(BF16)
    put_parts(parts, 2 * width, attend(proj[...], masks, width).astype(BF16))
    copies[3].wait()
    put_parts(parts, width, dot(order, cot_in[...]).astype(BF16))


def prepare_kernel(slabs, w_up_ref, w_down_ref, up_ref, down_ref):
    quarter = lax.axis_index("case")
    units = w_up_ref.shape[1]
    fine = units // slabs // 4
    pack = LANES // fine
    rows = lax.broadcasted_iota(jnp.int32, (4 * LANES, LANES), 0)
    cols = lax.broadcasted_iota(jnp.int32, (4 * LANES, LANES), 1)
    wanted = (cols // fine) * (4 * fine) + quarter * fine + (cols & (fine - 1))
    pick = (rows == wanted).astype(F32).astype(BF16)
    for group in range(slabs // pack):
        up_ref[:, group * LANES : (group + 1) * LANES] = dot(
            w_up_ref[:, group * 4 * LANES : (group + 1) * 4 * LANES], pick
        ).astype(BF16)
    for block in range(slabs):
        start = pl.multiple_of((block * 4 + quarter) * fine, 8)
        down_ref[block * fine : (block + 1) * fine, :] = w_down_ref[pl.ds(start, fine), :]


def lines_kernel(sizes, parts, *refs):
    got = refs[:parts]
    gain_one_ref, gain_two_ref, w_ref, w_out_ref = refs[parts : parts + 4]
    shared_ref, proj_ref, mixed_ref, residual_ref, hold_x = refs[parts + 4 :]
    width = w_ref.shape[0]
    hold_x[...] = joined(got, 0, width)
    x = hold_x[...].astype(F32)
    normed, _ = norm_stats(x)
    proj_ref[...] = dot((normed * gain_one_ref[...]).astype(BF16), w_ref[...]).astype(BF16)
    out_z = attend(proj_ref[...], line_masks(sizes, "z"), width).astype(BF16)
    mixed = (joined(got, 2 * width, 3 * width).astype(F32) + out_z.astype(F32)).astype(BF16)
    residual = (x + dot(mixed, w_out_ref[...])).astype(BF16)
    normed_two, _ = norm_stats(residual.astype(F32))
    shared_ref[:, :width] = (normed_two * gain_two_ref[...]).astype(BF16)
    shared_ref[:, width:] = joined(got, width, 2 * width)
    mixed_ref[...] = mixed
    residual_ref[...] = residual


def gelu_parts(upper):
    square = upper * upper
    tangent = jnp.tanh(ROOT_TWO_PI * (upper + 0.044715 * upper * square))
    half = 0.5 * (1.0 + tangent)
    slope = half + 0.5 * upper * (1.0 - tangent * tangent) * ROOT_TWO_PI * (
        1.0 + 3.0 * 0.044715 * square
    )
    return (upper * half).astype(BF16), slope


def mlp_kernel(
    shared_ref, residual_ref, gain_ref, w_out_ref, w_up_ref, w_down_ref, grad_ref, gres_ref
):
    width, units = w_up_ref.shape
    hidden, cot = shared_ref[:, :width], shared_ref[:, width:]
    normed, inverse = norm_stats(residual_ref[...].astype(F32))
    step = min(512, units)
    grad_hidden = jnp.zeros(normed.shape, F32)
    for at in range(0, units, step):
        _, slope = gelu_parts(dot(hidden, w_up_ref[:, at : at + step]))
        grad_upper = (dot_nt(cot, w_down_ref[at : at + step, :]) * slope).astype(BF16)
        grad_hidden += dot_nt(grad_upper, w_up_ref[:, at : at + step])
    grad_residual = cot.astype(F32) + norm_back(grad_hidden * gain_ref[...], normed, inverse)
    gres_ref[...] = grad_residual
    grad_ref[...] = dot_nt(grad_residual.astype(BF16), w_out_ref[...]).astype(BF16)


def lines_back_kernel(
    sizes, parts, proj_ref, grad_ref, gres_ref, mixed_ref, x_ref, gain_ref, w_ref, back_ref, pack_ref
):
    width = w_ref.shape[0]
    pack_ref[:, 4 * width : 5 * width] = mixed_ref[...]
    pack_ref[:, 5 * width :] = gres_ref[...].astype(BF16)
    attend_back(proj_ref[...], grad_ref[...], line_masks(sizes, "z"), width, pack_ref, width)
    normed, inverse = norm_stats(x_ref[...].astype(F32))
    pack_ref[:, :width] = (normed * gain_ref[...]).astype(BF16)
    grad_hidden = dot_nt(pack_ref[:, width : 4 * width], w_ref[...])
    back = norm_back(grad_hidden * gain_ref[...], normed, inverse)
    part = (gres_ref[...] + back).astype(BF16)
    for j, (spot, size) in enumerate(blocks_of(part.shape[0], parts)):
        back_ref[pl.ds(spot, size), :width] = grad_ref[j * size : (j + 1) * size, :]
        back_ref[pl.ds(spot, size), width:] = part[j * size : (j + 1) * size]


def blocks_of(count, parts):
    size = count // parts
    if parts == 1:
        return [(0, size)]
    me = lax.axis_index("slab")
    return [(pl.multiple_of((me ^ j) * size, 16), size) for j in range(parts)]


def partner_order(ref, parts, start, stop):
    return jnp.concatenate(
        [ref[pl.ds(spot, size), start:stop] for spot, size in blocks_of(ref.shape[0], parts)], axis=0
    )


def join_kernel(a_ref, b_ref, out_ref):
    rows = a_ref.shape[0]
    out_ref[:rows, :] = a_ref[...]
    out_ref[rows:, :] = b_ref[...]


def plane_grads_kernel(sizes, parts, *refs):
    back_ref, x_ref, gain_ref, w_ref, pack_ref, proj = refs
    width = w_ref.shape[0]
    normed, _ = norm_stats(x_ref[...].astype(F32))
    pack_ref[:, :width] = (normed * gain_ref[...]).astype(BF16)
    proj[...] = dot(pack_ref[:, :width], w_ref[...]).astype(BF16)
    grad = partner_order(back_ref, parts, 0, width)
    attend_back(proj[...], grad, line_masks(sizes, "xy"), width, pack_ref, width)


def plane_tokens_kernel(sizes, parts, *refs):
    back_ref, pack_ref, x_ref, gain_ref, w_ref, grad_ref, flag_ref = refs
    flag_ref[...] = jnp.zeros_like(flag_ref)
    width = w_ref.shape[0]
    normed, inverse = norm_stats(x_ref[...].astype(F32))
    grad_hidden = dot_nt(pack_ref[:, width:], w_ref[...])
    back = norm_back(grad_hidden * gain_ref[...], normed, inverse)
    part = partner_order(back_ref, parts, width, 2 * width).astype(F32)
    order = chunk_order(sizes, parts).astype(F32).astype(BF16)
    grad_ref[...] = dot_tn(order, (back + part).astype(BF16)).astype(BF16)


def place():
    slab, case = lax.axis_index("slab"), lax.axis_index("case")
    return slab & 1, case >> 1, case & 1, slab >> 1


def store_units(scratch, rows, units, x, flip, outs, at):
    blocks = outs[0].shape[0]
    for z in range(blocks):
        start = pl.multiple_of((z * 2 + (x ^ flip)) * rows, 8)
        block = scratch[pl.ds(start, rows), 0 : units * LANES].astype(BF16)
        for unit in range(units):
            outs[flip][z, at + unit * rows : at + (unit + 1) * rows, :] = block[
                :, unit * LANES : (unit + 1) * LANES
            ]


def grads_mlp_kernel(factor, here_ref, there_ref, w_up_ref, w_down_ref, keep_ref, send_ref, down, up):
    width, units = w_up_ref.shape
    x, _, _, _ = place()
    hidden = jnp.concatenate([ref[:, :width] for ref in (here_ref, there_ref)], axis=0)
    cot = jnp.concatenate([ref[:, width:] for ref in (here_ref, there_ref)], axis=0)
    active, slope = gelu_parts(dot(hidden, w_up_ref[...]))
    grad_upper = (dot_nt(cot, w_down_ref[...]) * slope).astype(BF16)
    down[...] = dot_tn(active, cot) * factor
    up[...] = dot_tn(hidden, grad_upper) * factor
    spans, rows = keep_ref.shape[:2]
    for flip, out in ((0, keep_ref), (1, send_ref)):
        for z in range(spans):
            at = pl.ds(pl.multiple_of((z * 2 + (x ^ flip)) * rows, 8), rows)
            out[z, :, :width] = down[at, :].astype(BF16)
            out[z, :, width:] = up[at, :].astype(BF16)


def grads_qkv_kernel(factor, width, slabs, za_ref, zb_ref, pa_ref, pb_ref, *refs):
    outs, scratch = refs[:4], refs[4]
    x, y, core, _ = place()
    size, narrow = 3 * width // 4, width // 4
    rows = width // slabs
    hidden = jnp.concatenate([r[:, :width] for r in (za_ref, zb_ref, pa_ref, pb_ref)], axis=0)
    mixed = jnp.concatenate([r[:, 4 * width : 5 * width] for r in (za_ref, zb_ref)], axis=0)
    for flip_y in range(2):
        quarter = (y ^ flip_y) * 2 + core
        at = pl.multiple_of(width + quarter * size, LANES)
        cols = jnp.concatenate(
            [r[:, pl.ds(at, size)] for r in (za_ref, zb_ref, pa_ref, pb_ref)], axis=0
        )
        scratch[:, :size] = dot_tn(hidden, cols) * factor
        at = pl.multiple_of(5 * width + quarter * narrow, LANES)
        cols = jnp.concatenate([r[:, pl.ds(at, narrow)] for r in (za_ref, zb_ref)], axis=0)
        scratch[:, size:] = dot_tn(mixed, cols) * factor
        for flip in range(2):
            store_units(scratch, rows, width // LANES, x, flip, outs[2 * flip_y : 2 * flip_y + 2], 0)


def fold_kernel(shift, radix, count, *refs):
    ins, outs = refs[:count], refs[count:]
    digit = (lax.axis_index("slab") >> shift) & (radix - 1)
    rest = ins[0].shape[0] // radix
    for j in range(radix):
        for k in range(rest):
            at = (digit ^ j) * rest + k
            total = ins[0][at].astype(F32)
            for ref in ins[1:]:
                total += ref[at].astype(F32)
            outs[j][k] = total.astype(BF16)


def fold(shift, radix, pieces, after=()):
    first = pieces[0].shape
    outs = [shape_of((first[0] // radix,) + first[1:], BF16)] * radix
    kernel = functools.partial(fold_kernel, shift, radix, len(pieces))
    return call(kernel, outs, *pieces, after=after)


def swap_pairs(slabs, cases, flip_slab, flip_case):
    return [
        (s * cases + c, (s ^ flip_slab) * cases + (c ^ flip_case))
        for s in range(slabs)
        for c in range(cases)
    ]


def gain_sums(grad, w_rows, gain_ref):
    rows, width = grad.shape[0], gain_ref.shape[1]
    spot = lax.axis_index("slab") * rows + lax.broadcasted_iota(jnp.int32, (rows, width), 0)
    lanes = lax.broadcasted_iota(jnp.int32, (rows, width), 1)
    gain = jnp.sum(jnp.where(lanes == spot, gain_ref[...], 0.0), axis=1, keepdims=True)
    total = jnp.sum(grad * w_rows.astype(F32), axis=1, keepdims=True) / gain
    return jnp.transpose(jnp.broadcast_to(total, (rows, LANES)))[0:1, :]


def place_mlp_kernel(slabs, width, units, *refs):
    pieces, (gain_ref, w_up_ref, w_ref) = refs[:4], refs[4:7]
    up, down, two, w_rows, held, up_rows, sems = refs[7:]
    rows = width // slabs
    here = pl.ds(pl.multiple_of(lax.axis_index("slab") * rows, 8), rows)
    copies = [
        pltpu.make_async_copy(w_up_ref.at[here], up_rows, sems.at[0]),
        pltpu.make_async_copy(w_ref.at[here], w_rows, sems.at[1]),
    ]
    for copy in copies:
        copy.start()
    case = lax.axis_index("case")
    for j in range(4):
        held[case ^ j] = pieces[j][0].astype(F32)
    fine = units // 4 // slabs
    for quarter in range(4):
        down[quarter * rows : (quarter + 1) * rows, :] = held[quarter, :, :width]
    for block in range(slabs):
        up[:, block * 4 * fine : (block + 1) * 4 * fine] = jnp.concatenate(
            [held[quarter, :, width + block * fine : width + (block + 1) * fine] for quarter in range(4)],
            axis=1,
        )
    for copy in copies:
        copy.wait()
    two[...] = gain_sums(up[...], up_rows[...], gain_ref)


def place_qkv_kernel(slabs, width, *refs):
    pieces, (gain_ref, w_rows), (qkv, out, one) = refs[:4], refs[4:6], refs[6:]
    case = lax.axis_index("case")
    rows = width // slabs
    size = 3 * width // 4
    for j in range(4):
        quarter = case ^ j
        for unit in range(width // LANES):
            piece = pieces[j][0, unit * rows : (unit + 1) * rows, :].astype(F32)
            if unit < size // LANES:
                start = pl.multiple_of(quarter * size + unit * LANES, LANES)
                qkv[:, pl.ds(start, LANES)] = piece
            else:
                start = pl.multiple_of(quarter * (width // 4) + unit * LANES - size, LANES)
                out[:, pl.ds(start, LANES)] = piece
    one[...] = gain_sums(qkv[...], w_rows[...], gain_ref)


def body(tokens, cotangent, w_qkv, w_out, w_up, w_down, gain_attn, gain_mlp):
    slabs, cases = lax.axis_size("slab"), lax.axis_size("case")
    depth, height, across, width = tokens.shape[1:]
    units = w_up.shape[1]
    lines = height * across
    per = lines // slabs
    count = depth * lines
    sizes = (depth, per, across, count)
    factor = 1.0 / math.sqrt(count * slabs * cases)
    gain_one, gain_two = gain_attn.reshape(1, width), gain_mlp.reshape(1, width)
    spans = slabs // 2
    rows = width // slabs
    parts = slabs if depth * per % 16 == 0 else 1

    def permute(array, flip_slab, flip_case):
        return lax.ppermute(array, BOTH, swap_pairs(slabs, cases, flip_slab, flip_case))

    def exchange(blocks):
        if parts == 1:
            return [lax.all_to_all(blocks[0], "slab", split_axis=0, concat_axis=0, tiled=True)]
        got = {j: permute(blocks[j], j, 0) for j in range(parts - 1, 0, -1)}
        return [blocks[0]] + [got[j] for j in range(1, parts)]

    proj_bf = shape_of((count, 3 * width), BF16)
    rows_bf = shape_of((count, width), BF16)
    *mine, hold_x = call(
        functools.partial(plane_kernel, sizes),
        [shape_of((count // parts, 3 * width), BF16)] * parts + [rows_bf],
        tokens.reshape(count, width),
        cotangent.reshape(count, width),
        gain_one,
        w_qkv,
        near=[False] * 4,
        scratch=[
            pltpu.VMEM((count, width), BF16),
            pltpu.VMEM((count, width), BF16),
            pltpu.VMEM((1, width), F32),
            pltpu.VMEM((width, 3 * width), BF16),
            pltpu.VMEM((count, 3 * width), BF16),
            pltpu.SemaphoreType.DMA((4,)),
        ],
    )
    w_up_mine, w_down_mine = call(
        functools.partial(prepare_kernel, slabs),
        [shape_of((width, units // 4), BF16), shape_of((units // 4, width), BF16)],
        w_up,
        w_down,
    )
    got = exchange(mine)
    shared, proj_z, mixed, residual, hold_z = call(
        functools.partial(lines_kernel, sizes, parts),
        [shape_of((count, 2 * width), BF16), proj_bf, rows_bf, rows_bf, rows_bf],
        *got,
        gain_one,
        gain_two,
        w_qkv,
        w_out,
        after=[w_up_mine],
    )
    shared_y = permute(shared, 0, 2)
    grad_mixed, grad_residual = call(
        mlp_kernel,
        [rows_bf, shape_of((count, width), F32)],
        shared,
        residual,
        gain_two,
        w_out,
        w_up,
        w_down,
    )
    back, pack_z = call(
        functools.partial(lines_back_kernel, sizes, parts),
        [shape_of((count, 2 * width), BF16), shape_of((count, 6 * width), BF16)],
        proj_z,
        grad_mixed,
        grad_residual,
        mixed,
        hold_z,
        gain_one,
        w_qkv,
    )
    back = lax.all_to_all(back, "slab", split_axis=0, concat_axis=0, tiled=True)
    pack_z_core = permute(pack_z, 0, 1)
    (pack_p,) = call(
        functools.partial(plane_grads_kernel, sizes, parts),
        [shape_of((count, 4 * width), BF16)],
        back,
        hold_x,
        gain_one,
        w_qkv,
        scratch=[pltpu.VMEM((count, 3 * width), BF16)],
    )
    (around,) = call(
        join_kernel, [shape_of((2 * count, 2 * width), BF16)], shared, shared_y, after=[pack_p]
    )
    big_keep, big_send = call(
        functools.partial(grads_mlp_kernel, factor),
        [shape_of((spans, rows, 2 * width), BF16)] * 2,
        around,
        permute(around, 0, 1),
        w_up_mine,
        w_down_mine,
        scratch=[pltpu.VMEM((units // 4, width), F32), pltpu.VMEM((width, units // 4), F32)],
    )
    small = call(
        functools.partial(grads_qkv_kernel, factor, width, slabs),
        [shape_of((spans, rows * (width // LANES), LANES), BF16)] * 4,
        pack_z,
        pack_z_core,
        pack_p,
        permute(pack_p, 0, 1),
        after=[big_keep],
        scratch=[pltpu.VMEM((width, width), F32)],
    )
    ready = small[0]
    small = [small[0], permute(small[1], 1, 0), permute(small[2], 0, 2), permute(small[3], 1, 2)]
    grad_tokens, flag = call(
        functools.partial(plane_tokens_kernel, sizes, parts),
        [rows_bf, shape_of((8, LANES), F32)],
        back,
        pack_p,
        hold_x,
        gain_one,
        w_qkv,
        after=[ready],
    )

    def reduce_z(pieces, after=()):
        left = spans
        while left > 1:
            radix = min(4, left)
            left //= radix
            shift = (left * 2).bit_length() - 1
            split = fold(shift, radix, pieces, after)
            pieces = [split[0]] + [permute(split[j], j << shift, 0) for j in range(1, radix)]
        return pieces

    def gather(pieces, after=()):
        (last,) = fold(0, 1, pieces, after)
        return [last] + [permute(last, 0, j) for j in range(1, 4)]

    big = reduce_z([big_keep, permute(big_send, 1, 0)], [flag])
    small = reduce_z(small)
    big = gather(big, [small[0]])
    full_up, full_down, full_two, w_rows = call(
        functools.partial(place_mlp_kernel, slabs, width, units),
        [
            shape_of((rows, units), F32),
            shape_of((units // slabs, width), F32),
            shape_of((1, rows), F32),
            shape_of((rows, 3 * width), BF16),
        ],
        *big,
        gain_two,
        w_up,
        w_qkv,
        near=[True] * 5 + [False] * 2,
        scratch=[
            pltpu.VMEM((4, rows, 2 * width), F32),
            pltpu.VMEM((rows, units), BF16),
            pltpu.SemaphoreType.DMA((2,)),
        ],
    )
    small = gather(small)
    full_qkv, full_out, full_one = call(
        functools.partial(place_qkv_kernel, slabs, width),
        [shape_of((rows, 3 * width), F32), shape_of((rows, width), F32), shape_of((1, rows), F32)],
        *small,
        gain_one,
        w_rows,
    )
    return (
        grad_tokens.reshape(tokens.shape),
        full_qkv,
        full_out,
        full_up,
        full_down,
        full_one.reshape(rows),
        full_two.reshape(rows),
    )


def solution(mesh):
    grid = P("case", "slab", None, None, None)
    return jax.shard_map(
        body,
        mesh=mesh,
        in_specs=(grid, grid, P(), P(), P(), P(), P(), P()),
        out_specs=(
            grid,
            P("slab", None),
            P("slab", None),
            P("slab", None),
            P("slab", None),
            P("slab"),
            P("slab"),
        ),
        check_vma=False,
    )
```

```python
import functools
import math

import jax
import jax.numpy as jnp
from jax import lax
from jax.experimental import pallas as pl
from jax.experimental.pallas import tpu as pltpu
from jax.sharding import PartitionSpec as P

HEADS = 8
LANES = 128
EPSILON = 1e-06
ROOT_TWO_PI = math.sqrt(2.0 / math.pi)
F32 = jnp.float32
BF16 = jnp.bfloat16
BOTH = ("slab", "case")
VMEM_BYTES = 24 * 1024 * 1024


def dot(a, b):
    return lax.dot_general(a, b, (((1,), (0,)), ((), ())), preferred_element_type=F32)


def dot_nt(a, b):
    return lax.dot_general(a, b, (((1,), (1,)), ((), ())), preferred_element_type=F32)


def dot_tn(a, b):
    return lax.dot_general(a, b, (((0,), (0,)), ((), ())), preferred_element_type=F32)


def norm_stats(values):
    inverse = lax.rsqrt(jnp.mean(values * values, axis=-1, keepdims=True) + EPSILON)
    return values * inverse, inverse


def norm_back(scaled, normed, inverse):
    return inverse * (scaled - normed * jnp.mean(scaled * normed, axis=-1, keepdims=True))


def call(kernel, outs, *args, after=(), scratch=(), near=None, flops=10**7):
    count = len(args)
    near = [True] * count if near is None else near

    def run(*refs):
        kernel(*refs[:count], *refs[count + len(after) :])

    vmem, far = pl.BlockSpec(memory_space=pltpu.VMEM), pl.BlockSpec(memory_space=pltpu.HBM)
    return pl.pallas_call(
        run,
        out_shape=outs,
        in_specs=[vmem if one else far for one in near] + [pl.BlockSpec(memory_space=pl.ANY)] * len(after),
        out_specs=[vmem] * len(outs),
        scratch_shapes=list(scratch),
        cost_estimate=pl.CostEstimate(flops=flops, transcendentals=0, bytes_accessed=10**4),
        compiler_params=pltpu.CompilerParams(vmem_limit_bytes=VMEM_BYTES),
    )(
        *[
            arg if one else pltpu.with_memory_space_constraint(arg, pltpu.HBM)
            for arg, one in zip(args, near)
        ],
        *after,
    )


def shape_of(shape, dtype):
    return jax.ShapeDtypeStruct(shape, dtype)


def line_masks(sizes, kind):
    depth, per, across, count = sizes
    rows = lax.broadcasted_iota(jnp.int32, (2 * count, count), 0) & (count - 1)
    cols = lax.broadcasted_iota(jnp.int32, (2 * count, count), 1)

    def parts(t):
        chunk = t // (depth * per)
        plane = (t // per) & (depth - 1)
        spot = chunk * per + (t & (per - 1))
        return plane, spot // across, spot & (across - 1), t & (per - 1)

    a, b = parts(rows), parts(cols)
    if kind == "z":
        return [a[3] == b[3]]
    same = a[0] == b[0]
    return [same & (a[1] == b[1]), same & (a[2] == b[2])]


def softmax_in(scores, mask):
    held = jnp.where(mask, scores, -1e30)
    weights = jnp.exp(held - jnp.max(held, axis=-1, keepdims=True))
    return weights / jnp.sum(weights, axis=-1, keepdims=True)


def pair_parts(proj, pair, width):
    at = pair * LANES
    return [proj[:, which * width + at : which * width + at + LANES] for which in range(3)]


def halves():
    lane = lax.broadcasted_iota(jnp.int32, (1, LANES), 1)
    low = (lane < LANES // 2).astype(F32)
    return low.astype(BF16), (1.0 - low).astype(BF16)


def stack(block, low, high):
    return jnp.concatenate([block * low, block * high], axis=0)


def side(block):
    count = block.shape[0] // 2
    return jnp.concatenate([block[:count], block[count:]], axis=1)


def attend(proj, masks, width):
    low, high = halves()
    scale = (width // HEADS) ** (-0.5)
    outs = []
    for pair in range(HEADS // 2):
        q2, k2, v2 = pair_parts(proj, pair, width)
        scores = dot_nt(stack(q2, low, high), k2) * scale
        probs = sum(softmax_in(scores, mask).astype(BF16).astype(F32) for mask in masks)
        outs.append(dot(side(probs.astype(BF16)), stack(v2, low, high)))
    return jnp.concatenate(outs, axis=1)


def attend_back(proj, grad, masks, width, out_ref, at):
    low, high = halves()
    scale = (width // HEADS) ** (-0.5)
    for pair in range(HEADS // 2):
        q2, k2, v2 = pair_parts(proj, pair, width)
        g2 = grad[:, pair * LANES : (pair + 1) * LANES]
        qs, gs = stack(q2, low, high), stack(g2, low, high)
        scores = dot_nt(qs, k2) * scale
        grad_probs = dot_nt(gs, v2)
        probs = jnp.zeros_like(scores)
        grad_scores = jnp.zeros_like(scores)
        for mask in masks:
            one = softmax_in(scores, mask)
            probs += one.astype(BF16).astype(F32)
            grad_scores += one * (grad_probs - jnp.sum(one * grad_probs, axis=-1, keepdims=True))
        probs, grad_scores = probs.astype(BF16), grad_scores.astype(BF16)
        found = (
            dot(side(grad_scores), stack(k2, low, high)) * scale,
            dot_tn(grad_scores, qs) * scale,
            dot_tn(probs, gs),
        )
        for which in range(3):
            start = at + which * width + pair * LANES
            out_ref[0 : q2.shape[0], start : start + LANES] = found[which].astype(BF16)


def chunk_order(sizes, parts):
    depth, per, _, count = sizes
    rows = lax.broadcasted_iota(jnp.int32, (count, count), 0)
    cols = lax.broadcasted_iota(jnp.int32, (count, count), 1)
    chunk = rows // (depth * per)
    if parts > 1:
        chunk = chunk ^ lax.axis_index("slab")
    plane = (rows // per) & (depth - 1)
    return plane * (count // depth) + chunk * per + (rows & (per - 1)) == cols


def put_parts(refs, at, value):
    rows = refs[0].shape[0]
    for j, ref in enumerate(refs):
        ref[:, at : at + value.shape[1]] = value[j * rows : (j + 1) * rows]


def joined(refs, start, stop):
    return jnp.concatenate([ref[:, start:stop] for ref in refs], axis=0)


def plane_kernel(sizes, x_ref, cot_ref, gain_ref, w_ref, *refs):
    parts, hold_x = refs[:-7], refs[-7]
    x_in, cot_in, gain_in, w_in, proj, sems = refs[-6:]
    copies = [
        pltpu.make_async_copy(src, dst, sems.at[i])
        for i, (src, dst) in enumerate(
            ((x_ref, x_in), (gain_ref, gain_in), (w_ref, w_in), (cot_ref, cot_in))
        )
    ]
    for copy in copies:
        copy.start()
    width = w_in.shape[0]
    order = chunk_order(sizes, len(parts)).astype(F32).astype(BF16)
    masks = line_masks(sizes, "xy")
    copies[0].wait()
    x = dot(order, x_in[...])
    hold_x[...] = x.astype(BF16)
    put_parts(parts, 0, hold_x[...])
    copies[1].wait()
    normed, _ = norm_stats(x)
    hidden = (normed * gain_in[...]).astype(BF16)
    copies[2].wait()
    proj[...] = dot(hidden, w_in[...]).astype(BF16)
    put_parts(parts, 2 * width, attend(proj[...], masks, width).astype(BF16))
    copies[3].wait()
    put_parts(parts, width, dot(order, cot_in[...]).astype(BF16))


def prepare_kernel(slabs, w_up_ref, w_down_ref, up_ref, down_ref):
    quarter = lax.axis_index("case")
    units = w_up_ref.shape[1]
    fine = units // slabs // 4
    rows = lax.broadcasted_iota(jnp.int32, (8 * LANES, LANES), 0)
    cols = lax.broadcasted_iota(jnp.int32, (8 * LANES, LANES), 1)
    for flip in range(2):
        x = (lax.axis_index("slab") & 1) ^ flip
        wanted = ((cols // fine * 2 + x) * 4 + quarter) * fine + (cols & (fine - 1))
        pick = (rows == wanted).astype(F32).astype(BF16)
        start = flip * units // 8
        for group in range(units // 8 // LANES):
            up_ref[:, start + group * LANES : start + (group + 1) * LANES] = dot(
                w_up_ref[:, group * 8 * LANES : (group + 1) * 8 * LANES], pick
            ).astype(BF16)
        for z in range(slabs // 2):
            at = pl.multiple_of(((z * 2 + x) * 4 + quarter) * fine, 8)
            down_ref[start + z * fine : start + (z + 1) * fine, :] = w_down_ref[pl.ds(at, fine), :]


def lines_kernel(sizes, parts, *refs):
    got = refs[:parts]
    gain_one_ref, gain_two_ref, w_ref, w_out_ref = refs[parts : parts + 4]
    shared_ref, proj_ref, mixed_ref, residual_ref, hold_x = refs[parts + 4 :]
    width = w_ref.shape[0]
    hold_x[...] = joined(got, 0, width)
    x = hold_x[...].astype(F32)
    normed, _ = norm_stats(x)
    proj_ref[...] = dot((normed * gain_one_ref[...]).astype(BF16), w_ref[...]).astype(BF16)
    out_z = attend(proj_ref[...], line_masks(sizes, "z"), width).astype(BF16)
    mixed = (joined(got, 2 * width, 3 * width).astype(F32) + out_z.astype(F32)).astype(BF16)
    residual = (x + dot(mixed, w_out_ref[...])).astype(BF16)
    normed_two, _ = norm_stats(residual.astype(F32))
    shared_ref[:, :width] = (normed_two * gain_two_ref[...]).astype(BF16)
    shared_ref[:, width:] = joined(got, width, 2 * width)
    mixed_ref[...] = mixed
    residual_ref[...] = residual


def gelu_parts(upper):
    square = upper * upper
    tangent = jnp.tanh(ROOT_TWO_PI * (upper + 0.044715 * upper * square))
    half = 0.5 * (1.0 + tangent)
    slope = half + 0.5 * upper * (1.0 - tangent * tangent) * ROOT_TWO_PI * (
        1.0 + 3.0 * 0.044715 * square
    )
    return (upper * half).astype(BF16), slope


def mlp_kernel(
    shared_ref, residual_ref, gain_ref, w_out_ref, w_up_ref, w_down_ref, grad_ref, gres_ref
):
    width, units = w_up_ref.shape
    hidden, cot = shared_ref[:, :width], shared_ref[:, width:]
    normed, inverse = norm_stats(residual_ref[...].astype(F32))
    step = min(512, units)
    grad_hidden = jnp.zeros(normed.shape, F32)
    for at in range(0, units, step):
        _, slope = gelu_parts(dot(hidden, w_up_ref[:, at : at + step]))
        grad_upper = (dot_nt(cot, w_down_ref[at : at + step, :]) * slope).astype(BF16)
        grad_hidden += dot_nt(grad_upper, w_up_ref[:, at : at + step])
    grad_residual = cot.astype(F32) + norm_back(grad_hidden * gain_ref[...], normed, inverse)
    gres_ref[...] = grad_residual
    grad_ref[...] = dot_nt(grad_residual.astype(BF16), w_out_ref[...]).astype(BF16)


def lines_back_kernel(
    sizes, parts, proj_ref, grad_ref, gres_ref, mixed_ref, x_ref, gain_ref, w_ref, back_ref, pack_ref
):
    width = w_ref.shape[0]
    pack_ref[:, 4 * width : 5 * width] = mixed_ref[...]
    pack_ref[:, 5 * width :] = gres_ref[...].astype(BF16)
    attend_back(proj_ref[...], grad_ref[...], line_masks(sizes, "z"), width, pack_ref, width)
    normed, inverse = norm_stats(x_ref[...].astype(F32))
    pack_ref[:, :width] = (normed * gain_ref[...]).astype(BF16)
    grad_hidden = dot_nt(pack_ref[:, width : 4 * width], w_ref[...])
    back = norm_back(grad_hidden * gain_ref[...], normed, inverse)
    part = (gres_ref[...] + back).astype(BF16)
    for j, (spot, size) in enumerate(blocks_of(part.shape[0], parts)):
        back_ref[pl.ds(spot, size), :width] = grad_ref[j * size : (j + 1) * size, :]
        back_ref[pl.ds(spot, size), width:] = part[j * size : (j + 1) * size]


def blocks_of(count, parts):
    size = count // parts
    if parts == 1:
        return [(0, size)]
    me = lax.axis_index("slab")
    return [(pl.multiple_of((me ^ j) * size, 16), size) for j in range(parts)]


def partner_order(ref, parts, start, stop):
    return jnp.concatenate(
        [ref[pl.ds(spot, size), start:stop] for spot, size in blocks_of(ref.shape[0], parts)], axis=0
    )


def copy_kernel(in_ref, out_ref):
    out_ref[...] = in_ref[...]


def join_kernel(*refs):
    out_ref = refs[-1]
    rows = refs[0].shape[0]
    for j, ref in enumerate(refs[:-1]):
        out_ref[j * rows : (j + 1) * rows, :] = ref[...]


def plane_grads_kernel(sizes, parts, *refs):
    back_ref, x_ref, gain_ref, w_ref, pack_ref, proj = refs
    width = w_ref.shape[0]
    normed, _ = norm_stats(x_ref[...].astype(F32))
    pack_ref[:, :width] = (normed * gain_ref[...]).astype(BF16)
    proj[...] = dot(pack_ref[:, :width], w_ref[...]).astype(BF16)
    grad = partner_order(back_ref, parts, 0, width)
    attend_back(proj[...], grad, line_masks(sizes, "xy"), width, pack_ref, width)


def plane_tokens_kernel(sizes, parts, *refs):
    back_ref, pack_ref, x_ref, gain_ref, w_ref, grad_ref, flag_ref = refs
    flag_ref[...] = jnp.zeros_like(flag_ref)
    width = w_ref.shape[0]
    normed, inverse = norm_stats(x_ref[...].astype(F32))
    grad_hidden = dot_nt(pack_ref[:, width:], w_ref[...])
    back = norm_back(grad_hidden * gain_ref[...], normed, inverse)
    part = partner_order(back_ref, parts, width, 2 * width).astype(F32)
    order = chunk_order(sizes, parts).astype(F32).astype(BF16)
    grad_ref[...] = dot_tn(order, (back + part).astype(BF16)).astype(BF16)


def place():
    slab, case = lax.axis_index("slab"), lax.axis_index("case")
    return slab & 1, case >> 1, case & 1, slab >> 1


def store_units(scratch, rows, units, x, flip, outs, at):
    blocks = outs[0].shape[0]
    for z in range(blocks):
        start = pl.multiple_of((z * 2 + (x ^ flip)) * rows, 8)
        block = scratch[pl.ds(start, rows), 0 : units * LANES].astype(BF16)
        for unit in range(units):
            outs[flip][z, at + unit * rows : at + (unit + 1) * rows, :] = block[
                :, unit * LANES : (unit + 1) * LANES
            ]


def grads_mlp_kernel(factor, shift, here_ref, there_ref, w_up_ref, w_down_ref, *refs):
    outs, down, up = refs[:-2], refs[-2], refs[-1]
    width, units = w_up_ref.shape
    slab = lax.axis_index("slab")
    digit = (slab >> shift) & (len(outs) - 1)
    hidden = jnp.concatenate([ref[:, :width] for ref in (here_ref, there_ref)], axis=0)
    cot = jnp.concatenate([ref[:, width:] for ref in (here_ref, there_ref)], axis=0)
    half = units // 2
    for at in (0, half):
        active, slope = gelu_parts(dot(hidden, w_up_ref[:, at : at + half]))
        grad_upper = (dot_nt(cot, w_down_ref[at : at + half, :]) * slope).astype(BF16)
        up[:, at : at + half] = dot_tn(hidden, grad_upper) * factor
        if at == 0:
            down[...] = dot_tn(active, cot) * factor
    rest, rows = outs[0].shape[:2]
    for j, out in enumerate(outs):
        for k in range(rest):
            z = (digit ^ j) * rest + k
            at = pl.ds(pl.multiple_of(z * rows, 8), rows)
            out[k, :, :width] = down[at, :].astype(BF16)
            at = pl.ds(pl.multiple_of((z * 2 + (slab & 1)) * rows, 8), rows)
            out[k, :, width:] = up[at, :].astype(BF16)


def grads_qkv_kernel(factor, width, slabs, za_ref, zb_ref, pa_ref, pb_ref, *refs):
    outs, scratch = refs[:4], refs[4]
    x, y, core, _ = place()
    size, narrow = 3 * width // 4, width // 4
    rows = width // slabs
    hidden = jnp.concatenate([r[:, :width] for r in (za_ref, zb_ref, pa_ref, pb_ref)], axis=0)
    mixed = jnp.concatenate([r[:, 4 * width : 5 * width] for r in (za_ref, zb_ref)], axis=0)
    for flip_y in range(2):
        quarter = (y ^ flip_y) * 2 + core
        at = pl.multiple_of(width + quarter * size, LANES)
        cols = jnp.concatenate(
            [r[:, pl.ds(at, size)] for r in (za_ref, zb_ref, pa_ref, pb_ref)], axis=0
        )
        scratch[:, :size] = dot_tn(hidden, cols) * factor
        at = pl.multiple_of(5 * width + quarter * narrow, LANES)
        cols = jnp.concatenate([r[:, pl.ds(at, narrow)] for r in (za_ref, zb_ref)], axis=0)
        scratch[:, size:] = dot_tn(mixed, cols) * factor
        for flip in range(2):
            store_units(scratch, rows, width // LANES, x, flip, outs[2 * flip_y : 2 * flip_y + 2], 0)


def fold_kernel(shift, radix, count, *refs):
    ins, outs = refs[:count], refs[count:]
    digit = (lax.axis_index("slab") >> shift) & (radix - 1)
    rest = ins[0].shape[0] // radix
    for j in range(radix):
        for k in range(rest):
            at = (digit ^ j) * rest + k
            total = ins[0][at].astype(F32)
            for ref in ins[1:]:
                total += ref[at].astype(F32)
            outs[j][k] = total.astype(BF16)


def fold(shift, radix, pieces, after=()):
    first = pieces[0].shape
    outs = [shape_of((first[0] // radix,) + first[1:], BF16)] * radix
    kernel = functools.partial(fold_kernel, shift, radix, len(pieces))
    return call(kernel, outs, *pieces, after=after)


def swap_pairs(slabs, cases, flip_slab, flip_case):
    return [
        (s * cases + c, (s ^ flip_slab) * cases + (c ^ flip_case))
        for s in range(slabs)
        for c in range(cases)
    ]


def gain_sums(grad, w_rows, gain_ref):
    rows, width = grad.shape[0], gain_ref.shape[1]
    spot = lax.axis_index("slab") * rows + lax.broadcasted_iota(jnp.int32, (rows, width), 0)
    lanes = lax.broadcasted_iota(jnp.int32, (rows, width), 1)
    gain = jnp.sum(jnp.where(lanes == spot, gain_ref[...], 0.0), axis=1, keepdims=True)
    total = jnp.sum(grad * w_rows.astype(F32), axis=1, keepdims=True) / gain
    return jnp.transpose(jnp.broadcast_to(total, (rows, LANES)))[0:1, :]


def place_mlp_kernel(slabs, width, units, *refs):
    pieces, (gain_ref, w_up_ref, w_ref) = refs[:4], refs[4:7]
    up, down, two, w_rows, held, up_rows, sems = refs[7:]
    rows = width // slabs
    here = pl.ds(pl.multiple_of(lax.axis_index("slab") * rows, 8), rows)
    copies = [
        pltpu.make_async_copy(w_up_ref.at[here], up_rows, sems.at[0]),
        pltpu.make_async_copy(w_ref.at[here], w_rows, sems.at[1]),
    ]
    for copy in copies:
        copy.start()
    case, x = lax.axis_index("case"), lax.axis_index("slab") & 1
    eighth, fine = units // 8, units // 4 // slabs
    for j in range(4):
        piece = pieces[j][0].astype(F32)
        held[case ^ j, :, :width] = piece[:, :width]
        for flip in range(2):
            at = pl.multiple_of(width + (x ^ flip) * eighth, LANES)
            held[case ^ j, :, pl.ds(at, eighth)] = piece[
                :, width + flip * eighth : width + (flip + 1) * eighth
            ]
    for quarter in range(4):
        down[quarter * rows : (quarter + 1) * rows, :] = held[quarter, :, :width]
    for block in range(slabs):
        up[:, block * 4 * fine : (block + 1) * 4 * fine] = jnp.concatenate(
            [
                held[quarter, :, pl.ds(width + block % 2 * eighth + block // 2 * fine, fine)]
                for quarter in range(4)
            ],
            axis=1,
        )
    for copy in copies:
        copy.wait()
    two[...] = gain_sums(up[...], up_rows[...], gain_ref)


def place_qkv_kernel(slabs, width, *refs):
    pieces, (gain_ref, w_rows), (qkv, out, one) = refs[:4], refs[4:6], refs[6:]
    case = lax.axis_index("case")
    rows = width // slabs
    size = 3 * width // 4
    for j in range(4):
        quarter = case ^ j
        for unit in range(width // LANES):
            piece = pieces[j][0, unit * rows : (unit + 1) * rows, :].astype(F32)
            if unit < size // LANES:
                start = pl.multiple_of(quarter * size + unit * LANES, LANES)
                qkv[:, pl.ds(start, LANES)] = piece
            else:
                start = pl.multiple_of(quarter * (width // 4) + unit * LANES - size, LANES)
                out[:, pl.ds(start, LANES)] = piece
    one[...] = gain_sums(qkv[...], w_rows[...], gain_ref)


def body(tokens, cotangent, w_qkv, w_out, w_up, w_down, gain_attn, gain_mlp):
    slabs, cases = lax.axis_size("slab"), lax.axis_size("case")
    depth, height, across, width = tokens.shape[1:]
    units = w_up.shape[1]
    lines = height * across
    per = lines // slabs
    count = depth * lines
    sizes = (depth, per, across, count)
    factor = 1.0 / math.sqrt(count * slabs * cases)
    gain_one, gain_two = gain_attn.reshape(1, width), gain_mlp.reshape(1, width)
    spans = slabs // 2
    rows = width // slabs
    parts = slabs if depth * per % 16 == 0 else 1

    def permute(array, flip_slab, flip_case):
        return lax.ppermute(array, BOTH, swap_pairs(slabs, cases, flip_slab, flip_case))

    def exchange(blocks):
        if parts == 1:
            return [lax.all_to_all(blocks[0], "slab", split_axis=0, concat_axis=0, tiled=True)]
        got = {j: permute(blocks[j], j, 0) for j in range(parts - 1, 0, -1)}
        return [blocks[0]] + [got[j] for j in range(1, parts)]

    proj_bf = shape_of((count, 3 * width), BF16)
    rows_bf = shape_of((count, width), BF16)
    *mine, hold_x = call(
        functools.partial(plane_kernel, sizes),
        [shape_of((count // parts, 3 * width), BF16)] * parts + [rows_bf],
        tokens.reshape(count, width),
        cotangent.reshape(count, width),
        gain_one,
        w_qkv,
        near=[False] * 4,
        scratch=[
            pltpu.VMEM((count, width), BF16),
            pltpu.VMEM((count, width), BF16),
            pltpu.VMEM((1, width), F32),
            pltpu.VMEM((width, 3 * width), BF16),
            pltpu.VMEM((count, 3 * width), BF16),
            pltpu.SemaphoreType.DMA((4,)),
        ],
    )
    w_up_mine, w_down_mine = call(
        functools.partial(prepare_kernel, slabs),
        [shape_of((width, units // 4), BF16), shape_of((units // 4, width), BF16)],
        w_up,
        w_down,
    )
    got = exchange(mine)
    shared, proj_z, mixed, residual, hold_z = call(
        functools.partial(lines_kernel, sizes, parts),
        [shape_of((count, 2 * width), BF16), proj_bf, rows_bf, rows_bf, rows_bf],
        *got,
        gain_one,
        gain_two,
        w_qkv,
        w_out,
        after=[w_up_mine],
    )
    shared_x, shared_y = permute(shared, 1, 0), permute(shared, 0, 2)
    grad_mixed, grad_residual = call(
        mlp_kernel,
        [rows_bf, shape_of((count, width), F32)],
        shared,
        residual,
        gain_two,
        w_out,
        w_up,
        w_down,
    )
    back, pack_z = call(
        functools.partial(lines_back_kernel, sizes, parts),
        [shape_of((count, 2 * width), BF16), shape_of((count, 6 * width), BF16)],
        proj_z,
        grad_mixed,
        grad_residual,
        mixed,
        hold_z,
        gain_one,
        w_qkv,
    )
    (back,) = call(
        copy_kernel, [shape_of((count, 2 * width), BF16)], back, after=[shared_x, shared_y]
    )
    back = lax.all_to_all(back, "slab", split_axis=0, concat_axis=0, tiled=True)
    pack_z_core = permute(pack_z, 0, 1)
    (pack_p,) = call(
        functools.partial(plane_grads_kernel, sizes, parts),
        [shape_of((count, 4 * width), BF16)],
        back,
        hold_x,
        gain_one,
        w_qkv,
        scratch=[pltpu.VMEM((count, 3 * width), BF16)],
    )
    (around,) = call(
        join_kernel,
        [shape_of((4 * count, 2 * width), BF16)],
        shared,
        shared_x,
        shared_y,
        permute(shared_x, 0, 2),
        after=[pack_p],
    )
    radix = min(4, spans)
    shift = (slabs // radix).bit_length() - 1
    big = call(
        functools.partial(grads_mlp_kernel, factor, shift),
        [shape_of((spans // radix, rows, 2 * width), BF16)] * radix,
        around,
        permute(around, 0, 1),
        w_up_mine,
        w_down_mine,
        scratch=[pltpu.VMEM((units // 8, width), F32), pltpu.VMEM((width, units // 4), F32)],
    )
    early = big[0]
    small = call(
        functools.partial(grads_qkv_kernel, factor, width, slabs),
        [shape_of((spans, rows * (width // LANES), LANES), BF16)] * 4,
        pack_z,
        pack_z_core,
        pack_p,
        permute(pack_p, 0, 1),
        scratch=[pltpu.VMEM((width, width), F32)],
    )
    ready = small[0]
    small = [small[0], permute(small[1], 1, 0), permute(small[2], 0, 2), permute(small[3], 1, 2)]
    grad_tokens, flag = call(
        functools.partial(plane_tokens_kernel, sizes, parts),
        [rows_bf, shape_of((8, LANES), F32)],
        back,
        pack_p,
        hold_x,
        gain_one,
        w_qkv,
        after=[ready, early],
    )

    def reduce_z(split):
        left = spans
        while True:
            radix = len(split)
            left //= radix
            shift = (left * 2).bit_length() - 1
            pieces = [split[0]] + [permute(split[j], j << shift, 0) for j in range(1, radix)]
            if left == 1:
                return pieces
            radix = min(4, left)
            split = fold((left // radix * 2).bit_length() - 1, radix, pieces)

    def gather(last):
        return [last] + [permute(last, 0, j) for j in range(1, 4)]

    big = reduce_z(big)
    small = reduce_z(fold(shift, radix, small, [flag]))
    big = gather(fold(0, 1, big, [small[0]])[0])
    full_up, full_down, full_two, w_rows = call(
        functools.partial(place_mlp_kernel, slabs, width, units),
        [
            shape_of((rows, units), F32),
            shape_of((units // slabs, width), F32),
            shape_of((1, rows), F32),
            shape_of((rows, 3 * width), BF16),
        ],
        *big,
        gain_two,
        w_up,
        w_qkv,
        near=[True] * 5 + [False] * 2,
        scratch=[
            pltpu.VMEM((4, rows, 2 * width), F32),
            pltpu.VMEM((rows, units), BF16),
            pltpu.SemaphoreType.DMA((2,)),
        ],
    )
    small = gather(fold(0, 1, small)[0])
    full_qkv, full_out, full_one = call(
        functools.partial(place_qkv_kernel, slabs, width),
        [shape_of((rows, 3 * width), F32), shape_of((rows, width), F32), shape_of((1, rows), F32)],
        *small,
        gain_one,
        w_rows,
    )
    return (
        grad_tokens.reshape(tokens.shape),
        full_qkv,
        full_out,
        full_up,
        full_down,
        full_one.reshape(rows),
        full_two.reshape(rows),
    )


def solution(mesh):
    grid = P("case", "slab", None, None, None)
    return jax.shard_map(
        body,
        mesh=mesh,
        in_specs=(grid, grid, P(), P(), P(), P(), P(), P()),
        out_specs=(
            grid,
            P("slab", None),
            P("slab", None),
            P("slab", None),
            P("slab", None),
            P("slab"),
            P("slab"),
        ),
        check_vma=False,
    )
```

```python
import functools
import math

import jax
import jax.numpy as jnp
from jax import lax
from jax.experimental import pallas as pl
from jax.experimental.pallas import tpu as pltpu
from jax.sharding import PartitionSpec as P

HEADS = 8
LANES = 128
EPSILON = 1e-06
ROOT_TWO_PI = math.sqrt(2.0 / math.pi)
F32 = jnp.float32
BF16 = jnp.bfloat16
BOTH = ("slab", "case")
VMEM_BYTES = 24 * 1024 * 1024


def dot(a, b):
    return lax.dot_general(a, b, (((1,), (0,)), ((), ())), preferred_element_type=F32)


def dot_nt(a, b):
    return lax.dot_general(a, b, (((1,), (1,)), ((), ())), preferred_element_type=F32)


def dot_tn(a, b):
    return lax.dot_general(a, b, (((0,), (0,)), ((), ())), preferred_element_type=F32)


def norm_stats(values):
    inverse = lax.rsqrt(jnp.mean(values * values, axis=-1, keepdims=True) + EPSILON)
    return values * inverse, inverse


def norm_back(scaled, normed, inverse):
    return inverse * (scaled - normed * jnp.mean(scaled * normed, axis=-1, keepdims=True))


def call(kernel, outs, *args, after=(), scratch=(), near=None, flops=10**7):
    count = len(args)
    near = [True] * count if near is None else near

    def run(*refs):
        kernel(*refs[:count], *refs[count + len(after) :])

    vmem, far = pl.BlockSpec(memory_space=pltpu.VMEM), pl.BlockSpec(memory_space=pltpu.HBM)
    return pl.pallas_call(
        run,
        out_shape=outs,
        in_specs=[vmem if one else far for one in near] + [pl.BlockSpec(memory_space=pl.ANY)] * len(after),
        out_specs=[vmem] * len(outs),
        scratch_shapes=list(scratch),
        cost_estimate=pl.CostEstimate(flops=flops, transcendentals=0, bytes_accessed=10**4),
        compiler_params=pltpu.CompilerParams(vmem_limit_bytes=VMEM_BYTES),
    )(
        *[
            arg if one else pltpu.with_memory_space_constraint(arg, pltpu.HBM)
            for arg, one in zip(args, near)
        ],
        *after,
    )


def shape_of(shape, dtype):
    return jax.ShapeDtypeStruct(shape, dtype)


def line_masks(sizes, kind):
    depth, per, across, count = sizes
    rows = lax.broadcasted_iota(jnp.int32, (2 * count, count), 0) & (count - 1)
    cols = lax.broadcasted_iota(jnp.int32, (2 * count, count), 1)

    def parts(t):
        chunk = t // (depth * per)
        plane = (t // per) & (depth - 1)
        spot = chunk * per + (t & (per - 1))
        return plane, spot // across, spot & (across - 1), t & (per - 1)

    a, b = parts(rows), parts(cols)
    if kind == "z":
        return [a[3] == b[3]]
    same = a[0] == b[0]
    return [same & (a[1] == b[1]), same & (a[2] == b[2])]


def softmax_in(scores, mask):
    held = jnp.where(mask, scores, -1e30)
    weights = jnp.exp(held - jnp.max(held, axis=-1, keepdims=True))
    return weights / jnp.sum(weights, axis=-1, keepdims=True)


def pair_parts(proj, pair, width):
    at = pair * LANES
    return [proj[:, which * width + at : which * width + at + LANES] for which in range(3)]


def halves():
    lane = lax.broadcasted_iota(jnp.int32, (1, LANES), 1)
    low = (lane < LANES // 2).astype(F32)
    return low.astype(BF16), (1.0 - low).astype(BF16)


def stack(block, low, high):
    return jnp.concatenate([block * low, block * high], axis=0)


def side(block):
    count = block.shape[0] // 2
    return jnp.concatenate([block[:count], block[count:]], axis=1)


def attend(proj, masks, width):
    low, high = halves()
    scale = (width // HEADS) ** (-0.5)
    outs = []
    for pair in range(HEADS // 2):
        q2, k2, v2 = pair_parts(proj, pair, width)
        scores = dot_nt(stack(q2, low, high), k2) * scale
        probs = sum(softmax_in(scores, mask).astype(BF16).astype(F32) for mask in masks)
        outs.append(dot(side(probs.astype(BF16)), stack(v2, low, high)))
    return jnp.concatenate(outs, axis=1)


def attend_back(proj, grad, masks, width, out_ref, at):
    low, high = halves()
    scale = (width // HEADS) ** (-0.5)
    for pair in range(HEADS // 2):
        q2, k2, v2 = pair_parts(proj, pair, width)
        g2 = grad[:, pair * LANES : (pair + 1) * LANES]
        qs, gs = stack(q2, low, high), stack(g2, low, high)
        scores = dot_nt(qs, k2) * scale
        grad_probs = dot_nt(gs, v2)
        probs = jnp.zeros_like(scores)
        grad_scores = jnp.zeros_like(scores)
        for mask in masks:
            one = softmax_in(scores, mask)
            probs += one.astype(BF16).astype(F32)
            grad_scores += one * (grad_probs - jnp.sum(one * grad_probs, axis=-1, keepdims=True))
        probs, grad_scores = probs.astype(BF16), grad_scores.astype(BF16)
        found = (
            dot(side(grad_scores), stack(k2, low, high)) * scale,
            dot_tn(grad_scores, qs) * scale,
            dot_tn(probs, gs),
        )
        for which in range(3):
            start = at + which * width + pair * LANES
            out_ref[0 : q2.shape[0], start : start + LANES] = found[which].astype(BF16)


def chunk_order(sizes, parts):
    depth, per, _, count = sizes
    rows = lax.broadcasted_iota(jnp.int32, (count, count), 0)
    cols = lax.broadcasted_iota(jnp.int32, (count, count), 1)
    chunk = rows // (depth * per)
    if parts > 1:
        chunk = chunk ^ lax.axis_index("slab")
    plane = (rows // per) & (depth - 1)
    return plane * (count // depth) + chunk * per + (rows & (per - 1)) == cols


def put_parts(refs, at, value):
    rows = refs[0].shape[0]
    for j, ref in enumerate(refs):
        ref[:, at : at + value.shape[1]] = value[j * rows : (j + 1) * rows]


def joined(refs, start, stop):
    return jnp.concatenate([ref[:, start:stop] for ref in refs], axis=0)


def plane_kernel(sizes, x_ref, cot_ref, gain_ref, w_ref, *refs):
    parts, hold_x = refs[:-7], refs[-7]
    x_in, cot_in, gain_in, w_in, proj, sems = refs[-6:]
    copies = [
        pltpu.make_async_copy(src, dst, sems.at[i])
        for i, (src, dst) in enumerate(
            ((x_ref, x_in), (gain_ref, gain_in), (w_ref, w_in), (cot_ref, cot_in))
        )
    ]
    for copy in copies:
        copy.start()
    width = w_in.shape[0]
    order = chunk_order(sizes, len(parts)).astype(F32).astype(BF16)
    masks = line_masks(sizes, "xy")
    copies[0].wait()
    x = dot(order, x_in[...])
    hold_x[...] = x.astype(BF16)
    put_parts(parts, 0, hold_x[...])
    copies[1].wait()
    normed, _ = norm_stats(x)
    hidden = (normed * gain_in[...]).astype(BF16)
    copies[2].wait()
    proj[...] = dot(hidden, w_in[...]).astype(BF16)
    put_parts(parts, 2 * width, attend(proj[...], masks, width).astype(BF16))
    copies[3].wait()
    put_parts(parts, width, dot(order, cot_in[...]).astype(BF16))


def prepare_kernel(slabs, w_up_ref, w_down_ref, up_ref, down_ref):
    quarter = lax.axis_index("case")
    units = w_up_ref.shape[1]
    fine = units // slabs // 4
    rows = lax.broadcasted_iota(jnp.int32, (8 * LANES, LANES), 0)
    cols = lax.broadcasted_iota(jnp.int32, (8 * LANES, LANES), 1)
    for flip in range(2):
        x = (lax.axis_index("slab") & 1) ^ flip
        wanted = ((cols // fine * 2 + x) * 4 + quarter) * fine + (cols & (fine - 1))
        pick = (rows == wanted).astype(F32).astype(BF16)
        start = flip * units // 8
        for group in range(units // 8 // LANES):
            up_ref[:, start + group * LANES : start + (group + 1) * LANES] = dot(
                w_up_ref[:, group * 8 * LANES : (group + 1) * 8 * LANES], pick
            ).astype(BF16)
        for z in range(slabs // 2):
            at = pl.multiple_of(((z * 2 + x) * 4 + quarter) * fine, 8)
            down_ref[start + z * fine : start + (z + 1) * fine, :] = w_down_ref[pl.ds(at, fine), :]


def lines_kernel(sizes, parts, *refs):
    got = refs[:parts]
    gain_one_ref, gain_two_ref, w_ref, w_out_ref = refs[parts : parts + 4]
    shared_ref, proj_ref, mixed_ref, residual_ref, hold_x = refs[parts + 4 :]
    width = w_ref.shape[0]
    hold_x[...] = joined(got, 0, width)
    x = hold_x[...].astype(F32)
    normed, _ = norm_stats(x)
    proj_ref[...] = dot((normed * gain_one_ref[...]).astype(BF16), w_ref[...]).astype(BF16)
    out_z = attend(proj_ref[...], line_masks(sizes, "z"), width).astype(BF16)
    mixed = (joined(got, 2 * width, 3 * width).astype(F32) + out_z.astype(F32)).astype(BF16)
    residual = (x + dot(mixed, w_out_ref[...])).astype(BF16)
    normed_two, _ = norm_stats(residual.astype(F32))
    shared_ref[:, :width] = (normed_two * gain_two_ref[...]).astype(BF16)
    shared_ref[:, width:] = joined(got, width, 2 * width)
    mixed_ref[...] = mixed
    residual_ref[...] = residual


def gelu_parts(upper):
    square = upper * upper
    tangent = jnp.tanh(ROOT_TWO_PI * (upper + 0.044715 * upper * square))
    half = 0.5 * (1.0 + tangent)
    slope = half + 0.5 * upper * (1.0 - tangent * tangent) * ROOT_TWO_PI * (
        1.0 + 3.0 * 0.044715 * square
    )
    return (upper * half).astype(BF16), slope


def mlp_kernel(
    shared_ref, residual_ref, gain_ref, w_out_ref, w_up_ref, w_down_ref, grad_ref, gres_ref
):
    width, units = w_up_ref.shape
    hidden, cot = shared_ref[:, :width], shared_ref[:, width:]
    normed, inverse = norm_stats(residual_ref[...].astype(F32))
    step = min(512, units)
    grad_hidden = jnp.zeros(normed.shape, F32)
    for at in range(0, units, step):
        _, slope = gelu_parts(dot(hidden, w_up_ref[:, at : at + step]))
        grad_upper = (dot_nt(cot, w_down_ref[at : at + step, :]) * slope).astype(BF16)
        grad_hidden += dot_nt(grad_upper, w_up_ref[:, at : at + step])
    grad_residual = cot.astype(F32) + norm_back(grad_hidden * gain_ref[...], normed, inverse)
    gres_ref[...] = grad_residual
    grad_ref[...] = dot_nt(grad_residual.astype(BF16), w_out_ref[...]).astype(BF16)


def lines_back_kernel(
    sizes, parts, proj_ref, grad_ref, gres_ref, mixed_ref, x_ref, gain_ref, w_ref, back_ref, pack_ref
):
    width = w_ref.shape[0]
    pack_ref[:, 4 * width : 5 * width] = mixed_ref[...]
    pack_ref[:, 5 * width :] = gres_ref[...].astype(BF16)
    attend_back(proj_ref[...], grad_ref[...], line_masks(sizes, "z"), width, pack_ref, width)
    normed, inverse = norm_stats(x_ref[...].astype(F32))
    pack_ref[:, :width] = (normed * gain_ref[...]).astype(BF16)
    grad_hidden = dot_nt(pack_ref[:, width : 4 * width], w_ref[...])
    back = norm_back(grad_hidden * gain_ref[...], normed, inverse)
    part = (gres_ref[...] + back).astype(BF16)
    for j, (spot, size) in enumerate(blocks_of(part.shape[0], parts)):
        back_ref[pl.ds(spot, size), :width] = grad_ref[j * size : (j + 1) * size, :]
        back_ref[pl.ds(spot, size), width:] = part[j * size : (j + 1) * size]


def blocks_of(count, parts):
    size = count // parts
    if parts == 1:
        return [(0, size)]
    me = lax.axis_index("slab")
    return [(pl.multiple_of((me ^ j) * size, 16), size) for j in range(parts)]


def partner_order(ref, parts, start, stop):
    return jnp.concatenate(
        [ref[pl.ds(spot, size), start:stop] for spot, size in blocks_of(ref.shape[0], parts)], axis=0
    )


def copy_kernel(in_ref, out_ref):
    out_ref[...] = in_ref[...]


def join_kernel(*refs):
    out_ref = refs[-1]
    rows = refs[0].shape[0]
    for j, ref in enumerate(refs[:-1]):
        out_ref[j * rows : (j + 1) * rows, :] = ref[...]


def plane_grads_kernel(sizes, parts, *refs):
    back_ref, x_ref, gain_ref, w_ref, pack_ref, proj = refs
    width = w_ref.shape[0]
    normed, _ = norm_stats(x_ref[...].astype(F32))
    pack_ref[:, :width] = (normed * gain_ref[...]).astype(BF16)
    proj[...] = dot(pack_ref[:, :width], w_ref[...]).astype(BF16)
    grad = partner_order(back_ref, parts, 0, width)
    attend_back(proj[...], grad, line_masks(sizes, "xy"), width, pack_ref, width)


def plane_tokens_kernel(sizes, parts, *refs):
    back_ref, pack_ref, x_ref, gain_ref, w_ref, grad_ref, flag_ref = refs
    flag_ref[...] = jnp.zeros_like(flag_ref)
    width = w_ref.shape[0]
    normed, inverse = norm_stats(x_ref[...].astype(F32))
    grad_hidden = dot_nt(pack_ref[:, width:], w_ref[...])
    back = norm_back(grad_hidden * gain_ref[...], normed, inverse)
    part = partner_order(back_ref, parts, width, 2 * width).astype(F32)
    order = chunk_order(sizes, parts).astype(F32).astype(BF16)
    grad_ref[...] = dot_tn(order, (back + part).astype(BF16)).astype(BF16)


def place():
    slab, case = lax.axis_index("slab"), lax.axis_index("case")
    return slab & 1, case >> 1, case & 1, slab >> 1


def store_units(scratch, rows, units, x, flip, outs, at):
    blocks = outs[0].shape[0]
    for z in range(blocks):
        start = pl.multiple_of((z * 2 + (x ^ flip)) * rows, 8)
        block = scratch[pl.ds(start, rows), 0 : units * LANES].astype(BF16)
        for unit in range(units):
            outs[flip][z, at + unit * rows : at + (unit + 1) * rows, :] = block[
                :, unit * LANES : (unit + 1) * LANES
            ]


def grads_mlp_kernel(factor, shift, here_ref, there_ref, w_up_ref, w_down_ref, *refs):
    outs, down, up = refs[:-2], refs[-2], refs[-1]
    width, units = w_up_ref.shape
    slab = lax.axis_index("slab")
    digit = (slab >> shift) & (len(outs) - 1)
    hidden = jnp.concatenate([ref[:, :width] for ref in (here_ref, there_ref)], axis=0)
    cot = jnp.concatenate([ref[:, width:] for ref in (here_ref, there_ref)], axis=0)
    half = units // 2
    for at in (0, half):
        active, slope = gelu_parts(dot(hidden, w_up_ref[:, at : at + half]))
        grad_upper = (dot_nt(cot, w_down_ref[at : at + half, :]) * slope).astype(BF16)
        up[:, at : at + half] = dot_tn(hidden, grad_upper) * factor
        if at == 0:
            down[...] = dot_tn(active, cot) * factor
    rest, rows = outs[0].shape[:2]
    for j, out in enumerate(outs):
        for k in range(rest):
            z = (digit ^ j) * rest + k
            at = pl.ds(pl.multiple_of(z * rows, 8), rows)
            out[k, :, :width] = down[at, :].astype(BF16)
            at = pl.ds(pl.multiple_of((z * 2 + (slab & 1)) * rows, 8), rows)
            out[k, :, width:] = up[at, :].astype(BF16)


def grads_qkv_kernel(factor, width, slabs, za_ref, zb_ref, pa_ref, pb_ref, *refs):
    outs, scratch = refs[:4], refs[4]
    x, y, core, _ = place()
    size, narrow = 3 * width // 4, width // 4
    rows = width // slabs
    hidden = jnp.concatenate([r[:, :width] for r in (za_ref, zb_ref, pa_ref, pb_ref)], axis=0)
    mixed = jnp.concatenate([r[:, 4 * width : 5 * width] for r in (za_ref, zb_ref)], axis=0)
    for flip_y in range(2):
        quarter = (y ^ flip_y) * 2 + core
        at = pl.multiple_of(width + quarter * size, LANES)
        cols = jnp.concatenate(
            [r[:, pl.ds(at, size)] for r in (za_ref, zb_ref, pa_ref, pb_ref)], axis=0
        )
        scratch[:, :size] = dot_tn(hidden, cols) * factor
        at = pl.multiple_of(5 * width + quarter * narrow, LANES)
        cols = jnp.concatenate([r[:, pl.ds(at, narrow)] for r in (za_ref, zb_ref)], axis=0)
        scratch[:, size:] = dot_tn(mixed, cols) * factor
        for flip in range(2):
            store_units(scratch, rows, width // LANES, x, flip, outs[2 * flip_y : 2 * flip_y + 2], 0)


def fold_kernel(shift, radix, count, *refs):
    ins, outs = refs[:count], refs[count:]
    digit = (lax.axis_index("slab") >> shift) & (radix - 1)
    rest = ins[0].shape[0] // radix
    for j in range(radix):
        for k in range(rest):
            at = (digit ^ j) * rest + k
            total = ins[0][at].astype(F32)
            for ref in ins[1:]:
                total += ref[at].astype(F32)
            outs[j][k] = total.astype(BF16)


def fold(shift, radix, pieces, after=()):
    first = pieces[0].shape
    outs = [shape_of((first[0] // radix,) + first[1:], BF16)] * radix
    kernel = functools.partial(fold_kernel, shift, radix, len(pieces))
    return call(kernel, outs, *pieces, after=after)


def swap_pairs(slabs, cases, flip_slab, flip_case):
    return [
        (s * cases + c, (s ^ flip_slab) * cases + (c ^ flip_case))
        for s in range(slabs)
        for c in range(cases)
    ]


def gain_sums(grad, w_rows, gain_ref):
    rows, width = grad.shape[0], gain_ref.shape[1]
    spot = lax.axis_index("slab") * rows + lax.broadcasted_iota(jnp.int32, (rows, width), 0)
    lanes = lax.broadcasted_iota(jnp.int32, (rows, width), 1)
    gain = jnp.sum(jnp.where(lanes == spot, gain_ref[...], 0.0), axis=1, keepdims=True)
    total = jnp.sum(grad * w_rows.astype(F32), axis=1, keepdims=True) / gain
    return jnp.transpose(jnp.broadcast_to(total, (rows, LANES)))[0:1, :]


def place_mlp_kernel(slabs, width, units, *refs):
    pieces, (gain_ref, w_up_ref, w_ref) = refs[:4], refs[4:7]
    up, down, two, w_rows, held, up_rows, sems = refs[7:]
    rows = width // slabs
    here = pl.ds(pl.multiple_of(lax.axis_index("slab") * rows, 8), rows)
    copies = [
        pltpu.make_async_copy(w_up_ref.at[here], up_rows, sems.at[0]),
        pltpu.make_async_copy(w_ref.at[here], w_rows, sems.at[1]),
    ]
    for copy in copies:
        copy.start()
    case, x = lax.axis_index("case"), lax.axis_index("slab") & 1
    eighth, fine = units // 8, units // 4 // slabs
    for j in range(4):
        piece = pieces[j][0].astype(F32)
        held[case ^ j, :, :width] = piece[:, :width]
        for flip in range(2):
            at = pl.multiple_of(width + (x ^ flip) * eighth, LANES)
            held[case ^ j, :, pl.ds(at, eighth)] = piece[
                :, width + flip * eighth : width + (flip + 1) * eighth
            ]
    for quarter in range(4):
        down[quarter * rows : (quarter + 1) * rows, :] = held[quarter, :, :width]
    for block in range(slabs):
        up[:, block * 4 * fine : (block + 1) * 4 * fine] = jnp.concatenate(
            [
                held[quarter, :, pl.ds(width + block % 2 * eighth + block // 2 * fine, fine)]
                for quarter in range(4)
            ],
            axis=1,
        )
    for copy in copies:
        copy.wait()
    two[...] = gain_sums(up[...], up_rows[...], gain_ref)


def place_qkv_kernel(slabs, width, *refs):
    pieces, (gain_ref, w_rows), (qkv, out, one) = refs[:4], refs[4:6], refs[6:]
    case = lax.axis_index("case")
    rows = width // slabs
    size = 3 * width // 4
    for j in range(4):
        quarter = case ^ j
        for unit in range(width // LANES):
            piece = pieces[j][0, unit * rows : (unit + 1) * rows, :].astype(F32)
            if unit < size // LANES:
                start = pl.multiple_of(quarter * size + unit * LANES, LANES)
                qkv[:, pl.ds(start, LANES)] = piece
            else:
                start = pl.multiple_of(quarter * (width // 4) + unit * LANES - size, LANES)
                out[:, pl.ds(start, LANES)] = piece
    one[...] = gain_sums(qkv[...], w_rows[...], gain_ref)


def body(tokens, cotangent, w_qkv, w_out, w_up, w_down, gain_attn, gain_mlp):
    slabs, cases = lax.axis_size("slab"), lax.axis_size("case")
    depth, height, across, width = tokens.shape[1:]
    units = w_up.shape[1]
    lines = height * across
    per = lines // slabs
    count = depth * lines
    sizes = (depth, per, across, count)
    factor = 1.0 / math.sqrt(count * slabs * cases)
    gain_one, gain_two = gain_attn.reshape(1, width), gain_mlp.reshape(1, width)
    spans = slabs // 2
    rows = width // slabs
    parts = slabs if depth * per % 16 == 0 else 1

    def permute(array, flip_slab, flip_case):
        return lax.ppermute(array, BOTH, swap_pairs(slabs, cases, flip_slab, flip_case))

    def exchange(blocks):
        if parts == 1:
            return [lax.all_to_all(blocks[0], "slab", split_axis=0, concat_axis=0, tiled=True)]
        got = {j: permute(blocks[j], j, 0) for j in range(parts - 1, 0, -1)}
        return [blocks[0]] + [got[j] for j in range(1, parts)]

    proj_bf = shape_of((count, 3 * width), BF16)
    rows_bf = shape_of((count, width), BF16)
    *mine, hold_x = call(
        functools.partial(plane_kernel, sizes),
        [shape_of((count // parts, 3 * width), BF16)] * parts + [rows_bf],
        tokens.reshape(count, width),
        cotangent.reshape(count, width),
        gain_one,
        w_qkv,
        near=[False] * 4,
        scratch=[
            pltpu.VMEM((count, width), BF16),
            pltpu.VMEM((count, width), BF16),
            pltpu.VMEM((1, width), F32),
            pltpu.VMEM((width, 3 * width), BF16),
            pltpu.VMEM((count, 3 * width), BF16),
            pltpu.SemaphoreType.DMA((4,)),
        ],
    )
    w_up_mine, w_down_mine = call(
        functools.partial(prepare_kernel, slabs),
        [shape_of((width, units // 4), BF16), shape_of((units // 4, width), BF16)],
        w_up,
        w_down,
    )
    got = exchange(mine)
    shared, proj_z, mixed, residual, hold_z = call(
        functools.partial(lines_kernel, sizes, parts),
        [shape_of((count, 2 * width), BF16), proj_bf, rows_bf, rows_bf, rows_bf],
        *got,
        gain_one,
        gain_two,
        w_qkv,
        w_out,
        after=[w_up_mine],
    )
    shared_x, shared_y = permute(shared, 1, 0), permute(shared, 0, 2)
    grad_mixed, grad_residual = call(
        mlp_kernel,
        [rows_bf, shape_of((count, width), F32)],
        shared,
        residual,
        gain_two,
        w_out,
        w_up,
        w_down,
    )
    back, pack_z = call(
        functools.partial(lines_back_kernel, sizes, parts),
        [shape_of((count, 2 * width), BF16), shape_of((count, 6 * width), BF16)],
        proj_z,
        grad_mixed,
        grad_residual,
        mixed,
        hold_z,
        gain_one,
        w_qkv,
    )
    (back,) = call(
        copy_kernel, [shape_of((count, 2 * width), BF16)], back, after=[shared_x, shared_y]
    )
    shared_xy = permute(shared_x, 0, 2)
    back = lax.all_to_all(back, "slab", split_axis=0, concat_axis=0, tiled=True)
    pack_z_core = permute(pack_z, 0, 1)
    (pack_p,) = call(
        functools.partial(plane_grads_kernel, sizes, parts),
        [shape_of((count, 4 * width), BF16)],
        back,
        hold_x,
        gain_one,
        w_qkv,
        after=[shared_xy],
        scratch=[pltpu.VMEM((count, 3 * width), BF16)],
    )
    pack_p_core = permute(pack_p, 0, 1)
    (around,) = call(
        join_kernel,
        [shape_of((4 * count, 2 * width), BF16)],
        shared,
        shared_x,
        shared_y,
        shared_xy,
        after=[pack_p_core, pack_z_core],
    )
    radix = min(4, spans)
    shift = (slabs // radix).bit_length() - 1
    big = call(
        functools.partial(grads_mlp_kernel, factor, shift),
        [shape_of((spans // radix, rows, 2 * width), BF16)] * radix,
        around,
        permute(around, 0, 1),
        w_up_mine,
        w_down_mine,
        scratch=[pltpu.VMEM((units // 8, width), F32), pltpu.VMEM((width, units // 4), F32)],
    )
    early = big[0]
    small = call(
        functools.partial(grads_qkv_kernel, factor, width, slabs),
        [shape_of((spans, rows * (width // LANES), LANES), BF16)] * 4,
        pack_z,
        pack_z_core,
        pack_p,
        pack_p_core,
        scratch=[pltpu.VMEM((width, width), F32)],
    )
    ready = small[0]
    small = [small[0], permute(small[1], 1, 0), permute(small[2], 0, 2), permute(small[3], 1, 2)]
    grad_tokens, flag = call(
        functools.partial(plane_tokens_kernel, sizes, parts),
        [rows_bf, shape_of((8, LANES), F32)],
        back,
        pack_p,
        hold_x,
        gain_one,
        w_qkv,
        after=[ready, early],
    )

    def reduce_z(split):
        left = spans
        while True:
            radix = len(split)
            left //= radix
            shift = (left * 2).bit_length() - 1
            pieces = [split[0]] + [permute(split[j], j << shift, 0) for j in range(1, radix)]
            if left == 1:
                return pieces
            radix = min(4, left)
            split = fold((left // radix * 2).bit_length() - 1, radix, pieces)

    def gather(last):
        return [last] + [permute(last, 0, j) for j in range(1, 4)]

    big = reduce_z(big)
    small = reduce_z(fold(shift, radix, small, [flag]))
    big = gather(fold(0, 1, big, [small[0]])[0])
    full_up, full_down, full_two, w_rows = call(
        functools.partial(place_mlp_kernel, slabs, width, units),
        [
            shape_of((rows, units), F32),
            shape_of((units // slabs, width), F32),
            shape_of((1, rows), F32),
            shape_of((rows, 3 * width), BF16),
        ],
        *big,
        gain_two,
        w_up,
        w_qkv,
        near=[True] * 5 + [False] * 2,
        scratch=[
            pltpu.VMEM((4, rows, 2 * width), F32),
            pltpu.VMEM((rows, units), BF16),
            pltpu.SemaphoreType.DMA((2,)),
        ],
    )
    small = gather(fold(0, 1, small)[0])
    full_qkv, full_out, full_one = call(
        functools.partial(place_qkv_kernel, slabs, width),
        [shape_of((rows, 3 * width), F32), shape_of((rows, width), F32), shape_of((1, rows), F32)],
        *small,
        gain_one,
        w_rows,
    )
    return (
        grad_tokens.reshape(tokens.shape),
        full_qkv,
        full_out,
        full_up,
        full_down,
        full_one.reshape(rows),
        full_two.reshape(rows),
    )


def solution(mesh):
    grid = P("case", "slab", None, None, None)
    return jax.shard_map(
        body,
        mesh=mesh,
        in_specs=(grid, grid, P(), P(), P(), P(), P(), P()),
        out_specs=(
            grid,
            P("slab", None),
            P("slab", None),
            P("slab", None),
            P("slab", None),
            P("slab"),
            P("slab"),
        ),
        check_vma=False,
    )
```

```python
import functools
import math

import jax
import jax.numpy as jnp
from jax import lax
from jax.experimental import pallas as pl
from jax.experimental.pallas import tpu as pltpu
from jax.sharding import PartitionSpec as P

HEADS = 8
LANES = 128
EPSILON = 1e-06
ROOT_TWO_PI = math.sqrt(2.0 / math.pi)
F32 = jnp.float32
BF16 = jnp.bfloat16
BOTH = ("slab", "case")
VMEM_BYTES = 24 * 1024 * 1024


def dot(a, b):
    return lax.dot_general(a, b, (((1,), (0,)), ((), ())), preferred_element_type=F32)


def dot_nt(a, b):
    return lax.dot_general(a, b, (((1,), (1,)), ((), ())), preferred_element_type=F32)


def dot_tn(a, b):
    return lax.dot_general(a, b, (((0,), (0,)), ((), ())), preferred_element_type=F32)


def norm_stats(values):
    inverse = lax.rsqrt(jnp.mean(values * values, axis=-1, keepdims=True) + EPSILON)
    return values * inverse, inverse


def norm_back(scaled, normed, inverse):
    return inverse * (scaled - normed * jnp.mean(scaled * normed, axis=-1, keepdims=True))


def call(kernel, outs, *args, after=(), scratch=(), near=None, flops=10**7):
    count = len(args)
    near = [True] * count if near is None else near

    def run(*refs):
        kernel(*refs[:count], *refs[count + len(after) :])

    vmem, far = pl.BlockSpec(memory_space=pltpu.VMEM), pl.BlockSpec(memory_space=pltpu.HBM)
    return pl.pallas_call(
        run,
        out_shape=outs,
        in_specs=[vmem if one else far for one in near] + [pl.BlockSpec(memory_space=pl.ANY)] * len(after),
        out_specs=[vmem] * len(outs),
        scratch_shapes=list(scratch),
        cost_estimate=pl.CostEstimate(flops=flops, transcendentals=0, bytes_accessed=10**4),
        compiler_params=pltpu.CompilerParams(vmem_limit_bytes=VMEM_BYTES),
    )(
        *[
            arg if one else pltpu.with_memory_space_constraint(arg, pltpu.HBM)
            for arg, one in zip(args, near)
        ],
        *after,
    )


def shape_of(shape, dtype):
    return jax.ShapeDtypeStruct(shape, dtype)


def line_masks(sizes, kind):
    depth, per, across, count = sizes
    rows = lax.broadcasted_iota(jnp.int32, (2 * count, count), 0) & (count - 1)
    cols = lax.broadcasted_iota(jnp.int32, (2 * count, count), 1)

    def parts(t):
        chunk = t // (depth * per)
        plane = (t // per) & (depth - 1)
        spot = chunk * per + (t & (per - 1))
        return plane, spot // across, spot & (across - 1), t & (per - 1)

    a, b = parts(rows), parts(cols)
    if kind == "z":
        return [a[3] == b[3]]
    same = a[0] == b[0]
    return [same & (a[1] == b[1]), same & (a[2] == b[2])]


def softmax_in(scores, mask):
    held = jnp.where(mask, scores, -1e30)
    weights = jnp.exp(held - jnp.max(held, axis=-1, keepdims=True))
    return weights / jnp.sum(weights, axis=-1, keepdims=True)


def pair_parts(proj, pair, width):
    at = pair * LANES
    return [proj[:, which * width + at : which * width + at + LANES] for which in range(3)]


def halves():
    lane = lax.broadcasted_iota(jnp.int32, (1, LANES), 1)
    low = (lane < LANES // 2).astype(F32)
    return low.astype(BF16), (1.0 - low).astype(BF16)


def stack(block, low, high):
    return jnp.concatenate([block * low, block * high], axis=0)


def side(block):
    count = block.shape[0] // 2
    return jnp.concatenate([block[:count], block[count:]], axis=1)


def attend(proj, masks, width):
    low, high = halves()
    scale = (width // HEADS) ** (-0.5)
    outs = []
    for pair in range(HEADS // 2):
        q2, k2, v2 = pair_parts(proj, pair, width)
        scores = dot_nt(stack(q2, low, high), k2) * scale
        probs = sum(softmax_in(scores, mask).astype(BF16).astype(F32) for mask in masks)
        outs.append(dot(side(probs.astype(BF16)), stack(v2, low, high)))
    return jnp.concatenate(outs, axis=1)


def attend_back(proj, grad, masks, width, out_ref, at):
    low, high = halves()
    scale = (width // HEADS) ** (-0.5)
    for pair in range(HEADS // 2):
        q2, k2, v2 = pair_parts(proj, pair, width)
        g2 = grad[:, pair * LANES : (pair + 1) * LANES]
        qs, gs = stack(q2, low, high), stack(g2, low, high)
        scores = dot_nt(qs, k2) * scale
        grad_probs = dot_nt(gs, v2)
        probs = jnp.zeros_like(scores)
        grad_scores = jnp.zeros_like(scores)
        for mask in masks:
            one = softmax_in(scores, mask)
            probs += one.astype(BF16).astype(F32)
            grad_scores += one * (grad_probs - jnp.sum(one * grad_probs, axis=-1, keepdims=True))
        probs, grad_scores = probs.astype(BF16), grad_scores.astype(BF16)
        found = (
            dot(side(grad_scores), stack(k2, low, high)) * scale,
            dot_tn(grad_scores, qs) * scale,
            dot_tn(probs, gs),
        )
        for which in range(3):
            start = at + which * width + pair * LANES
            out_ref[0 : q2.shape[0], start : start + LANES] = found[which].astype(BF16)


def chunk_order(sizes, parts):
    depth, per, _, count = sizes
    rows = lax.broadcasted_iota(jnp.int32, (count, count), 0)
    cols = lax.broadcasted_iota(jnp.int32, (count, count), 1)
    chunk = rows // (depth * per)
    if parts > 1:
        chunk = chunk ^ lax.axis_index("slab")
    plane = (rows // per) & (depth - 1)
    return plane * (count // depth) + chunk * per + (rows & (per - 1)) == cols


def put_parts(refs, at, value):
    rows = refs[0].shape[0]
    for j, ref in enumerate(refs):
        ref[:, at : at + value.shape[1]] = value[j * rows : (j + 1) * rows]


def joined(refs, start, stop):
    return jnp.concatenate([ref[:, start:stop] for ref in refs], axis=0)


def plane_kernel(sizes, x_ref, cot_ref, gain_ref, w_ref, *refs):
    parts, hold_x = refs[:-7], refs[-7]
    x_in, cot_in, gain_in, w_in, proj, sems = refs[-6:]
    copies = [
        pltpu.make_async_copy(src, dst, sems.at[i])
        for i, (src, dst) in enumerate(
            ((x_ref, x_in), (gain_ref, gain_in), (w_ref, w_in), (cot_ref, cot_in))
        )
    ]
    for copy in copies:
        copy.start()
    width = w_in.shape[0]
    order = chunk_order(sizes, len(parts)).astype(F32).astype(BF16)
    masks = line_masks(sizes, "xy")
    copies[0].wait()
    x = dot(order, x_in[...])
    hold_x[...] = x.astype(BF16)
    put_parts(parts, 0, hold_x[...])
    copies[1].wait()
    normed, _ = norm_stats(x)
    hidden = (normed * gain_in[...]).astype(BF16)
    copies[2].wait()
    proj[...] = dot(hidden, w_in[...]).astype(BF16)
    put_parts(parts, 2 * width, attend(proj[...], masks, width).astype(BF16))
    copies[3].wait()
    put_parts(parts, width, dot(order, cot_in[...]).astype(BF16))


def prepare_kernel(slabs, w_up_ref, w_down_ref, up_ref, down_ref):
    quarter = lax.axis_index("case")
    units = w_up_ref.shape[1]
    fine = units // slabs // 4
    rows = lax.broadcasted_iota(jnp.int32, (8 * LANES, LANES), 0)
    cols = lax.broadcasted_iota(jnp.int32, (8 * LANES, LANES), 1)
    for flip in range(2):
        x = (lax.axis_index("slab") & 1) ^ flip
        wanted = ((cols // fine * 2 + x) * 4 + quarter) * fine + (cols & (fine - 1))
        pick = (rows == wanted).astype(F32).astype(BF16)
        start = flip * units // 8
        for group in range(units // 8 // LANES):
            up_ref[:, start + group * LANES : start + (group + 1) * LANES] = dot(
                w_up_ref[:, group * 8 * LANES : (group + 1) * 8 * LANES], pick
            ).astype(BF16)
        for z in range(slabs // 2):
            at = pl.multiple_of(((z * 2 + x) * 4 + quarter) * fine, 8)
            down_ref[start + z * fine : start + (z + 1) * fine, :] = w_down_ref[pl.ds(at, fine), :]


def lines_kernel(sizes, parts, *refs):
    got = refs[:parts]
    gain_one_ref, gain_two_ref, w_ref, w_out_ref = refs[parts : parts + 4]
    shared_ref, proj_ref, mixed_ref, residual_ref, hold_x = refs[parts + 4 :]
    width = w_ref.shape[0]
    hold_x[...] = joined(got, 0, width)
    x = hold_x[...].astype(F32)
    normed, _ = norm_stats(x)
    proj_ref[...] = dot((normed * gain_one_ref[...]).astype(BF16), w_ref[...]).astype(BF16)
    out_z = attend(proj_ref[...], line_masks(sizes, "z"), width).astype(BF16)
    mixed = (joined(got, 2 * width, 3 * width).astype(F32) + out_z.astype(F32)).astype(BF16)
    residual = (x + dot(mixed, w_out_ref[...])).astype(BF16)
    normed_two, _ = norm_stats(residual.astype(F32))
    shared_ref[:, :width] = (normed_two * gain_two_ref[...]).astype(BF16)
    shared_ref[:, width:] = joined(got, width, 2 * width)
    mixed_ref[...] = mixed
    residual_ref[...] = residual


def gelu_parts(upper):
    square = upper * upper
    tangent = jnp.tanh(ROOT_TWO_PI * (upper + 0.044715 * upper * square))
    half = 0.5 * (1.0 + tangent)
    slope = half + 0.5 * upper * (1.0 - tangent * tangent) * ROOT_TWO_PI * (
        1.0 + 3.0 * 0.044715 * square
    )
    return (upper * half).astype(BF16), slope


def mlp_kernel(
    shared_ref, residual_ref, gain_ref, w_out_ref, w_up_ref, w_down_ref, grad_ref, gres_ref
):
    width, units = w_up_ref.shape
    hidden, cot = shared_ref[:, :width], shared_ref[:, width:]
    normed, inverse = norm_stats(residual_ref[...].astype(F32))
    step = min(512, units)
    grad_hidden = jnp.zeros(normed.shape, F32)
    for at in range(0, units, step):
        _, slope = gelu_parts(dot(hidden, w_up_ref[:, at : at + step]))
        grad_upper = (dot_nt(cot, w_down_ref[at : at + step, :]) * slope).astype(BF16)
        grad_hidden += dot_nt(grad_upper, w_up_ref[:, at : at + step])
    grad_residual = cot.astype(F32) + norm_back(grad_hidden * gain_ref[...], normed, inverse)
    gres_ref[...] = grad_residual
    grad_ref[...] = dot_nt(grad_residual.astype(BF16), w_out_ref[...]).astype(BF16)


def lines_back_kernel(
    sizes, parts, proj_ref, grad_ref, gres_ref, mixed_ref, x_ref, gain_ref, w_ref, back_ref, pack_ref
):
    width = w_ref.shape[0]
    pack_ref[:, 4 * width : 5 * width] = mixed_ref[...]
    pack_ref[:, 5 * width :] = gres_ref[...].astype(BF16)
    attend_back(proj_ref[...], grad_ref[...], line_masks(sizes, "z"), width, pack_ref, width)
    normed, inverse = norm_stats(x_ref[...].astype(F32))
    pack_ref[:, :width] = (normed * gain_ref[...]).astype(BF16)
    grad_hidden = dot_nt(pack_ref[:, width : 4 * width], w_ref[...])
    back = norm_back(grad_hidden * gain_ref[...], normed, inverse)
    part = (gres_ref[...] + back).astype(BF16)
    for j, (spot, size) in enumerate(blocks_of(part.shape[0], parts)):
        back_ref[pl.ds(spot, size), :width] = grad_ref[j * size : (j + 1) * size, :]
        back_ref[pl.ds(spot, size), width:] = part[j * size : (j + 1) * size]


def blocks_of(count, parts):
    size = count // parts
    if parts == 1:
        return [(0, size)]
    me = lax.axis_index("slab")
    return [(pl.multiple_of((me ^ j) * size, 16), size) for j in range(parts)]


def partner_order(ref, parts, start, stop):
    return jnp.concatenate(
        [ref[pl.ds(spot, size), start:stop] for spot, size in blocks_of(ref.shape[0], parts)], axis=0
    )


def copy_kernel(in_ref, out_ref):
    out_ref[...] = in_ref[...]


def join_kernel(*refs):
    out_ref = refs[-1]
    rows = refs[0].shape[0]
    for j, ref in enumerate(refs[:-1]):
        out_ref[j * rows : (j + 1) * rows, :] = ref[...]


def plane_grads_kernel(sizes, parts, *refs):
    back_ref, x_ref, gain_ref, w_ref, pack_ref, proj = refs
    width = w_ref.shape[0]
    normed, _ = norm_stats(x_ref[...].astype(F32))
    pack_ref[:, :width] = (normed * gain_ref[...]).astype(BF16)
    proj[...] = dot(pack_ref[:, :width], w_ref[...]).astype(BF16)
    grad = partner_order(back_ref, parts, 0, width)
    attend_back(proj[...], grad, line_masks(sizes, "xy"), width, pack_ref, width)


def plane_tokens_kernel(sizes, parts, *refs):
    back_ref, pack_ref, x_ref, gain_ref, w_ref, grad_ref, flag_ref = refs
    flag_ref[...] = jnp.zeros_like(flag_ref)
    width = w_ref.shape[0]
    normed, inverse = norm_stats(x_ref[...].astype(F32))
    grad_hidden = dot_nt(pack_ref[:, width:], w_ref[...])
    back = norm_back(grad_hidden * gain_ref[...], normed, inverse)
    part = partner_order(back_ref, parts, width, 2 * width).astype(F32)
    order = chunk_order(sizes, parts).astype(F32).astype(BF16)
    grad_ref[...] = dot_tn(order, (back + part).astype(BF16)).astype(BF16)


def place():
    slab, case = lax.axis_index("slab"), lax.axis_index("case")
    return slab & 1, case >> 1, case & 1, slab >> 1


def store_units(scratch, rows, units, x, flip, outs, at):
    blocks = outs[0].shape[0]
    for z in range(blocks):
        start = pl.multiple_of((z * 2 + (x ^ flip)) * rows, 8)
        block = scratch[pl.ds(start, rows), 0 : units * LANES].astype(BF16)
        for unit in range(units):
            outs[flip][z, at + unit * rows : at + (unit + 1) * rows, :] = block[
                :, unit * LANES : (unit + 1) * LANES
            ]


def grads_mlp_kernel(factor, shift, here_ref, there_ref, w_up_ref, w_down_ref, *refs):
    outs, down, up = refs[:-2], refs[-2], refs[-1]
    width, units = w_up_ref.shape
    slab = lax.axis_index("slab")
    digit = (slab >> shift) & (len(outs) - 1)
    hidden = jnp.concatenate([ref[:, :width] for ref in (here_ref, there_ref)], axis=0)
    cot = jnp.concatenate([ref[:, width:] for ref in (here_ref, there_ref)], axis=0)
    half = units // 2
    for at in (0, half):
        active, slope = gelu_parts(dot(hidden, w_up_ref[:, at : at + half]))
        grad_upper = (dot_nt(cot, w_down_ref[at : at + half, :]) * slope).astype(BF16)
        up[:, at : at + half] = dot_tn(hidden, grad_upper) * factor
        if at == 0:
            down[...] = dot_tn(active, cot) * factor
    rest, rows = outs[0].shape[:2]
    for j, out in enumerate(outs):
        for k in range(rest):
            z = (digit ^ j) * rest + k
            at = pl.ds(pl.multiple_of(z * rows, 8), rows)
            out[k, :, :width] = down[at, :].astype(BF16)
            at = pl.ds(pl.multiple_of((z * 2 + (slab & 1)) * rows, 8), rows)
            out[k, :, width:] = up[at, :].astype(BF16)


def grads_qkv_kernel(factor, width, slabs, za_ref, zb_ref, pa_ref, pb_ref, *refs):
    outs, scratch = refs[:4], refs[4]
    x, y, core, _ = place()
    size, narrow = 3 * width // 4, width // 4
    rows = width // slabs
    hidden = jnp.concatenate([r[:, :width] for r in (za_ref, zb_ref, pa_ref, pb_ref)], axis=0)
    mixed = jnp.concatenate([r[:, 4 * width : 5 * width] for r in (za_ref, zb_ref)], axis=0)
    for flip_y in range(2):
        quarter = (y ^ flip_y) * 2 + core
        at = pl.multiple_of(width + quarter * size, LANES)
        cols = jnp.concatenate(
            [r[:, pl.ds(at, size)] for r in (za_ref, zb_ref, pa_ref, pb_ref)], axis=0
        )
        scratch[:, :size] = dot_tn(hidden, cols) * factor
        at = pl.multiple_of(5 * width + quarter * narrow, LANES)
        cols = jnp.concatenate([r[:, pl.ds(at, narrow)] for r in (za_ref, zb_ref)], axis=0)
        scratch[:, size:] = dot_tn(mixed, cols) * factor
        for flip in range(2):
            store_units(scratch, rows, width // LANES, x, flip, outs[2 * flip_y : 2 * flip_y + 2], 0)


def fold_kernel(shift, radix, count, *refs):
    ins, outs = refs[:count], refs[count:]
    digit = (lax.axis_index("slab") >> shift) & (radix - 1)
    rest = ins[0].shape[0] // radix
    for j in range(radix):
        for k in range(rest):
            at = (digit ^ j) * rest + k
            total = ins[0][at].astype(F32)
            for ref in ins[1:]:
                total += ref[at].astype(F32)
            outs[j][k] = total.astype(BF16)


def fold(shift, radix, pieces, after=()):
    first = pieces[0].shape
    outs = [shape_of((first[0] // radix,) + first[1:], BF16)] * radix
    kernel = functools.partial(fold_kernel, shift, radix, len(pieces))
    return call(kernel, outs, *pieces, after=after)


def swap_pairs(slabs, cases, flip_slab, flip_case):
    return [
        (s * cases + c, (s ^ flip_slab) * cases + (c ^ flip_case))
        for s in range(slabs)
        for c in range(cases)
    ]


def gain_sums(grad, w_rows, gain_ref):
    rows, width = grad.shape[0], gain_ref.shape[1]
    spot = lax.axis_index("slab") * rows + lax.broadcasted_iota(jnp.int32, (rows, width), 0)
    lanes = lax.broadcasted_iota(jnp.int32, (rows, width), 1)
    gain = jnp.sum(jnp.where(lanes == spot, gain_ref[...], 0.0), axis=1, keepdims=True)
    total = jnp.sum(grad * w_rows.astype(F32), axis=1, keepdims=True) / gain
    return jnp.transpose(jnp.broadcast_to(total, (rows, LANES)))[0:1, :]


def place_mlp_kernel(slabs, width, units, *refs):
    pieces, (gain_ref, w_up_ref, w_ref) = refs[:4], refs[4:7]
    up, down, two, w_rows, held, up_rows, sems = refs[7:]
    rows = width // slabs
    here = pl.ds(pl.multiple_of(lax.axis_index("slab") * rows, 8), rows)
    copies = [
        pltpu.make_async_copy(w_up_ref.at[here], up_rows, sems.at[0]),
        pltpu.make_async_copy(w_ref.at[here], w_rows, sems.at[1]),
    ]
    for copy in copies:
        copy.start()
    case, x = lax.axis_index("case"), lax.axis_index("slab") & 1
    eighth, fine = units // 8, units // 4 // slabs
    for j in range(4):
        piece = pieces[j][0].astype(F32)
        held[case ^ j, :, :width] = piece[:, :width]
        for flip in range(2):
            at = pl.multiple_of(width + (x ^ flip) * eighth, LANES)
            held[case ^ j, :, pl.ds(at, eighth)] = piece[
                :, width + flip * eighth : width + (flip + 1) * eighth
            ]
    for quarter in range(4):
        down[quarter * rows : (quarter + 1) * rows, :] = held[quarter, :, :width]
    for block in range(slabs):
        up[:, block * 4 * fine : (block + 1) * 4 * fine] = jnp.concatenate(
            [
                held[quarter, :, pl.ds(width + block % 2 * eighth + block // 2 * fine, fine)]
                for quarter in range(4)
            ],
            axis=1,
        )
    for copy in copies:
        copy.wait()
    two[...] = gain_sums(up[...], up_rows[...], gain_ref)


def place_qkv_kernel(slabs, width, *refs):
    pieces, (gain_ref, w_rows), (qkv, out, one) = refs[:4], refs[4:6], refs[6:]
    case = lax.axis_index("case")
    rows = width // slabs
    size = 3 * width // 4
    for j in range(4):
        quarter = case ^ j
        for unit in range(width // LANES):
            piece = pieces[j][0, unit * rows : (unit + 1) * rows, :].astype(F32)
            if unit < size // LANES:
                start = pl.multiple_of(quarter * size + unit * LANES, LANES)
                qkv[:, pl.ds(start, LANES)] = piece
            else:
                start = pl.multiple_of(quarter * (width // 4) + unit * LANES - size, LANES)
                out[:, pl.ds(start, LANES)] = piece
    one[...] = gain_sums(qkv[...], w_rows[...], gain_ref)


def body(tokens, cotangent, w_qkv, w_out, w_up, w_down, gain_attn, gain_mlp):
    slabs, cases = lax.axis_size("slab"), lax.axis_size("case")
    depth, height, across, width = tokens.shape[1:]
    units = w_up.shape[1]
    lines = height * across
    per = lines // slabs
    count = depth * lines
    sizes = (depth, per, across, count)
    factor = 1.0 / math.sqrt(count * slabs * cases)
    gain_one, gain_two = gain_attn.reshape(1, width), gain_mlp.reshape(1, width)
    spans = slabs // 2
    rows = width // slabs
    parts = slabs if depth * per % 16 == 0 else 1

    def permute(array, flip_slab, flip_case):
        return lax.ppermute(array, BOTH, swap_pairs(slabs, cases, flip_slab, flip_case))

    def exchange(blocks):
        if parts == 1:
            return [lax.all_to_all(blocks[0], "slab", split_axis=0, concat_axis=0, tiled=True)]
        got = {j: permute(blocks[j], j, 0) for j in range(parts - 1, 0, -1)}
        return [blocks[0]] + [got[j] for j in range(1, parts)]

    proj_bf = shape_of((count, 3 * width), BF16)
    rows_bf = shape_of((count, width), BF16)
    *mine, hold_x = call(
        functools.partial(plane_kernel, sizes),
        [shape_of((count // parts, 3 * width), BF16)] * parts + [rows_bf],
        tokens.reshape(count, width),
        cotangent.reshape(count, width),
        gain_one,
        w_qkv,
        near=[False] * 4,
        scratch=[
            pltpu.VMEM((count, width), BF16),
            pltpu.VMEM((count, width), BF16),
            pltpu.VMEM((1, width), F32),
            pltpu.VMEM((width, 3 * width), BF16),
            pltpu.VMEM((count, 3 * width), BF16),
            pltpu.SemaphoreType.DMA((4,)),
        ],
    )
    w_up_mine, w_down_mine = call(
        functools.partial(prepare_kernel, slabs),
        [shape_of((width, units // 4), BF16), shape_of((units // 4, width), BF16)],
        w_up,
        w_down,
    )
    got = exchange(mine)
    shared, proj_z, mixed, residual, hold_z = call(
        functools.partial(lines_kernel, sizes, parts),
        [shape_of((count, 2 * width), BF16), proj_bf, rows_bf, rows_bf, rows_bf],
        *got,
        gain_one,
        gain_two,
        w_qkv,
        w_out,
        after=[w_up_mine],
    )
    shared_x, shared_y = permute(shared, 1, 0), permute(shared, 0, 2)
    grad_mixed, grad_residual = call(
        mlp_kernel,
        [rows_bf, shape_of((count, width), F32)],
        shared,
        residual,
        gain_two,
        w_out,
        w_up,
        w_down,
    )
    back, pack_z = call(
        functools.partial(lines_back_kernel, sizes, parts),
        [shape_of((count, 2 * width), BF16), shape_of((count, 6 * width), BF16)],
        proj_z,
        grad_mixed,
        grad_residual,
        mixed,
        hold_z,
        gain_one,
        w_qkv,
    )
    (back,) = call(
        copy_kernel, [shape_of((count, 2 * width), BF16)], back, after=[shared_x, shared_y]
    )
    back = lax.all_to_all(back, "slab", split_axis=0, concat_axis=0, tiled=True)
    pack_z_core = permute(pack_z, 0, 1)
    (pack_p,) = call(
        functools.partial(plane_grads_kernel, sizes, parts),
        [shape_of((count, 4 * width), BF16)],
        back,
        hold_x,
        gain_one,
        w_qkv,
        scratch=[pltpu.VMEM((count, 3 * width), BF16)],
    )
    (around,) = call(
        join_kernel,
        [shape_of((4 * count, 2 * width), BF16)],
        shared,
        shared_x,
        shared_y,
        permute(shared_x, 0, 2),
        after=[pack_p],
    )
    radix = min(4, spans)
    shift = (slabs // radix).bit_length() - 1
    big = call(
        functools.partial(grads_mlp_kernel, factor, shift),
        [shape_of((spans // radix, rows, 2 * width), BF16)] * radix,
        around,
        permute(around, 0, 1),
        w_up_mine,
        w_down_mine,
        scratch=[pltpu.VMEM((units // 8, width), F32), pltpu.VMEM((width, units // 4), F32)],
    )
    early = big[0]
    small = call(
        functools.partial(grads_qkv_kernel, factor, width, slabs),
        [shape_of((spans, rows * (width // LANES), LANES), BF16)] * 4,
        pack_z,
        pack_z_core,
        pack_p,
        permute(pack_p, 0, 1),
        scratch=[pltpu.VMEM((width, width), F32)],
    )
    ready = small[0]
    small = [small[0], permute(small[1], 1, 0), permute(small[2], 0, 2), permute(small[3], 1, 2)]
    grad_tokens, flag = call(
        functools.partial(plane_tokens_kernel, sizes, parts),
        [rows_bf, shape_of((8, LANES), F32)],
        back,
        pack_p,
        hold_x,
        gain_one,
        w_qkv,
        after=[ready, early],
    )

    def reduce_z(split):
        left = spans
        while True:
            radix = len(split)
            left //= radix
            shift = (left * 2).bit_length() - 1
            pieces = [split[0]] + [permute(split[j], j << shift, 0) for j in range(1, radix)]
            if left == 1:
                return pieces
            radix = min(4, left)
            split = fold((left // radix * 2).bit_length() - 1, radix, pieces)

    def gather(last, relay=False):
        other = permute(last, 0, 2)
        both = permute(other, 0, 1) if relay else permute(last, 0, 3)
        return [last, permute(last, 0, 1), other, both]

    big = reduce_z(big)
    small = reduce_z(fold(shift, radix, small, [flag]))
    big = gather(fold(0, 1, big, [small[0]])[0], True)
    full_up, full_down, full_two, w_rows = call(
        functools.partial(place_mlp_kernel, slabs, width, units),
        [
            shape_of((rows, units), F32),
            shape_of((units // slabs, width), F32),
            shape_of((1, rows), F32),
            shape_of((rows, 3 * width), BF16),
        ],
        *big,
        gain_two,
        w_up,
        w_qkv,
        near=[True] * 5 + [False] * 2,
        scratch=[
            pltpu.VMEM((4, rows, 2 * width), F32),
            pltpu.VMEM((rows, units), BF16),
            pltpu.SemaphoreType.DMA((2,)),
        ],
    )
    small = gather(fold(0, 1, small)[0])
    full_qkv, full_out, full_one = call(
        functools.partial(place_qkv_kernel, slabs, width),
        [shape_of((rows, 3 * width), F32), shape_of((rows, width), F32), shape_of((1, rows), F32)],
        *small,
        gain_one,
        w_rows,
    )
    return (
        grad_tokens.reshape(tokens.shape),
        full_qkv,
        full_out,
        full_up,
        full_down,
        full_one.reshape(rows),
        full_two.reshape(rows),
    )


def solution(mesh):
    grid = P("case", "slab", None, None, None)
    return jax.shard_map(
        body,
        mesh=mesh,
        in_specs=(grid, grid, P(), P(), P(), P(), P(), P()),
        out_specs=(
            grid,
            P("slab", None),
            P("slab", None),
            P("slab", None),
            P("slab", None),
            P("slab"),
            P("slab"),
        ),
        check_vma=False,
    )
```

```python
import functools
import math

import jax
import jax.numpy as jnp
from jax import lax
from jax.experimental import pallas as pl
from jax.experimental.pallas import tpu as pltpu
from jax.sharding import PartitionSpec as P

HEADS = 8
LANES = 128
EPSILON = 1e-06
ROOT_TWO_PI = math.sqrt(2.0 / math.pi)
F32 = jnp.float32
BF16 = jnp.bfloat16
BOTH = ("slab", "case")
VMEM_BYTES = 24 * 1024 * 1024


def dot(a, b):
    return lax.dot_general(a, b, (((1,), (0,)), ((), ())), preferred_element_type=F32)


def dot_nt(a, b):
    return lax.dot_general(a, b, (((1,), (1,)), ((), ())), preferred_element_type=F32)


def dot_tn(a, b):
    return lax.dot_general(a, b, (((0,), (0,)), ((), ())), preferred_element_type=F32)


def norm_stats(values):
    inverse = lax.rsqrt(jnp.mean(values * values, axis=-1, keepdims=True) + EPSILON)
    return values * inverse, inverse


def norm_back(scaled, normed, inverse):
    return inverse * (scaled - normed * jnp.mean(scaled * normed, axis=-1, keepdims=True))


def call(kernel, outs, *args, after=(), scratch=(), near=None, flops=10**7):
    count = len(args)
    near = [True] * count if near is None else near

    def run(*refs):
        kernel(*refs[:count], *refs[count + len(after) :])

    vmem, far = pl.BlockSpec(memory_space=pltpu.VMEM), pl.BlockSpec(memory_space=pltpu.HBM)
    return pl.pallas_call(
        run,
        out_shape=outs,
        in_specs=[vmem if one else far for one in near] + [pl.BlockSpec(memory_space=pl.ANY)] * len(after),
        out_specs=[vmem] * len(outs),
        scratch_shapes=list(scratch),
        cost_estimate=pl.CostEstimate(flops=flops, transcendentals=0, bytes_accessed=10**4),
        compiler_params=pltpu.CompilerParams(vmem_limit_bytes=VMEM_BYTES),
    )(
        *[
            arg if one else pltpu.with_memory_space_constraint(arg, pltpu.HBM)
            for arg, one in zip(args, near)
        ],
        *after,
    )


def shape_of(shape, dtype):
    return jax.ShapeDtypeStruct(shape, dtype)


def line_masks(sizes, kind):
    depth, per, across, count = sizes
    rows = lax.broadcasted_iota(jnp.int32, (2 * count, count), 0) & (count - 1)
    cols = lax.broadcasted_iota(jnp.int32, (2 * count, count), 1)

    def parts(t):
        chunk = t // (depth * per)
        plane = (t // per) & (depth - 1)
        spot = chunk * per + (t & (per - 1))
        return plane, spot // across, spot & (across - 1), t & (per - 1)

    a, b = parts(rows), parts(cols)
    if kind == "z":
        return [a[3] == b[3]]
    same = a[0] == b[0]
    return [same & (a[1] == b[1]), same & (a[2] == b[2])]


def softmax_in(scores, mask):
    held = jnp.where(mask, scores, -1e30)
    weights = jnp.exp(held - jnp.max(held, axis=-1, keepdims=True))
    return weights / jnp.sum(weights, axis=-1, keepdims=True)


def pair_parts(proj, pair, width):
    at = pair * LANES
    return [proj[:, which * width + at : which * width + at + LANES] for which in range(3)]


def halves():
    lane = lax.broadcasted_iota(jnp.int32, (1, LANES), 1)
    low = (lane < LANES // 2).astype(F32)
    return low.astype(BF16), (1.0 - low).astype(BF16)


def stack(block, low, high):
    return jnp.concatenate([block * low, block * high], axis=0)


def side(block):
    count = block.shape[0] // 2
    return jnp.concatenate([block[:count], block[count:]], axis=1)


def attend(proj, masks, width):
    low, high = halves()
    scale = (width // HEADS) ** (-0.5)
    outs = []
    for pair in range(HEADS // 2):
        q2, k2, v2 = pair_parts(proj, pair, width)
        scores = dot_nt(stack(q2, low, high), k2) * scale
        probs = sum(softmax_in(scores, mask).astype(BF16).astype(F32) for mask in masks)
        outs.append(dot(side(probs.astype(BF16)), stack(v2, low, high)))
    return jnp.concatenate(outs, axis=1)


def attend_back(proj, grad, masks, width, out_ref, at):
    low, high = halves()
    scale = (width // HEADS) ** (-0.5)
    for pair in range(HEADS // 2):
        q2, k2, v2 = pair_parts(proj, pair, width)
        g2 = grad[:, pair * LANES : (pair + 1) * LANES]
        qs, gs = stack(q2, low, high), stack(g2, low, high)
        scores = dot_nt(qs, k2) * scale
        grad_probs = dot_nt(gs, v2)
        probs = jnp.zeros_like(scores)
        grad_scores = jnp.zeros_like(scores)
        for mask in masks:
            one = softmax_in(scores, mask)
            probs += one.astype(BF16).astype(F32)
            grad_scores += one * (grad_probs - jnp.sum(one * grad_probs, axis=-1, keepdims=True))
        probs, grad_scores = probs.astype(BF16), grad_scores.astype(BF16)
        found = (
            dot(side(grad_scores), stack(k2, low, high)) * scale,
            dot_tn(grad_scores, qs) * scale,
            dot_tn(probs, gs),
        )
        for which in range(3):
            start = at + which * width + pair * LANES
            out_ref[0 : q2.shape[0], start : start + LANES] = found[which].astype(BF16)


def chunk_order(sizes, parts):
    depth, per, _, count = sizes
    rows = lax.broadcasted_iota(jnp.int32, (count, count), 0)
    cols = lax.broadcasted_iota(jnp.int32, (count, count), 1)
    chunk = rows // (depth * per)
    if parts > 1:
        chunk = chunk ^ lax.axis_index("slab")
    plane = (rows // per) & (depth - 1)
    return plane * (count // depth) + chunk * per + (rows & (per - 1)) == cols


def put_parts(refs, at, value):
    rows = refs[0].shape[0]
    for j, ref in enumerate(refs):
        ref[:, at : at + value.shape[1]] = value[j * rows : (j + 1) * rows]


def joined(refs, start, stop):
    return jnp.concatenate([ref[:, start:stop] for ref in refs], axis=0)


def plane_kernel(sizes, x_ref, cot_ref, gain_ref, w_ref, *refs):
    parts, hold_x = refs[:-7], refs[-7]
    x_in, cot_in, gain_in, w_in, proj, sems = refs[-6:]
    copies = [
        pltpu.make_async_copy(src, dst, sems.at[i])
        for i, (src, dst) in enumerate(
            ((x_ref, x_in), (gain_ref, gain_in), (w_ref, w_in), (cot_ref, cot_in))
        )
    ]
    for copy in copies:
        copy.start()
    width = w_in.shape[0]
    order = chunk_order(sizes, len(parts)).astype(F32).astype(BF16)
    masks = line_masks(sizes, "xy")
    copies[0].wait()
    x = dot(order, x_in[...])
    hold_x[...] = x.astype(BF16)
    put_parts(parts, 0, hold_x[...])
    copies[1].wait()
    normed, _ = norm_stats(x)
    hidden = (normed * gain_in[...]).astype(BF16)
    copies[2].wait()
    proj[...] = dot(hidden, w_in[...]).astype(BF16)
    put_parts(parts, 2 * width, attend(proj[...], masks, width).astype(BF16))
    copies[3].wait()
    put_parts(parts, width, dot(order, cot_in[...]).astype(BF16))


def prepare_kernel(slabs, w_up_ref, w_down_ref, up_ref, down_ref):
    quarter = lax.axis_index("case")
    units = w_up_ref.shape[1]
    fine = units // slabs // 4
    rows = lax.broadcasted_iota(jnp.int32, (8 * LANES, LANES), 0)
    cols = lax.broadcasted_iota(jnp.int32, (8 * LANES, LANES), 1)
    for flip in range(2):
        x = (lax.axis_index("slab") & 1) ^ flip
        wanted = ((cols // fine * 2 + x) * 4 + quarter) * fine + (cols & (fine - 1))
        pick = (rows == wanted).astype(F32).astype(BF16)
        start = flip * units // 8
        for group in range(units // 8 // LANES):
            up_ref[:, start + group * LANES : start + (group + 1) * LANES] = dot(
                w_up_ref[:, group * 8 * LANES : (group + 1) * 8 * LANES], pick
            ).astype(BF16)
        for z in range(slabs // 2):
            at = pl.multiple_of(((z * 2 + x) * 4 + quarter) * fine, 8)
            down_ref[start + z * fine : start + (z + 1) * fine, :] = w_down_ref[pl.ds(at, fine), :]


def lines_kernel(sizes, parts, *refs):
    got = refs[:parts]
    gain_one_ref, gain_two_ref, w_ref, w_out_ref = refs[parts : parts + 4]
    shared_ref, proj_ref, mixed_ref, residual_ref, hold_x = refs[parts + 4 :]
    width = w_ref.shape[0]
    hold_x[...] = joined(got, 0, width)
    x = hold_x[...].astype(F32)
    normed, _ = norm_stats(x)
    proj_ref[...] = dot((normed * gain_one_ref[...]).astype(BF16), w_ref[...]).astype(BF16)
    out_z = attend(proj_ref[...], line_masks(sizes, "z"), width).astype(BF16)
    mixed = (joined(got, 2 * width, 3 * width).astype(F32) + out_z.astype(F32)).astype(BF16)
    residual = (x + dot(mixed, w_out_ref[...])).astype(BF16)
    normed_two, _ = norm_stats(residual.astype(F32))
    shared_ref[:, :width] = (normed_two * gain_two_ref[...]).astype(BF16)
    shared_ref[:, width:] = joined(got, width, 2 * width)
    mixed_ref[...] = mixed
    residual_ref[...] = residual


def gelu_parts(upper):
    square = upper * upper
    tangent = jnp.tanh(ROOT_TWO_PI * (upper + 0.044715 * upper * square))
    half = 0.5 * (1.0 + tangent)
    slope = half + 0.5 * upper * (1.0 - tangent * tangent) * ROOT_TWO_PI * (
        1.0 + 3.0 * 0.044715 * square
    )
    return (upper * half).astype(BF16), slope


def mlp_kernel(
    shared_ref, residual_ref, gain_ref, w_out_ref, w_up_ref, w_down_ref, grad_ref, gres_ref
):
    width, units = w_up_ref.shape
    hidden, cot = shared_ref[:, :width], shared_ref[:, width:]
    normed, inverse = norm_stats(residual_ref[...].astype(F32))
    step = min(512, units)
    grad_hidden = jnp.zeros(normed.shape, F32)
    for at in range(0, units, step):
        _, slope = gelu_parts(dot(hidden, w_up_ref[:, at : at + step]))
        grad_upper = (dot_nt(cot, w_down_ref[at : at + step, :]) * slope).astype(BF16)
        grad_hidden += dot_nt(grad_upper, w_up_ref[:, at : at + step])
    grad_residual = cot.astype(F32) + norm_back(grad_hidden * gain_ref[...], normed, inverse)
    gres_ref[...] = grad_residual
    grad_ref[...] = dot_nt(grad_residual.astype(BF16), w_out_ref[...]).astype(BF16)


def lines_back_kernel(
    sizes, parts, proj_ref, grad_ref, gres_ref, mixed_ref, x_ref, gain_ref, w_ref, back_ref, pack_ref
):
    width = w_ref.shape[0]
    pack_ref[:, 4 * width : 5 * width] = mixed_ref[...]
    pack_ref[:, 5 * width :] = gres_ref[...].astype(BF16)
    attend_back(proj_ref[...], grad_ref[...], line_masks(sizes, "z"), width, pack_ref, width)
    normed, inverse = norm_stats(x_ref[...].astype(F32))
    pack_ref[:, :width] = (normed * gain_ref[...]).astype(BF16)
    grad_hidden = dot_nt(pack_ref[:, width : 4 * width], w_ref[...])
    back = norm_back(grad_hidden * gain_ref[...], normed, inverse)
    part = (gres_ref[...] + back).astype(BF16)
    for j, (spot, size) in enumerate(blocks_of(part.shape[0], parts)):
        back_ref[pl.ds(spot, size), :width] = grad_ref[j * size : (j + 1) * size, :]
        back_ref[pl.ds(spot, size), width:] = part[j * size : (j + 1) * size]


def blocks_of(count, parts):
    size = count // parts
    if parts == 1:
        return [(0, size)]
    me = lax.axis_index("slab")
    return [(pl.multiple_of((me ^ j) * size, 16), size) for j in range(parts)]


def partner_order(ref, parts, start, stop):
    return jnp.concatenate(
        [ref[pl.ds(spot, size), start:stop] for spot, size in blocks_of(ref.shape[0], parts)], axis=0
    )


def copy_kernel(in_ref, out_ref):
    out_ref[...] = in_ref[...]


def join_kernel(*refs):
    out_ref = refs[-1]
    rows = refs[0].shape[0]
    for j, ref in enumerate(refs[:-1]):
        out_ref[j * rows : (j + 1) * rows, :] = ref[...]


def plane_grads_kernel(sizes, parts, *refs):
    back_ref, x_ref, gain_ref, w_ref, pack_ref, proj = refs
    width = w_ref.shape[0]
    normed, _ = norm_stats(x_ref[...].astype(F32))
    pack_ref[:, :width] = (normed * gain_ref[...]).astype(BF16)
    proj[...] = dot(pack_ref[:, :width], w_ref[...]).astype(BF16)
    grad = partner_order(back_ref, parts, 0, width)
    attend_back(proj[...], grad, line_masks(sizes, "xy"), width, pack_ref, width)


def plane_tokens_kernel(sizes, parts, *refs):
    back_ref, pack_ref, x_ref, gain_ref, w_ref, grad_ref, flag_ref = refs
    flag_ref[...] = jnp.zeros_like(flag_ref)
    width = w_ref.shape[0]
    normed, inverse = norm_stats(x_ref[...].astype(F32))
    grad_hidden = dot_nt(pack_ref[:, width:], w_ref[...])
    back = norm_back(grad_hidden * gain_ref[...], normed, inverse)
    part = partner_order(back_ref, parts, width, 2 * width).astype(F32)
    order = chunk_order(sizes, parts).astype(F32).astype(BF16)
    grad_ref[...] = dot_tn(order, (back + part).astype(BF16)).astype(BF16)


def place():
    slab, case = lax.axis_index("slab"), lax.axis_index("case")
    return slab & 1, case >> 1, case & 1, slab >> 1


def store_units(scratch, rows, units, x, flip, outs, at):
    blocks = outs[0].shape[0]
    for z in range(blocks):
        start = pl.multiple_of((z * 2 + (x ^ flip)) * rows, 8)
        block = scratch[pl.ds(start, rows), 0 : units * LANES].astype(BF16)
        for unit in range(units):
            outs[flip][z, at + unit * rows : at + (unit + 1) * rows, :] = block[
                :, unit * LANES : (unit + 1) * LANES
            ]


def grads_mlp_kernel(factor, shift, here_ref, there_ref, w_up_ref, w_down_ref, *refs):
    outs, down, up = refs[:-2], refs[-2], refs[-1]
    width, units = w_up_ref.shape
    slab = lax.axis_index("slab")
    digit = (slab >> shift) & (len(outs) - 1)
    hidden = jnp.concatenate([ref[:, :width] for ref in (here_ref, there_ref)], axis=0)
    cot = jnp.concatenate([ref[:, width:] for ref in (here_ref, there_ref)], axis=0)
    half = units // 2
    for at in (0, half):
        active, slope = gelu_parts(dot(hidden, w_up_ref[:, at : at + half]))
        grad_upper = (dot_nt(cot, w_down_ref[at : at + half, :]) * slope).astype(BF16)
        up[:, at : at + half] = dot_tn(hidden, grad_upper) * factor
        if at == 0:
            down[...] = dot_tn(active, cot) * factor
    rest, rows = outs[0].shape[:2]
    for j, out in enumerate(outs):
        for k in range(rest):
            z = (digit ^ j) * rest + k
            at = pl.ds(pl.multiple_of(z * rows, 8), rows)
            out[k, :, :width] = down[at, :].astype(BF16)
            at = pl.ds(pl.multiple_of((z * 2 + (slab & 1)) * rows, 8), rows)
            out[k, :, width:] = up[at, :].astype(BF16)


def grads_qkv_kernel(factor, width, slabs, za_ref, zb_ref, pa_ref, pb_ref, *refs):
    outs, scratch = refs[:4], refs[4]
    x, y, core, _ = place()
    size, narrow = 3 * width // 4, width // 4
    rows = width // slabs
    hidden = jnp.concatenate([r[:, :width] for r in (za_ref, zb_ref, pa_ref, pb_ref)], axis=0)
    mixed = jnp.concatenate([r[:, 4 * width : 5 * width] for r in (za_ref, zb_ref)], axis=0)
    for flip_y in range(2):
        quarter = (y ^ flip_y) * 2 + core
        at = pl.multiple_of(width + quarter * size, LANES)
        cols = jnp.concatenate(
            [r[:, pl.ds(at, size)] for r in (za_ref, zb_ref, pa_ref, pb_ref)], axis=0
        )
        scratch[:, :size] = dot_tn(hidden, cols) * factor
        at = pl.multiple_of(5 * width + quarter * narrow, LANES)
        cols = jnp.concatenate([r[:, pl.ds(at, narrow)] for r in (za_ref, zb_ref)], axis=0)
        scratch[:, size:] = dot_tn(mixed, cols) * factor
        for flip in range(2):
            store_units(scratch, rows, width // LANES, x, flip, outs[2 * flip_y : 2 * flip_y + 2], 0)


def fold_kernel(shift, radix, count, *refs):
    ins, outs = refs[:count], refs[count:]
    digit = (lax.axis_index("slab") >> shift) & (radix - 1)
    rest = ins[0].shape[0] // radix
    for j in range(radix):
        for k in range(rest):
            at = (digit ^ j) * rest + k
            total = ins[0][at].astype(F32)
            for ref in ins[1:]:
                total += ref[at].astype(F32)
            outs[j][k] = total.astype(BF16)


def fold(shift, radix, pieces, after=()):
    first = pieces[0].shape
    outs = [shape_of((first[0] // radix,) + first[1:], BF16)] * radix
    kernel = functools.partial(fold_kernel, shift, radix, len(pieces))
    return call(kernel, outs, *pieces, after=after)


def swap_pairs(slabs, cases, flip_slab, flip_case):
    return [
        (s * cases + c, (s ^ flip_slab) * cases + (c ^ flip_case))
        for s in range(slabs)
        for c in range(cases)
    ]


def gain_sums(grad, w_rows, gain_ref):
    rows, width = grad.shape[0], gain_ref.shape[1]
    spot = lax.axis_index("slab") * rows + lax.broadcasted_iota(jnp.int32, (rows, width), 0)
    lanes = lax.broadcasted_iota(jnp.int32, (rows, width), 1)
    gain = jnp.sum(jnp.where(lanes == spot, gain_ref[...], 0.0), axis=1, keepdims=True)
    total = jnp.sum(grad * w_rows.astype(F32), axis=1, keepdims=True) / gain
    return jnp.transpose(jnp.broadcast_to(total, (rows, LANES)))[0:1, :]


def place_mlp_kernel(slabs, width, units, *refs):
    pieces, (gain_ref, w_up_ref, w_ref) = refs[:4], refs[4:7]
    up, down, two, w_rows, held, up_rows, sems = refs[7:]
    rows = width // slabs
    here = pl.ds(pl.multiple_of(lax.axis_index("slab") * rows, 8), rows)
    copies = [
        pltpu.make_async_copy(w_up_ref.at[here], up_rows, sems.at[0]),
        pltpu.make_async_copy(w_ref.at[here], w_rows, sems.at[1]),
    ]
    for copy in copies:
        copy.start()
    case, x = lax.axis_index("case"), lax.axis_index("slab") & 1
    eighth, fine = units // 8, units // 4 // slabs
    for j in range(4):
        piece = pieces[j][0].astype(F32)
        held[case ^ j, :, :width] = piece[:, :width]
        for flip in range(2):
            at = pl.multiple_of(width + (x ^ flip) * eighth, LANES)
            held[case ^ j, :, pl.ds(at, eighth)] = piece[
                :, width + flip * eighth : width + (flip + 1) * eighth
            ]
    for quarter in range(4):
        down[quarter * rows : (quarter + 1) * rows, :] = held[quarter, :, :width]
    for block in range(slabs):
        up[:, block * 4 * fine : (block + 1) * 4 * fine] = jnp.concatenate(
            [
                held[quarter, :, pl.ds(width + block % 2 * eighth + block // 2 * fine, fine)]
                for quarter in range(4)
            ],
            axis=1,
        )
    for copy in copies:
        copy.wait()
    two[...] = gain_sums(up[...], up_rows[...], gain_ref)


def place_qkv_kernel(slabs, width, *refs):
    pieces, (gain_ref, w_rows), (qkv, out, one) = refs[:4], refs[4:6], refs[6:]
    case = lax.axis_index("case")
    rows = width // slabs
    size = 3 * width // 4
    for j in range(4):
        quarter = case ^ j
        for unit in range(width // LANES):
            piece = pieces[j][0, unit * rows : (unit + 1) * rows, :].astype(F32)
            if unit < size // LANES:
                start = pl.multiple_of(quarter * size + unit * LANES, LANES)
                qkv[:, pl.ds(start, LANES)] = piece
            else:
                start = pl.multiple_of(quarter * (width // 4) + unit * LANES - size, LANES)
                out[:, pl.ds(start, LANES)] = piece
    one[...] = gain_sums(qkv[...], w_rows[...], gain_ref)


def body(tokens, cotangent, w_qkv, w_out, w_up, w_down, gain_attn, gain_mlp):
    slabs, cases = lax.axis_size("slab"), lax.axis_size("case")
    depth, height, across, width = tokens.shape[1:]
    units = w_up.shape[1]
    lines = height * across
    per = lines // slabs
    count = depth * lines
    sizes = (depth, per, across, count)
    factor = 1.0 / math.sqrt(count * slabs * cases)
    gain_one, gain_two = gain_attn.reshape(1, width), gain_mlp.reshape(1, width)
    spans = slabs // 2
    rows = width // slabs
    parts = slabs if depth * per % 16 == 0 else 1

    def permute(array, flip_slab, flip_case):
        return lax.ppermute(array, BOTH, swap_pairs(slabs, cases, flip_slab, flip_case))

    def exchange(blocks):
        if parts == 1:
            return [lax.all_to_all(blocks[0], "slab", split_axis=0, concat_axis=0, tiled=True)]
        got = {j: permute(blocks[j], j, 0) for j in range(parts - 1, 0, -1)}
        return [blocks[0]] + [got[j] for j in range(1, parts)]

    proj_bf = shape_of((count, 3 * width), BF16)
    rows_bf = shape_of((count, width), BF16)
    *mine, hold_x = call(
        functools.partial(plane_kernel, sizes),
        [shape_of((count // parts, 3 * width), BF16)] * parts + [rows_bf],
        tokens.reshape(count, width),
        cotangent.reshape(count, width),
        gain_one,
        w_qkv,
        near=[False] * 4,
        scratch=[
            pltpu.VMEM((count, width), BF16),
            pltpu.VMEM((count, width), BF16),
            pltpu.VMEM((1, width), F32),
            pltpu.VMEM((width, 3 * width), BF16),
            pltpu.VMEM((count, 3 * width), BF16),
            pltpu.SemaphoreType.DMA((4,)),
        ],
    )
    w_up_mine, w_down_mine = call(
        functools.partial(prepare_kernel, slabs),
        [shape_of((width, units // 4), BF16), shape_of((units // 4, width), BF16)],
        w_up,
        w_down,
    )
    got = exchange(mine)
    shared, proj_z, mixed, residual, hold_z = call(
        functools.partial(lines_kernel, sizes, parts),
        [shape_of((count, 2 * width), BF16), proj_bf, rows_bf, rows_bf, rows_bf],
        *got,
        gain_one,
        gain_two,
        w_qkv,
        w_out,
        after=[w_up_mine],
    )
    shared_x, shared_y = permute(shared, 1, 0), permute(shared, 0, 2)
    grad_mixed, grad_residual = call(
        mlp_kernel,
        [rows_bf, shape_of((count, width), F32)],
        shared,
        residual,
        gain_two,
        w_out,
        w_up,
        w_down,
    )
    back, pack_z = call(
        functools.partial(lines_back_kernel, sizes, parts),
        [shape_of((count, 2 * width), BF16), shape_of((count, 6 * width), BF16)],
        proj_z,
        grad_mixed,
        grad_residual,
        mixed,
        hold_z,
        gain_one,
        w_qkv,
    )
    (back,) = call(
        copy_kernel, [shape_of((count, 2 * width), BF16)], back, after=[shared_x, shared_y]
    )
    back = lax.all_to_all(back, "slab", split_axis=0, concat_axis=0, tiled=True)
    pack_z_core = permute(pack_z, 0, 1)
    (pack_p,) = call(
        functools.partial(plane_grads_kernel, sizes, parts),
        [shape_of((count, 4 * width), BF16)],
        back,
        hold_x,
        gain_one,
        w_qkv,
        scratch=[pltpu.VMEM((count, 3 * width), BF16)],
    )
    (around,) = call(
        join_kernel,
        [shape_of((4 * count, 2 * width), BF16)],
        shared,
        shared_x,
        shared_y,
        permute(shared_x, 0, 2),
        after=[pack_p],
    )
    radix = min(4, spans)
    shift = (slabs // radix).bit_length() - 1
    big = call(
        functools.partial(grads_mlp_kernel, factor, shift),
        [shape_of((spans // radix, rows, 2 * width), BF16)] * radix,
        around,
        permute(around, 0, 1),
        w_up_mine,
        w_down_mine,
        scratch=[pltpu.VMEM((units // 8, width), F32), pltpu.VMEM((width, units // 4), F32)],
    )
    early = big[0]
    small = call(
        functools.partial(grads_qkv_kernel, factor, width, slabs),
        [shape_of((spans, rows * (width // LANES), LANES), BF16)] * 4,
        pack_z,
        pack_z_core,
        pack_p,
        permute(pack_p, 0, 1),
        scratch=[pltpu.VMEM((width, width), F32)],
    )
    ready = small[0]
    small = [small[0], permute(small[1], 1, 0), permute(small[2], 0, 2), permute(small[3], 1, 2)]
    grad_tokens, flag = call(
        functools.partial(plane_tokens_kernel, sizes, parts),
        [rows_bf, shape_of((8, LANES), F32)],
        back,
        pack_p,
        hold_x,
        gain_one,
        w_qkv,
        after=[ready, early],
    )

    def reduce_z(split):
        left = spans
        while True:
            radix = len(split)
            left //= radix
            shift = (left * 2).bit_length() - 1
            got = [permute(split[j], j << shift, 0) for j in range(radix - 1, 0, -1)]
            pieces = [split[0]] + got[::-1]
            if left == 1:
                return pieces
            radix = min(4, left)
            split = fold((left // radix * 2).bit_length() - 1, radix, pieces)

    def gather(last):
        return [last] + [permute(last, 0, j) for j in range(1, 4)]

    big = reduce_z(big)
    small = reduce_z(fold(shift, radix, small, [flag]))
    big = gather(fold(0, 1, big, [small[0]])[0])
    full_up, full_down, full_two, w_rows = call(
        functools.partial(place_mlp_kernel, slabs, width, units),
        [
            shape_of((rows, units), F32),
            shape_of((units // slabs, width), F32),
            shape_of((1, rows), F32),
            shape_of((rows, 3 * width), BF16),
        ],
        *big,
        gain_two,
        w_up,
        w_qkv,
        near=[True] * 5 + [False] * 2,
        scratch=[
            pltpu.VMEM((4, rows, 2 * width), F32),
            pltpu.VMEM((rows, units), BF16),
            pltpu.SemaphoreType.DMA((2,)),
        ],
    )
    small = gather(fold(0, 1, small)[0])
    full_qkv, full_out, full_one = call(
        functools.partial(place_qkv_kernel, slabs, width),
        [shape_of((rows, 3 * width), F32), shape_of((rows, width), F32), shape_of((1, rows), F32)],
        *small,
        gain_one,
        w_rows,
    )
    return (
        grad_tokens.reshape(tokens.shape),
        full_qkv,
        full_out,
        full_up,
        full_down,
        full_one.reshape(rows),
        full_two.reshape(rows),
    )


def solution(mesh):
    grid = P("case", "slab", None, None, None)
    return jax.shard_map(
        body,
        mesh=mesh,
        in_specs=(grid, grid, P(), P(), P(), P(), P(), P()),
        out_specs=(
            grid,
            P("slab", None),
            P("slab", None),
            P("slab", None),
            P("slab", None),
            P("slab"),
            P("slab"),
        ),
        check_vma=False,
    )
```

```python
import functools
import math

import jax
import jax.numpy as jnp
from jax import lax
from jax.experimental import pallas as pl
from jax.experimental.pallas import tpu as pltpu
from jax.sharding import PartitionSpec as P

HEADS = 8
LANES = 128
EPSILON = 1e-06
ROOT_TWO_PI = math.sqrt(2.0 / math.pi)
F32 = jnp.float32
BF16 = jnp.bfloat16
BOTH = ("slab", "case")
VMEM_BYTES = 24 * 1024 * 1024


def dot(a, b):
    return lax.dot_general(a, b, (((1,), (0,)), ((), ())), preferred_element_type=F32)


def dot_nt(a, b):
    return lax.dot_general(a, b, (((1,), (1,)), ((), ())), preferred_element_type=F32)


def dot_tn(a, b):
    return lax.dot_general(a, b, (((0,), (0,)), ((), ())), preferred_element_type=F32)


def norm_stats(values):
    inverse = lax.rsqrt(jnp.mean(values * values, axis=-1, keepdims=True) + EPSILON)
    return values * inverse, inverse


def norm_back(scaled, normed, inverse):
    return inverse * (scaled - normed * jnp.mean(scaled * normed, axis=-1, keepdims=True))


def call(kernel, outs, *args, after=(), scratch=(), near=None, flops=10**7):
    count = len(args)
    near = [True] * count if near is None else near

    def run(*refs):
        kernel(*refs[:count], *refs[count + len(after) :])

    vmem, far = pl.BlockSpec(memory_space=pltpu.VMEM), pl.BlockSpec(memory_space=pltpu.HBM)
    return pl.pallas_call(
        run,
        out_shape=outs,
        in_specs=[vmem if one else far for one in near] + [pl.BlockSpec(memory_space=pl.ANY)] * len(after),
        out_specs=[vmem] * len(outs),
        scratch_shapes=list(scratch),
        cost_estimate=pl.CostEstimate(flops=flops, transcendentals=0, bytes_accessed=10**4),
        compiler_params=pltpu.CompilerParams(vmem_limit_bytes=VMEM_BYTES),
    )(
        *[
            arg if one else pltpu.with_memory_space_constraint(arg, pltpu.HBM)
            for arg, one in zip(args, near)
        ],
        *after,
    )


def shape_of(shape, dtype):
    return jax.ShapeDtypeStruct(shape, dtype)


def line_masks(sizes, kind):
    depth, per, across, count = sizes
    rows = lax.broadcasted_iota(jnp.int32, (2 * count, count), 0) & (count - 1)
    cols = lax.broadcasted_iota(jnp.int32, (2 * count, count), 1)

    def parts(t):
        chunk = t // (depth * per)
        plane = (t // per) & (depth - 1)
        spot = chunk * per + (t & (per - 1))
        return plane, spot // across, spot & (across - 1), t & (per - 1)

    a, b = parts(rows), parts(cols)
    if kind == "z":
        return [a[3] == b[3]]
    same = a[0] == b[0]
    return [same & (a[1] == b[1]), same & (a[2] == b[2])]


def softmax_in(scores, mask):
    held = jnp.where(mask, scores, -1e30)
    weights = jnp.exp(held - jnp.max(held, axis=-1, keepdims=True))
    return weights / jnp.sum(weights, axis=-1, keepdims=True)


def pair_parts(proj, pair, width):
    at = pair * LANES
    return [proj[:, which * width + at : which * width + at + LANES] for which in range(3)]


def halves():
    lane = lax.broadcasted_iota(jnp.int32, (1, LANES), 1)
    low = (lane < LANES // 2).astype(F32)
    return low.astype(BF16), (1.0 - low).astype(BF16)


def stack(block, low, high):
    return jnp.concatenate([block * low, block * high], axis=0)


def side(block):
    count = block.shape[0] // 2
    return jnp.concatenate([block[:count], block[count:]], axis=1)


def attend(proj, masks, width):
    low, high = halves()
    scale = (width // HEADS) ** (-0.5)
    outs = []
    for pair in range(HEADS // 2):
        q2, k2, v2 = pair_parts(proj, pair, width)
        scores = dot_nt(stack(q2, low, high), k2) * scale
        probs = sum(softmax_in(scores, mask).astype(BF16).astype(F32) for mask in masks)
        outs.append(dot(side(probs.astype(BF16)), stack(v2, low, high)))
    return jnp.concatenate(outs, axis=1)


def attend_back(proj, grad, masks, width, out_ref, at):
    low, high = halves()
    scale = (width // HEADS) ** (-0.5)
    for pair in range(HEADS // 2):
        q2, k2, v2 = pair_parts(proj, pair, width)
        g2 = grad[:, pair * LANES : (pair + 1) * LANES]
        qs, gs = stack(q2, low, high), stack(g2, low, high)
        scores = dot_nt(qs, k2) * scale
        grad_probs = dot_nt(gs, v2)
        probs = jnp.zeros_like(scores)
        grad_scores = jnp.zeros_like(scores)
        for mask in masks:
            one = softmax_in(scores, mask)
            probs += one.astype(BF16).astype(F32)
            grad_scores += one * (grad_probs - jnp.sum(one * grad_probs, axis=-1, keepdims=True))
        probs, grad_scores = probs.astype(BF16), grad_scores.astype(BF16)
        found = (
            dot(side(grad_scores), stack(k2, low, high)) * scale,
            dot_tn(grad_scores, qs) * scale,
            dot_tn(probs, gs),
        )
        for which in range(3):
            start = at + which * width + pair * LANES
            out_ref[0 : q2.shape[0], start : start + LANES] = found[which].astype(BF16)


def chunk_order(sizes, parts):
    depth, per, _, count = sizes
    rows = lax.broadcasted_iota(jnp.int32, (count, count), 0)
    cols = lax.broadcasted_iota(jnp.int32, (count, count), 1)
    chunk = rows // (depth * per)
    if parts > 1:
        chunk = chunk ^ lax.axis_index("slab")
    plane = (rows // per) & (depth - 1)
    return plane * (count // depth) + chunk * per + (rows & (per - 1)) == cols


def put_parts(refs, at, value):
    rows = refs[0].shape[0]
    for j, ref in enumerate(refs):
        ref[:, at : at + value.shape[1]] = value[j * rows : (j + 1) * rows]


def joined(refs, start, stop):
    return jnp.concatenate([ref[:, start:stop] for ref in refs], axis=0)


def plane_kernel(sizes, x_ref, cot_ref, gain_ref, w_ref, *refs):
    parts, hold_x = refs[:-7], refs[-7]
    x_in, cot_in, gain_in, w_in, proj, sems = refs[-6:]
    copies = [
        pltpu.make_async_copy(src, dst, sems.at[i])
        for i, (src, dst) in enumerate(
            ((x_ref, x_in), (gain_ref, gain_in), (w_ref, w_in), (cot_ref, cot_in))
        )
    ]
    for copy in copies:
        copy.start()
    width = w_in.shape[0]
    order = chunk_order(sizes, len(parts)).astype(F32).astype(BF16)
    masks = line_masks(sizes, "xy")
    copies[0].wait()
    x = dot(order, x_in[...])
    hold_x[...] = x.astype(BF16)
    put_parts(parts, 0, hold_x[...])
    copies[1].wait()
    normed, _ = norm_stats(x)
    hidden = (normed * gain_in[...]).astype(BF16)
    copies[2].wait()
    proj[...] = dot(hidden, w_in[...]).astype(BF16)
    put_parts(parts, 2 * width, attend(proj[...], masks, width).astype(BF16))
    copies[3].wait()
    put_parts(parts, width, dot(order, cot_in[...]).astype(BF16))


def prepare_kernel(slabs, w_up_ref, w_down_ref, up_ref, down_ref):
    quarter = lax.axis_index("case")
    units = w_up_ref.shape[1]
    fine = units // slabs // 4
    rows = lax.broadcasted_iota(jnp.int32, (8 * LANES, LANES), 0)
    cols = lax.broadcasted_iota(jnp.int32, (8 * LANES, LANES), 1)
    for flip in range(2):
        x = (lax.axis_index("slab") & 1) ^ flip
        wanted = ((cols // fine * 2 + x) * 4 + quarter) * fine + (cols & (fine - 1))
        pick = (rows == wanted).astype(F32).astype(BF16)
        start = flip * units // 8
        for group in range(units // 8 // LANES):
            up_ref[:, start + group * LANES : start + (group + 1) * LANES] = dot(
                w_up_ref[:, group * 8 * LANES : (group + 1) * 8 * LANES], pick
            ).astype(BF16)
        for z in range(slabs // 2):
            at = pl.multiple_of(((z * 2 + x) * 4 + quarter) * fine, 8)
            down_ref[start + z * fine : start + (z + 1) * fine, :] = w_down_ref[pl.ds(at, fine), :]


def lines_kernel(sizes, parts, *refs):
    got = refs[:parts]
    gain_one_ref, gain_two_ref, w_ref, w_out_ref = refs[parts : parts + 4]
    shared_ref, proj_ref, mixed_ref, residual_ref, hold_x = refs[parts + 4 :]
    width = w_ref.shape[0]
    hold_x[...] = joined(got, 0, width)
    x = hold_x[...].astype(F32)
    normed, _ = norm_stats(x)
    proj_ref[...] = dot((normed * gain_one_ref[...]).astype(BF16), w_ref[...]).astype(BF16)
    out_z = attend(proj_ref[...], line_masks(sizes, "z"), width).astype(BF16)
    mixed = (joined(got, 2 * width, 3 * width).astype(F32) + out_z.astype(F32)).astype(BF16)
    residual = (x + dot(mixed, w_out_ref[...])).astype(BF16)
    normed_two, _ = norm_stats(residual.astype(F32))
    shared_ref[:, :width] = (normed_two * gain_two_ref[...]).astype(BF16)
    shared_ref[:, width:] = joined(got, width, 2 * width)
    mixed_ref[...] = mixed
    residual_ref[...] = residual


def gelu_parts(upper):
    square = upper * upper
    tangent = jnp.tanh(ROOT_TWO_PI * (upper + 0.044715 * upper * square))
    half = 0.5 * (1.0 + tangent)
    slope = half + 0.5 * upper * (1.0 - tangent * tangent) * ROOT_TWO_PI * (
        1.0 + 3.0 * 0.044715 * square
    )
    return (upper * half).astype(BF16), slope


def mlp_kernel(
    shared_ref, residual_ref, gain_ref, w_out_ref, w_up_ref, w_down_ref, grad_ref, gres_ref
):
    width, units = w_up_ref.shape
    hidden, cot = shared_ref[:, :width], shared_ref[:, width:]
    normed, inverse = norm_stats(residual_ref[...].astype(F32))
    step = min(512, units)
    grad_hidden = jnp.zeros(normed.shape, F32)
    for at in range(0, units, step):
        _, slope = gelu_parts(dot(hidden, w_up_ref[:, at : at + step]))
        grad_upper = (dot_nt(cot, w_down_ref[at : at + step, :]) * slope).astype(BF16)
        grad_hidden += dot_nt(grad_upper, w_up_ref[:, at : at + step])
    grad_residual = cot.astype(F32) + norm_back(grad_hidden * gain_ref[...], normed, inverse)
    gres_ref[...] = grad_residual
    grad_ref[...] = dot_nt(grad_residual.astype(BF16), w_out_ref[...]).astype(BF16)


def lines_back_kernel(
    sizes, parts, proj_ref, grad_ref, gres_ref, mixed_ref, x_ref, gain_ref, w_ref, back_ref, pack_ref
):
    width = w_ref.shape[0]
    pack_ref[:, 4 * width : 5 * width] = mixed_ref[...]
    pack_ref[:, 5 * width :] = gres_ref[...].astype(BF16)
    attend_back(proj_ref[...], grad_ref[...], line_masks(sizes, "z"), width, pack_ref, width)
    normed, inverse = norm_stats(x_ref[...].astype(F32))
    pack_ref[:, :width] = (normed * gain_ref[...]).astype(BF16)
    grad_hidden = dot_nt(pack_ref[:, width : 4 * width], w_ref[...])
    back = norm_back(grad_hidden * gain_ref[...], normed, inverse)
    part = (gres_ref[...] + back).astype(BF16)
    for j, (spot, size) in enumerate(blocks_of(part.shape[0], parts)):
        back_ref[pl.ds(spot, size), :width] = grad_ref[j * size : (j + 1) * size, :]
        back_ref[pl.ds(spot, size), width:] = part[j * size : (j + 1) * size]


def blocks_of(count, parts):
    size = count // parts
    if parts == 1:
        return [(0, size)]
    me = lax.axis_index("slab")
    return [(pl.multiple_of((me ^ j) * size, 16), size) for j in range(parts)]


def partner_order(ref, parts, start, stop):
    return jnp.concatenate(
        [ref[pl.ds(spot, size), start:stop] for spot, size in blocks_of(ref.shape[0], parts)], axis=0
    )


def copy_kernel(in_ref, out_ref):
    out_ref[...] = in_ref[...]


def join_kernel(*refs):
    out_ref = refs[-1]
    rows = refs[0].shape[0]
    for j, ref in enumerate(refs[:-1]):
        out_ref[j * rows : (j + 1) * rows, :] = ref[...]


def plane_grads_kernel(sizes, parts, *refs):
    back_ref, x_ref, gain_ref, w_ref, pack_ref, proj = refs
    width = w_ref.shape[0]
    normed, _ = norm_stats(x_ref[...].astype(F32))
    pack_ref[:, :width] = (normed * gain_ref[...]).astype(BF16)
    proj[...] = dot(pack_ref[:, :width], w_ref[...]).astype(BF16)
    grad = partner_order(back_ref, parts, 0, width)
    attend_back(proj[...], grad, line_masks(sizes, "xy"), width, pack_ref, width)


def plane_tokens_kernel(sizes, parts, *refs):
    back_ref, pack_ref, x_ref, gain_ref, w_ref, grad_ref, flag_ref = refs
    flag_ref[...] = jnp.zeros_like(flag_ref)
    width = w_ref.shape[0]
    normed, inverse = norm_stats(x_ref[...].astype(F32))
    grad_hidden = dot_nt(pack_ref[:, width:], w_ref[...])
    back = norm_back(grad_hidden * gain_ref[...], normed, inverse)
    part = partner_order(back_ref, parts, width, 2 * width).astype(F32)
    order = chunk_order(sizes, parts).astype(F32).astype(BF16)
    grad_ref[...] = dot_tn(order, (back + part).astype(BF16)).astype(BF16)


def place():
    slab, case = lax.axis_index("slab"), lax.axis_index("case")
    return slab & 1, case >> 1, case & 1, slab >> 1


def store_units(scratch, rows, units, x, flip, outs, at):
    blocks = outs[0].shape[0]
    for z in range(blocks):
        start = pl.multiple_of((z * 2 + (x ^ flip)) * rows, 8)
        block = scratch[pl.ds(start, rows), 0 : units * LANES].astype(BF16)
        for unit in range(units):
            outs[flip][z, at + unit * rows : at + (unit + 1) * rows, :] = block[
                :, unit * LANES : (unit + 1) * LANES
            ]


def grads_mlp_kernel(factor, shift, here_ref, there_ref, w_up_ref, w_down_ref, *refs):
    outs, down, up = refs[:-2], refs[-2], refs[-1]
    width, units = w_up_ref.shape
    slab = lax.axis_index("slab")
    digit = (slab >> shift) & (len(outs) - 1)
    hidden = jnp.concatenate([ref[:, :width] for ref in (here_ref, there_ref)], axis=0)
    cot = jnp.concatenate([ref[:, width:] for ref in (here_ref, there_ref)], axis=0)
    half = units // 2
    for at in (0, half):
        active, slope = gelu_parts(dot(hidden, w_up_ref[:, at : at + half]))
        grad_upper = (dot_nt(cot, w_down_ref[at : at + half, :]) * slope).astype(BF16)
        up[:, at : at + half] = dot_tn(hidden, grad_upper) * factor
        if at == 0:
            down[...] = dot_tn(active, cot) * factor
    rest, rows = outs[0].shape[:2]
    for j, out in enumerate(outs):
        for k in range(rest):
            z = (digit ^ j) * rest + k
            at = pl.ds(pl.multiple_of(z * rows, 8), rows)
            out[k, :, :width] = down[at, :].astype(BF16)
            at = pl.ds(pl.multiple_of((z * 2 + (slab & 1)) * rows, 8), rows)
            out[k, :, width:] = up[at, :].astype(BF16)


def grads_qkv_kernel(factor, width, slabs, za_ref, zb_ref, pa_ref, pb_ref, *refs):
    outs, scratch = refs[:4], refs[4]
    x, y, core, _ = place()
    size, narrow = 3 * width // 4, width // 4
    rows = width // slabs
    hidden = jnp.concatenate([r[:, :width] for r in (za_ref, zb_ref, pa_ref, pb_ref)], axis=0)
    mixed = jnp.concatenate([r[:, 4 * width : 5 * width] for r in (za_ref, zb_ref)], axis=0)
    for flip_y in range(2):
        quarter = (y ^ flip_y) * 2 + core
        at = pl.multiple_of(width + quarter * size, LANES)
        cols = jnp.concatenate(
            [r[:, pl.ds(at, size)] for r in (za_ref, zb_ref, pa_ref, pb_ref)], axis=0
        )
        scratch[:, :size] = dot_tn(hidden, cols) * factor
        at = pl.multiple_of(5 * width + quarter * narrow, LANES)
        cols = jnp.concatenate([r[:, pl.ds(at, narrow)] for r in (za_ref, zb_ref)], axis=0)
        scratch[:, size:] = dot_tn(mixed, cols) * factor
        for flip in range(2):
            store_units(scratch, rows, width // LANES, x, flip, outs[2 * flip_y : 2 * flip_y + 2], 0)


def fold_kernel(shift, radix, count, *refs):
    ins, outs = refs[:count], refs[count:]
    digit = (lax.axis_index("slab") >> shift) & (radix - 1)
    rest = ins[0].shape[0] // radix
    for j in range(radix):
        for k in range(rest):
            at = (digit ^ j) * rest + k
            total = ins[0][at].astype(F32)
            for ref in ins[1:]:
                total += ref[at].astype(F32)
            outs[j][k] = total.astype(BF16)


def fold(shift, radix, pieces, after=()):
    first = pieces[0].shape
    outs = [shape_of((first[0] // radix,) + first[1:], BF16)] * radix
    kernel = functools.partial(fold_kernel, shift, radix, len(pieces))
    return call(kernel, outs, *pieces, after=after)


def swap_pairs(slabs, cases, flip_slab, flip_case):
    return [
        (s * cases + c, (s ^ flip_slab) * cases + (c ^ flip_case))
        for s in range(slabs)
        for c in range(cases)
    ]


def gain_sums(grad, w_rows, gain_ref):
    rows, width = grad.shape[0], gain_ref.shape[1]
    spot = lax.axis_index("slab") * rows + lax.broadcasted_iota(jnp.int32, (rows, width), 0)
    lanes = lax.broadcasted_iota(jnp.int32, (rows, width), 1)
    gain = jnp.sum(jnp.where(lanes == spot, gain_ref[...], 0.0), axis=1, keepdims=True)
    total = jnp.sum(grad * w_rows.astype(F32), axis=1, keepdims=True) / gain
    return jnp.transpose(jnp.broadcast_to(total, (rows, LANES)))[0:1, :]


def place_mlp_kernel(slabs, width, units, *refs):
    pieces, (gain_ref, w_up_ref, w_ref) = refs[:4], refs[4:7]
    up, down, two, w_rows, held, up_rows, sems = refs[7:]
    rows = width // slabs
    here = pl.ds(pl.multiple_of(lax.axis_index("slab") * rows, 8), rows)
    copies = [
        pltpu.make_async_copy(w_up_ref.at[here], up_rows, sems.at[0]),
        pltpu.make_async_copy(w_ref.at[here], w_rows, sems.at[1]),
    ]
    for copy in copies:
        copy.start()
    case, x = lax.axis_index("case"), lax.axis_index("slab") & 1
    eighth, fine = units // 8, units // 4 // slabs
    for j in range(4):
        piece = pieces[j][0].astype(F32)
        held[case ^ j, :, :width] = piece[:, :width]
        for flip in range(2):
            at = pl.multiple_of(width + (x ^ flip) * eighth, LANES)
            held[case ^ j, :, pl.ds(at, eighth)] = piece[
                :, width + flip * eighth : width + (flip + 1) * eighth
            ]
    for quarter in range(4):
        down[quarter * rows : (quarter + 1) * rows, :] = held[quarter, :, :width]
    for block in range(slabs):
        up[:, block * 4 * fine : (block + 1) * 4 * fine] = jnp.concatenate(
            [
                held[quarter, :, pl.ds(width + block % 2 * eighth + block // 2 * fine, fine)]
                for quarter in range(4)
            ],
            axis=1,
        )
    for copy in copies:
        copy.wait()
    two[...] = gain_sums(up[...], up_rows[...], gain_ref)


def place_qkv_kernel(slabs, width, *refs):
    pieces, (gain_ref, w_rows), (qkv, out, one) = refs[:4], refs[4:6], refs[6:]
    case = lax.axis_index("case")
    rows = width // slabs
    size = 3 * width // 4
    for j in range(4):
        quarter = case ^ j
        for unit in range(width // LANES):
            piece = pieces[j][0, unit * rows : (unit + 1) * rows, :].astype(F32)
            if unit < size // LANES:
                start = pl.multiple_of(quarter * size + unit * LANES, LANES)
                qkv[:, pl.ds(start, LANES)] = piece
            else:
                start = pl.multiple_of(quarter * (width // 4) + unit * LANES - size, LANES)
                out[:, pl.ds(start, LANES)] = piece
    one[...] = gain_sums(qkv[...], w_rows[...], gain_ref)


def body(tokens, cotangent, w_qkv, w_out, w_up, w_down, gain_attn, gain_mlp):
    slabs, cases = lax.axis_size("slab"), lax.axis_size("case")
    depth, height, across, width = tokens.shape[1:]
    units = w_up.shape[1]
    lines = height * across
    per = lines // slabs
    count = depth * lines
    sizes = (depth, per, across, count)
    factor = 1.0 / math.sqrt(count * slabs * cases)
    gain_one, gain_two = gain_attn.reshape(1, width), gain_mlp.reshape(1, width)
    spans = slabs // 2
    rows = width // slabs
    parts = slabs if depth * per % 16 == 0 else 1

    def permute(array, flip_slab, flip_case):
        return lax.ppermute(array, BOTH, swap_pairs(slabs, cases, flip_slab, flip_case))

    def exchange(blocks):
        if parts == 1:
            return [lax.all_to_all(blocks[0], "slab", split_axis=0, concat_axis=0, tiled=True)]
        got = {j: permute(blocks[j], j, 0) for j in range(parts - 1, 0, -1)}
        return [blocks[0]] + [got[j] for j in range(1, parts)]

    proj_bf = shape_of((count, 3 * width), BF16)
    rows_bf = shape_of((count, width), BF16)
    *mine, hold_x = call(
        functools.partial(plane_kernel, sizes),
        [shape_of((count // parts, 3 * width), BF16)] * parts + [rows_bf],
        tokens.reshape(count, width),
        cotangent.reshape(count, width),
        gain_one,
        w_qkv,
        near=[False] * 4,
        scratch=[
            pltpu.VMEM((count, width), BF16),
            pltpu.VMEM((count, width), BF16),
            pltpu.VMEM((1, width), F32),
            pltpu.VMEM((width, 3 * width), BF16),
            pltpu.VMEM((count, 3 * width), BF16),
            pltpu.SemaphoreType.DMA((4,)),
        ],
    )
    w_up_mine, w_down_mine = call(
        functools.partial(prepare_kernel, slabs),
        [shape_of((width, units // 4), BF16), shape_of((units // 4, width), BF16)],
        w_up,
        w_down,
    )
    got = exchange(mine)
    shared, proj_z, mixed, residual, hold_z = call(
        functools.partial(lines_kernel, sizes, parts),
        [shape_of((count, 2 * width), BF16), proj_bf, rows_bf, rows_bf, rows_bf],
        *got,
        gain_one,
        gain_two,
        w_qkv,
        w_out,
        after=[w_up_mine],
    )
    shared_x, shared_y = permute(shared, 1, 0), permute(shared, 0, 2)
    grad_mixed, grad_residual = call(
        mlp_kernel,
        [rows_bf, shape_of((count, width), F32)],
        shared,
        residual,
        gain_two,
        w_out,
        w_up,
        w_down,
    )
    back, pack_z = call(
        functools.partial(lines_back_kernel, sizes, parts),
        [shape_of((count, 2 * width), BF16), shape_of((count, 6 * width), BF16)],
        proj_z,
        grad_mixed,
        grad_residual,
        mixed,
        hold_z,
        gain_one,
        w_qkv,
    )
    (back,) = call(
        copy_kernel, [shape_of((count, 2 * width), BF16)], back, after=[shared_x, shared_y]
    )
    back = lax.all_to_all(back, "slab", split_axis=0, concat_axis=0, tiled=True)
    pack_z_core = permute(pack_z, 0, 1)
    (pack_p,) = call(
        functools.partial(plane_grads_kernel, sizes, parts),
        [shape_of((count, 4 * width), BF16)],
        back,
        hold_x,
        gain_one,
        w_qkv,
        scratch=[pltpu.VMEM((count, 3 * width), BF16)],
    )
    small = call(
        functools.partial(grads_qkv_kernel, factor, width, slabs),
        [shape_of((spans, rows * (width // LANES), LANES), BF16)] * 4,
        pack_z,
        pack_z_core,
        pack_p,
        permute(pack_p, 0, 1),
        scratch=[pltpu.VMEM((width, width), F32)],
    )
    ready = small[0]
    (around,) = call(
        join_kernel,
        [shape_of((4 * count, 2 * width), BF16)],
        shared,
        shared_x,
        shared_y,
        permute(shared_x, 0, 2),
        after=[ready],
    )
    radix = min(4, spans)
    shift = (slabs // radix).bit_length() - 1
    big = call(
        functools.partial(grads_mlp_kernel, factor, shift),
        [shape_of((spans // radix, rows, 2 * width), BF16)] * radix,
        around,
        permute(around, 0, 1),
        w_up_mine,
        w_down_mine,
        scratch=[pltpu.VMEM((units // 8, width), F32), pltpu.VMEM((width, units // 4), F32)],
    )
    early = big[0]
    small = [small[0], permute(small[1], 1, 0), permute(small[2], 0, 2), permute(small[3], 1, 2)]
    grad_tokens, flag = call(
        functools.partial(plane_tokens_kernel, sizes, parts),
        [rows_bf, shape_of((8, LANES), F32)],
        back,
        pack_p,
        hold_x,
        gain_one,
        w_qkv,
        after=[ready, early],
    )

    def reduce_z(split):
        left = spans
        while True:
            radix = len(split)
            left //= radix
            shift = (left * 2).bit_length() - 1
            pieces = [split[0]] + [permute(split[j], j << shift, 0) for j in range(1, radix)]
            if left == 1:
                return pieces
            radix = min(4, left)
            split = fold((left // radix * 2).bit_length() - 1, radix, pieces)

    def gather(last):
        return [last] + [permute(last, 0, j) for j in range(1, 4)]

    big = reduce_z(big)
    small = reduce_z(fold(shift, radix, small, [flag]))
    big = gather(fold(0, 1, big, [small[0]])[0])
    full_up, full_down, full_two, w_rows = call(
        functools.partial(place_mlp_kernel, slabs, width, units),
        [
            shape_of((rows, units), F32),
            shape_of((units // slabs, width), F32),
            shape_of((1, rows), F32),
            shape_of((rows, 3 * width), BF16),
        ],
        *big,
        gain_two,
        w_up,
        w_qkv,
        near=[True] * 5 + [False] * 2,
        scratch=[
            pltpu.VMEM((4, rows, 2 * width), F32),
            pltpu.VMEM((rows, units), BF16),
            pltpu.SemaphoreType.DMA((2,)),
        ],
    )
    small = gather(fold(0, 1, small)[0])
    full_qkv, full_out, full_one = call(
        functools.partial(place_qkv_kernel, slabs, width),
        [shape_of((rows, 3 * width), F32), shape_of((rows, width), F32), shape_of((1, rows), F32)],
        *small,
        gain_one,
        w_rows,
    )
    return (
        grad_tokens.reshape(tokens.shape),
        full_qkv,
        full_out,
        full_up,
        full_down,
        full_one.reshape(rows),
        full_two.reshape(rows),
    )


def solution(mesh):
    grid = P("case", "slab", None, None, None)
    return jax.shard_map(
        body,
        mesh=mesh,
        in_specs=(grid, grid, P(), P(), P(), P(), P(), P()),
        out_specs=(
            grid,
            P("slab", None),
            P("slab", None),
            P("slab", None),
            P("slab", None),
            P("slab"),
            P("slab"),
        ),
        check_vma=False,
    )
```
